32 devices in a mesh: wide: 8 (over z, x), narrow: 4 (over y, core).
Axes of the slice: x: 2, y: 2, z: 4, core: 2. Of those that a mesh axis runs over, the one named last changes fastest.
Arguments:
- images: bfloat16 [3, 320, 8, 7, 2048], P(None, 'wide', 'narrow'), may hold values from -54 to 54
- upstream: bfloat16 [3, 320, 8, 7, 2048], P(None, 'wide', 'narrow'), may hold values from -6 to 6
- row_counts: int32 [3, 8, 4], P(None, 'wide', 'narrow'), may hold values from 1 to 2, as said below
- w_reduce: float32 [2048, 512], replicated, may hold values from -0.125 to 0.125
- w_spatial: float32 [4608, 512], replicated, may hold values from -0.09375 to 0.09375
- w_expand: float32 [512, 2048], replicated, may hold values from -0.25 to 0.25
- norm_gain: float32 [3072], replicated, may hold values from 0.5 to 1.5
- norm_bias: float32 [3072], replicated, may hold values from -1.75 to 1.75
- reduce_rows: float32 [2048], P('wide'), may hold values from 35200 to 140800
- reduce_cols: float32 [512], replicated, may hold values from 35200 to 140800
- spatial_rows: float32 [4608], P('wide'), may hold values from 21120 to 84480
- spatial_cols: float32 [512], replicated, may hold values from 21120 to 84480
- expand_rows: float32 [512], P('wide'), may hold values from 3520 to 14080
- expand_cols: float32 [2048], replicated, may hold values from 3520 to 14080
- norm_state: float32 [2, 3072], replicated, may hold values from 3520 to 168960
Outputs:
- output: bfloat16 [3, 320, 8, 7, 2048], P(None, 'wide', 'narrow')
- input_grad: bfloat16 [3, 320, 8, 7, 2048], P(None, 'wide', 'narrow')
- grad_reduce: float32 [2048, 512], P('wide')
- grad_spatial: float32 [4608, 512], P('wide')
- grad_expand: float32 [512, 2048], P('wide')
- reduce_rows_next: float32 [2048], P('wide')
- reduce_cols_next: float32 [512], replicated
- spatial_rows_next: float32 [4608], P('wide')
- spatial_cols_next: float32 [512], replicated
- expand_rows_next: float32 [512], P('wide')
- expand_cols_next: float32 [2048], replicated
- reduce_next: float32 [2048, 512], P('wide')
- spatial_next: float32 [4608, 512], P('wide')
- expand_next: float32 [512, 2048], P('wide')
- norm_grads: float32 [2, 3072], replicated
- norm_second: float32 [2, 3072], replicated
- norm_next: float32 [2, 3072], replicated
The draws below stay inside these ranges and needn't reach their ends.
Inputs may be any that keep to these rules, and one draw needn't show every extreme that they name: `row_counts`: on every device each resolution group has 1 or 2 counted rows; for group g the counts along narrow sum to 5 + g.
All inputs are finite; a program needn't handle non-finite values.
Results may differ from the reference program's by a relative error of at most 0.0096.
Values may be sent and summed in bfloat16 or wider, within the bound.
A program may use at most 320 MiB of HBM per device.

```python
import math
import jax
import jax.numpy as jnp
from jax import lax

C_IN = 2048
C_MID = 512
IMG_DEV = 40
GROUPS = 3
SLOTS = 2
WIDTH = 7
STEP = 10
IMAGES = 320
ROWS = 8
C_ALL = 3072
PATCH = 4608
NPIX = 35200
N_WIDE = 8
N_NARROW = 4


def draw_images(key, part):
    key = jax.random.fold_in(key, 11)
    full_shape = (GROUPS, IMAGES, ROWS, WIDTH, C_IN)
    image_place = lax.broadcasted_iota(jnp.float32, full_shape, 1) / max(IMAGES - 1, 1)
    row_place = lax.broadcasted_iota(jnp.float32, full_shape, 2) / (ROWS - 1)
    random_part = jnp.clip(jax.random.normal(key, full_shape, jnp.float32), -6.0, 6.0)
    factor = jnp.exp(jnp.log(3.0) * (image_place + row_place))
    return (random_part * factor).astype(jnp.bfloat16)


def draw_row_counts(key, part):
    key = jax.random.fold_in(key, 23)
    full_shape = (GROUPS, N_WIDE, N_NARROW)
    scores = jax.random.randint(key, full_shape, 0, 1 << 20) * N_NARROW + lax.broadcasted_iota(jnp.int32, full_shape, 2)
    ranks = jnp.argsort(jnp.argsort(scores, axis=2), axis=2)
    doubles = lax.broadcasted_iota(jnp.int32, full_shape, 0) + 1
    return (1 + (ranks < doubles).astype(jnp.int32)).astype(jnp.int32)


def draw_norm_state(key, part):
    key = jax.random.fold_in(key, 37)
    channel = lax.broadcasted_iota(jnp.int32, (2, C_ALL), 1)
    level = jnp.where(channel < C_MID, 6.0, jnp.where(channel < 2 * C_MID, 3.0, 0.5))
    spread = jnp.exp(jax.random.uniform(key, (2, C_ALL), jnp.float32, 0.0, jnp.log(4.0)))
    return 0.2 * NPIX * level * spread


def steps_of(rng, dims, split, smallest, high):
    loudness, own = 1.0, jax.random.fold_in(rng, 6)
    for axis_at, shards_of in split:
        steps = jnp.exp(jax.random.uniform(jax.random.fold_in(own, axis_at), (shards_of,), jnp.float32, smallest / len(split), high / len(split)))
        loudness = loudness * jnp.repeat(steps, dims[axis_at] // shards_of).reshape([-1 if axis == axis_at else 1 for axis in range(len(dims))])
    return loudness


def gaussian(key, dims, deviation, bound, split=(), held_as=jnp.bfloat16):
    entries = jax.random.normal(key, dims, jnp.float32) * deviation
    if len(split) > 0:
        entries = steps_of(key, dims, split, -0.22, 0.18) * entries
    return jnp.clip(entries, min=-bound, max=bound).astype(held_as)


def setup_inputs(seed: int = 0) -> dict:
    seeds = jax.random.split(jax.random.key(seed), 16)
    images = draw_images(jax.random.fold_in(seeds[15], 71), 0)
    upstream = gaussian(seeds[1], (GROUPS, IMAGES, ROWS, WIDTH, C_IN), 1.0, 6.0, ((1, 8), (2, 4)))
    row_counts = draw_row_counts(jax.random.fold_in(seeds[15], 71), 0)
    w_reduce = gaussian(seeds[3], (C_IN, C_MID), C_IN ** -0.5, 0.125, (), jnp.float32)
    w_spatial = gaussian(seeds[4], (PATCH, C_MID), PATCH ** -0.5, 0.09375, (), jnp.float32)
    w_expand = gaussian(seeds[5], (C_MID, C_IN), C_MID ** -0.5, 0.25, (), jnp.float32)
    norm_gain = jnp.clip(1.0 + 0.1 * jax.random.normal(seeds[6], (C_ALL,), jnp.float32), 0.5, 1.5)
    norm_bias = gaussian(seeds[7], (C_ALL,), 0.3, 1.75, (), jnp.float32)
    reduce_rows = jnp.clip(jnp.exp(math.log(140800.0) - 1.3862944 * jax.random.uniform(seeds[8], (C_IN,), jnp.float32) ** steps_of(seeds[8], (C_IN,), ((0, 8),), -0.2, 0.2)), 35200.0, 140800.0)
    reduce_cols = jnp.clip(jnp.exp(jax.random.uniform(seeds[9], (C_MID,), jnp.float32, math.log(35200.0), math.log(140800.0))), 35200.0, 140800.0)
    spatial_rows = jnp.clip(jnp.exp(math.log(84480.0) - 1.3862944 * jax.random.uniform(seeds[10], (PATCH,), jnp.float32) ** steps_of(seeds[10], (PATCH,), ((0, 8),), -0.2, 0.2)), 21120.0, 84480.0)
    spatial_cols = jnp.clip(jnp.exp(jax.random.uniform(seeds[11], (C_MID,), jnp.float32, math.log(21120.0), math.log(84480.0))), 21120.0, 84480.0)
    expand_rows = jnp.clip(jnp.exp(math.log(14080.0) - 1.3862944 * jax.random.uniform(seeds[12], (C_MID,), jnp.float32) ** steps_of(seeds[12], (C_MID,), ((0, 8),), -0.2, 0.2)), 3520.0, 14080.0)
    expand_cols = jnp.clip(jnp.exp(jax.random.uniform(seeds[13], (C_IN,), jnp.float32, math.log(3520.0), math.log(14080.0))), 3520.0, 14080.0)
    norm_state = draw_norm_state(jax.random.fold_in(seeds[15], 71), 0)
    return {"images": images, "upstream": upstream, "row_counts": row_counts, "w_reduce": w_reduce, "w_spatial": w_spatial, "w_expand": w_expand, "norm_gain": norm_gain, "norm_bias": norm_bias, "reduce_rows": reduce_rows, "reduce_cols": reduce_cols, "spatial_rows": spatial_rows, "spatial_cols": spatial_cols, "expand_rows": expand_rows, "expand_cols": expand_cols, "norm_state": norm_state}


EPS = 1e-05
EPS_ONE = 1e-30
HIGH = lax.Precision.HIGHEST

@jax.custom_vjp
def low(v):
    return lax.optimization_barrier(v.astype(jnp.bfloat16)).astype(jnp.float32)

@jax.custom_vjp
def low_back(v):
    return v

def low_keep(v):
    return (low(v), None)

def low_pass(kept, grad):
    return (grad,)

def back_keep(v):
    return (v, None)

def back_low(kept, grad):
    return (low(grad),)
low.defvjp(low_keep, low_pass)
low_back.defvjp(back_keep, back_low)

def normalize(values, valid_mask, number, gains, biases):
    mean = lax.optimization_barrier(jnp.sum(values * valid_mask, axis=0)) / number
    spread = lax.optimization_barrier(jnp.sum(values * values * valid_mask, axis=0)) / number - mean * mean
    return (values - mean) * lax.rsqrt(spread + EPS) * gains + biases

def patches_of(upper, middle, lower, across):
    pieces = []
    for row_set in (upper, middle, lower):
        padded = jnp.pad(row_set, [(0, 0)] * (row_set.ndim - 2) + [(1, 1), (0, 0)])
        for offset in range(3):
            pieces.append(lax.slice_in_dim(padded, offset, offset + across, axis=row_set.ndim - 2))
    return jnp.concatenate(pieces, axis=-1)

def neighbours(hidden, has_two):
    first_row = hidden[:, :, :, 0]
    second_row = hidden[:, :, :, 1]
    last_row = jnp.where(has_two, second_row, first_row)
    zero_row = jnp.zeros_like(first_row[:, :, :1])
    above = jnp.concatenate([zero_row, last_row[:, :, :-1]], axis=2)
    below = jnp.concatenate([first_row[:, :, 1:], zero_row], axis=2)
    upper = jnp.stack([above, first_row], axis=3)
    lower = jnp.stack([jnp.where(has_two, second_row, below), below], axis=3)
    return (upper, hidden, lower)

def factored(weight, gradient, rows_old, cols_old, beta):
    square = gradient * gradient + EPS_ONE
    rows_next = beta * rows_old + (1.0 - beta) * lax.optimization_barrier(jnp.mean(square, axis=1))
    cols_next = beta * cols_old + (1.0 - beta) * lax.optimization_barrier(jnp.mean(square, axis=0))
    second = rows_next[:, None] * cols_next[None, :] / jnp.mean(rows_next)
    rate = 0.5 * jnp.maximum(jnp.sqrt(jnp.mean(weight * weight)), 0.001)
    return (rows_next, cols_next, weight - rate * gradient * lax.rsqrt(second))

def reference(images, upstream, row_counts, w_reduce, w_spatial, w_expand, norm_gain, norm_bias, reduce_rows, reduce_cols, spatial_rows, spatial_cols, expand_rows, expand_cols, norm_state):
    per_image = jnp.repeat(row_counts, IMG_DEV, axis=1)
    slot_index = lax.broadcasted_iota(jnp.int32, (GROUPS, IMAGES, N_NARROW, SLOTS), 3)
    row_valid = slot_index < per_image[..., None]
    column_index = lax.broadcasted_iota(jnp.int32, (GROUPS, WIDTH), 1)
    group_index = lax.broadcasted_iota(jnp.int32, (GROUPS, WIDTH), 0)
    column_valid = column_index < group_index + 5
    valid = row_valid[..., None] & column_valid[:, None, None, None, :]
    valid_mask = valid.astype(jnp.float32).reshape(-1, 1)
    number = jnp.sum(valid_mask)
    has_two = (per_image == 2)[..., None, None]
    grid_shape = (GROUPS, IMAGES, N_NARROW, SLOTS, WIDTH)
    inputs = images.astype(jnp.float32).reshape(-1, C_IN)

    def forward(source, weight_one, weight_two, weight_three, gains, biases):
        conv_one = low_back(jnp.dot(source, low(weight_one), precision=HIGH, preferred_element_type=jnp.float32))
        pre_one = normalize(conv_one, valid_mask, number, gains[:C_MID], biases[:C_MID])
        hidden_one = low(jax.nn.gelu(pre_one) * valid_mask)
        upper, middle, lower = neighbours(hidden_one.reshape(grid_shape + (C_MID,)), has_two)
        patches = patches_of(upper, middle, lower, WIDTH).reshape(-1, 9 * C_MID)
        conv_two = low_back(jnp.dot(patches, low(weight_two), precision=HIGH, preferred_element_type=jnp.float32))
        pre_two = normalize(conv_two, valid_mask, number, gains[C_MID:2 * C_MID], biases[C_MID:2 * C_MID])
        hidden_two = low(jax.nn.gelu(pre_two) * valid_mask)
        conv_three = low_back(jnp.dot(hidden_two, low(weight_three), precision=HIGH, preferred_element_type=jnp.float32))
        pre_three = normalize(conv_three, valid_mask, number, gains[2 * C_MID:], biases[2 * C_MID:])
        return jax.nn.gelu(pre_three + source) * valid_mask
    result, pullback = jax.vjp(forward, inputs, w_reduce, w_spatial, w_expand, norm_gain, norm_bias)
    grads = pullback(upstream.astype(jnp.float32).reshape(-1, C_IN))
    output = result.astype(jnp.bfloat16).reshape(images.shape)
    input_grad = grads[0].astype(jnp.bfloat16).reshape(images.shape)
    beta = 1.0 - STEP ** (-0.8)
    reduce_rows_next, reduce_cols_next, reduce_next = factored(w_reduce, grads[1], reduce_rows, reduce_cols, beta)
    spatial_rows_next, spatial_cols_next, spatial_next = factored(w_spatial, grads[2], spatial_rows, spatial_cols, beta)
    expand_rows_next, expand_cols_next, expand_next = factored(w_expand, grads[3], expand_rows, expand_cols, beta)
    norm_grads = jnp.stack([grads[4], grads[5]])
    params = jnp.stack([norm_gain, norm_bias])
    norm_second = beta * norm_state + (1.0 - beta) * (norm_grads * norm_grads + EPS_ONE)
    rate = 0.5 * jnp.maximum(jnp.sqrt(lax.optimization_barrier(jnp.mean(params * params, axis=1))), 0.001)
    norm_next = params - rate[:, None] * norm_grads * lax.rsqrt(norm_second)
    return (output, input_grad, grads[1], grads[2], grads[3], reduce_rows_next, reduce_cols_next, spatial_rows_next, spatial_cols_next, expand_rows_next, expand_cols_next, reduce_next, spatial_next, expand_next, norm_grads, norm_second, norm_next)
```

```python
import functools

import jax
import jax.numpy as jnp
from jax import lax
from jax.experimental import pallas as pl
from jax.experimental.pallas import tpu as pltpu
from jax.sharding import PartitionSpec as P

MESH = pl.DeviceIdType.MESH
VMEM = pltpu.VMEM
F32 = jnp.float32
BF16 = jnp.bfloat16

STEP = 10
EPS = 1e-05
EPS_ONE = 1e-30
LIMIT = 63 * 1024 * 1024

COLUMNS = (5, 6, 7)
FIRST = (0, 5, 11)
PADDED = (1, 7, 14)
BLOCKS = 18
PADDED_BLOCKS = 22

C0 = 0.7978845608
C1 = C0 * 0.044715


def half_of(v):
    squared = v * v
    return 0.5 + 0.5 * jnp.tanh(v * (C0 + C1 * squared)), squared


def slope_of(v, h, squared):
    return h + v * h * (1.0 - h) * (2.0 * C0 + 6.0 * C1 * squared)


def dot(a, b):
    return jnp.dot(a, b, preferred_element_type=F32)


def dot_t(a, b):
    return lax.dot_general(a, b, (((1,), (1,)), ((), ())), preferred_element_type=F32)


def to_rows(lanes):
    size = 16 * lanes
    to = lax.broadcasted_iota(jnp.int32, (size, size), 0)
    at = lax.broadcasted_iota(jnp.int32, (size, size), 1)
    return (at == lax.rem(to, 8) * (2 * lanes) + to // 8).astype(F32).astype(BF16)


def from_rows(lanes):
    size = 16 * lanes
    to = lax.broadcasted_iota(jnp.int32, (size, size), 1)
    at = lax.broadcasted_iota(jnp.int32, (size, size), 0)
    return (at == lax.rem(to, 8) * (2 * lanes) + to // 8).astype(F32).astype(BF16)


def turn_in(order, load, stage):
    count = stage.shape[0]
    for k in range(0, count, 2):
        if k + 1 < count:
            both = dot(order, jnp.concatenate([load(k), load(k + 1)], axis=1))
            stage[k] = both[:, :128]
            stage[k + 1] = both[:, 128:]
        else:
            stage[k] = dot(order, load(k))


def turn_out(order, stage, store):
    count = stage.shape[0]
    for k in range(0, count, 2):
        if k + 1 < count:
            both = jnp.concatenate([stage[k].astype(BF16), stage[k + 1].astype(BF16)], axis=1)
            both = dot(order, both).astype(BF16)
            store(k, both[:, :128])
            store(k + 1, both[:, 128:])
        else:
            store(k, dot(order, stage[k].astype(BF16)).astype(BF16))


def staged(stage, c, slot):
    row = (2 * c + slot) * 8
    return jnp.concatenate([stage[k, row : row + 8, :] for k in range(stage.shape[0])], axis=0)


def put_staged(stage, c, slot, value):
    row = (2 * c + slot) * 8
    for k in range(stage.shape[0]):
        stage[k, row : row + 8, :] = value[8 * k : 8 * k + 8]


def cast_rows(value_ref, wb_ref, row, square):
    step = 64

    def add(k, square):
        value = value_ref[pl.ds(pl.multiple_of(k * step, step), step), :]
        wb_ref[pl.ds(pl.multiple_of(row + k * step, step), step), :] = value.astype(BF16)
        return square + jnp.sum((value * value).reshape(step // 8, 8, value.shape[1]), axis=0)

    return lax.fori_loop(0, value_ref.shape[0] // step, add, square)


def reduce_scratch(n, w, rows, channels):
    return [
        VMEM((n, rows, channels), F32),
        VMEM((w, rows, channels), F32),
        pltpu.SemaphoreType.DMA((n,)),
        pltpu.SemaphoreType.DMA((n,)),
        pltpu.SemaphoreType.DMA((w,)),
        pltpu.SemaphoreType.DMA((w,)),
    ]


def greet(n, w):
    me_n, me_w = lax.axis_index("narrow"), lax.axis_index("wide")
    barrier = pltpu.get_barrier_semaphore()
    for k in range(1, n):
        pl.semaphore_signal(
            barrier, inc=1, device_id={"narrow": lax.rem(me_n + k, n)}, device_id_type=MESH
        )
    for k in range(1, w):
        pl.semaphore_signal(
            barrier, inc=1, device_id={"wide": lax.rem(me_w + k, w)}, device_id_type=MESH
        )


def met(n, w):
    pl.semaphore_wait(pltpu.get_barrier_semaphore(), n + w - 2)


def sum_over(axis, size, value, slots, send, recv):
    me = lax.axis_index(axis)
    slots[me] = value
    copies = []
    for k in range(1, size):
        copy = pltpu.make_async_remote_copy(
            src_ref=slots.at[me],
            dst_ref=slots.at[me],
            send_sem=send.at[k],
            recv_sem=recv.at[k],
            device_id={axis: lax.rem(me + k, size)},
            device_id_type=MESH,
        )
        copy.start()
        copies.append(copy)
    for copy in copies:
        copy.wait_recv()
    total = slots[0]
    for k in range(1, size):
        total = total + slots[k]
    for copy in copies:
        copy.wait_send()
    return total


class SumAll:
    def __init__(self, n, w, scratch):
        self.axes = (("narrow", n, scratch[0], *scratch[2:4]), ("wide", w, scratch[1], *scratch[4:6]))
        self.copies = [[], []]

    def send(self, which, value):
        axis, size, slots, send, recv = self.axes[which]
        me = lax.axis_index(axis)
        slots[me] = value
        for k in range(1, size):
            copy = pltpu.make_async_remote_copy(
                src_ref=slots.at[me],
                dst_ref=slots.at[me],
                send_sem=send.at[k],
                recv_sem=recv.at[k],
                device_id={axis: lax.rem(me + k, size)},
                device_id_type=MESH,
            )
            copy.start()
            self.copies[which].append(copy)

    def total(self, which):
        _, size, slots, _, _ = self.axes[which]
        for copy in self.copies[which]:
            copy.wait_recv()
        total = slots[0]
        for k in range(1, size):
            total = total + slots[k]
        return total

    def begin(self, value):
        self.send(0, value)

    def middle(self):
        self.send(1, self.total(0))

    def end(self):
        total = self.total(1)
        for copies in self.copies:
            for copy in copies:
                copy.wait_send()
        return total


def forward_scale(stats, params, number):
    mean = stats[0:1] / number
    scale = lax.rsqrt(stats[1:2] / number - mean * mean + EPS)
    a = scale * params[0]
    return a, params[1] - mean * a, scale, mean


def backward_scale(stats, params, grads, number):
    mean = stats[0:1] / number
    scale = lax.rsqrt(stats[1:2] / number - mean * mean + EPS)
    a = scale * params[0]
    gain_grad, bias_grad = grads[0:1], grads[1:2]
    over = a / number
    return a, over * scale * gain_grad, over * (bias_grad - mean * scale * gain_grad)


def norm_params(gain_ref, bias_ref, which, inner):
    lane = (0, inner, 2 * inner, gain_ref.shape[1])
    at = slice(lane[which], lane[which + 1])
    return gain_ref[0:1, at], bias_ref[0:1, at]


def second_counts(counts_ref, g):
    return jnp.where(counts_ref[g] == 2, 1.0, 0.0)


def two_sums(first, second, m):
    return jnp.sum(first, axis=(0, 1))[None] + m * jnp.sum(second, axis=(0, 1))[None]


def padded_rows(count):
    return -(-count // 16) * 16


def halo_rows(images):
    starts, at = [], 0
    for g in range(3):
        starts.append(at)
        at += padded_rows(COLUMNS[g] * images)
    return starts, at


def pack_halo(value):
    count = value.shape[0] * value.shape[1]
    value = value.reshape(count, value.shape[2])
    extra = padded_rows(count) - count
    if extra:
        value = jnp.concatenate([value, jnp.zeros((extra, value.shape[1]), F32)], axis=0)
    return value.astype(BF16)


def unpack_halo(value, columns, images):
    return value.astype(F32)[: columns * images].reshape(columns, images, value.shape[1])


def halo_copies(n, g, count, starts, up_src, up_dst, down_src, down_dst, sems):
    me = lax.axis_index("narrow")
    rows = pl.ds(starts[g], count)
    forward = pltpu.make_async_remote_copy(
        src_ref=up_src.at[rows],
        dst_ref=up_dst.at[rows],
        send_sem=sems.at[0, g],
        recv_sem=sems.at[1, g],
        device_id={"narrow": lax.rem(me + 1, n)},
        device_id_type=MESH,
    )
    backward = pltpu.make_async_remote_copy(
        src_ref=down_src.at[rows],
        dst_ref=down_dst.at[rows],
        send_sem=sems.at[2, g],
        recv_sem=sems.at[3, g],
        device_id={"narrow": lax.rem(me + n - 1, n)},
        device_id_type=MESH,
    )
    return forward, backward


def halo_start(n, copies):
    me = lax.axis_index("narrow")

    @pl.when(me < n - 1)
    def _():
        copies[0].start()

    @pl.when(me > 0)
    def _():
        copies[1].start()


def halo_arrived(n, copies):
    me = lax.axis_index("narrow")

    @pl.when(me > 0)
    def _():
        copies[0].wait_recv()

    @pl.when(me < n - 1)
    def _():
        copies[1].wait_recv()


def halo_sent(n, copies):
    me = lax.axis_index("narrow")

    @pl.when(me < n - 1)
    def _():
        copies[0].wait_send()

    @pl.when(me > 0)
    def _():
        copies[1].wait_send()


def halo_edges(n, from_before, from_after):
    me = lax.axis_index("narrow")

    @pl.when(me == 0)
    def _():
        from_before[...] = jnp.zeros(from_before.shape, from_before.dtype)

    @pl.when(me == n - 1)
    def _():
        from_after[...] = jnp.zeros(from_after.shape, from_after.dtype)


RING = 6
CHUNK = 512


def place_of(t):
    g = (t >= FIRST[1]).astype(jnp.int32) + (t >= FIRST[2]).astype(jnp.int32)
    return g, t - jnp.where(g == 0, FIRST[0], jnp.where(g == 1, FIRST[1], FIRST[2]))


def forward_kernel(
    n, w, number, x_ref, reduce_ref, spatial_ref, expand_ref, gain_ref, bias_ref, counts_ref,
    rows_out, one_out, two_out, upper_out, middle_out, lower_out, hidden_out, three_out,
    reduce_out, spatial_out, expand_out,
    stat_one, stat_two, stat_three, square_reduce, square_spatial, square_expand,
    ring, rows, weight, wide_weight, reduce, spatial, expand, one, two, upper, middle, lower, hidden, three,
    stage_one, stage_two, order, last, first, above, below, halo_sems, ring_sems, weight_sems, wide_sem, out_sems,
    *scratch,
):
    m = [second_counts(counts_ref, g) for g in range(3)]
    stages = (stage_one, stage_two)
    sum_one = SumAll(n, w, scratch[:6])
    sum_two = SumAll(n, w, scratch[6:12])
    sum_three = SumAll(n, w, scratch[12:18])
    images = x_ref.shape[1]
    lanes = x_ref.shape[3] // 2
    channels = one.shape[3]
    block = 2 * images
    tail = BLOCKS * block
    starts, _ = halo_rows(images)
    outs = []

    def put(source, target):
        copy = pltpu.make_async_copy(source, target, out_sems.at[len(outs)])
        copy.start()
        outs.append(copy)

    def fetch(t):
        g, j = place_of(t)
        slot = lax.rem(t, RING)
        return pltpu.make_async_copy(x_ref.at[g, :, j], ring.at[slot], ring_sems.at[slot])

    sources = [reduce_ref.at[k : k + CHUNK] for k in range(0, reduce_ref.shape[0], CHUNK)]
    reduce_chunks = len(sources)
    sources += [spatial_ref.at[k : k + CHUNK] for k in range(0, spatial_ref.shape[0], CHUNK)]
    slots = weight.shape[0]

    def weight_copy(k):
        return pltpu.make_async_copy(sources[k], weight.at[k % slots], weight_sems.at[k % slots])

    for t in range(RING):
        fetch(jnp.int32(t)).start()
    for k in range(slots):
        weight_copy(k).start()
    wide_copy = pltpu.make_async_copy(expand_ref, wide_weight, wide_sem)
    wide_copy.start()
    greet(n, w)
    order[...] = to_rows(lanes)
    rows[tail:, :] = jnp.zeros((rows.shape[0] - tail, rows.shape[1]), BF16)
    for ref in (upper, middle, lower):
        for at in (0, PADDED[1] - 1, PADDED[2] - 1, PADDED_BLOCKS - 1):
            ref[at * block : (at + 1) * block] = jnp.zeros((block, channels), BF16)
    halo_edges(n, above, below)

    def cast_chunk(k, wb_ref, row, square):
        weight_copy(k).wait()
        square = cast_rows(weight.at[k % slots], wb_ref, row, square)
        if k + slots < len(sources):
            weight_copy(k + slots).start()
        return square

    def place(i, _):
        for k in range(2):
            fetch(2 * i + k).wait()
        for k, stage in enumerate(stages):
            slot = lax.rem(2 * i + k, RING)
            turn_in(
                order[...],
                lambda j, slot=slot: ring[slot, 8 * j : 8 * j + 8].reshape(16 * lanes, 128),
                stage,
            )
        for k, stage in enumerate(stages):
            row = pl.multiple_of((2 * i + k) * block, block)
            for c in range(lanes):
                rows[pl.ds(row, block), c * 128 : (c + 1) * 128] = jnp.concatenate(
                    [staged(stage, c, 0), staged(stage, c, 1)], axis=0
                ).astype(BF16)

        @pl.when(2 * i + RING < BLOCKS)
        def _():
            for k in range(2):
                fetch(2 * i + k + RING).start()

        return 0

    lax.fori_loop(0, BLOCKS // 2, place, 0)
    put(rows, rows_out)
    square = jnp.zeros((8, channels), F32)
    for k in range(reduce_chunks):
        square = cast_chunk(k, reduce, k * CHUNK, square)
    square_reduce[...] = jnp.sum(square, axis=0, keepdims=True)
    put(reduce, reduce_out)
    sums = jnp.zeros((1, channels), F32)
    squares = jnp.zeros((1, channels), F32)
    for g in range(3):
        at = slice(FIRST[g] * block, (FIRST[g] + COLUMNS[g]) * block)
        c = dot(rows[at, :], reduce[...]).reshape(COLUMNS[g], 2, images, channels)
        one[FIRST[g] : FIRST[g] + COLUMNS[g]] = c
        sums = sums + two_sums(c[:, 0], c[:, 1], m[g])
        squares = squares + two_sums(c[:, 0] * c[:, 0], c[:, 1] * c[:, 1], m[g])
    met(n, w)
    sum_one.begin(jnp.concatenate([sums, squares], axis=0))
    put(one, one_out)
    square = jnp.zeros((8, channels), F32)
    middle_chunk = (reduce_chunks + len(sources)) // 2
    for k in range(reduce_chunks, middle_chunk):
        square = cast_chunk(k, spatial, (k - reduce_chunks) * CHUNK, square)
    sum_one.middle()
    for k in range(middle_chunk, len(sources)):
        square = cast_chunk(k, spatial, (k - reduce_chunks) * CHUNK, square)
    square_spatial[...] = jnp.sum(square, axis=0, keepdims=True)
    put(spatial, spatial_out)
    stats = sum_one.end()
    stat_one[...] = stats

    a, b, _, _ = forward_scale(stats, norm_params(gain_ref, bias_ref, 0, channels), number)
    copies = []
    for g in range(3):
        v = one[FIRST[g] : FIRST[g] + COLUMNS[g]] * a + b
        value = v * half_of(v)[0]
        slot_one, slot_two = value[:, 0], value[:, 1] * m[g]
        count = padded_rows(COLUMNS[g] * images)
        first[starts[g] : starts[g] + count] = pack_halo(slot_one)
        last[starts[g] : starts[g] + count] = pack_halo(
            jnp.where(m[g] > 0.5, slot_two, slot_one)
        )
        copies.append(halo_copies(n, g, count, starts, last, above, first, below, halo_sems))
        halo_start(n, copies[g])
        both = jnp.stack([slot_one, slot_two], axis=1).reshape(COLUMNS[g] * block, channels)
        middle[PADDED[g] * block : (PADDED[g] + COLUMNS[g]) * block] = both.astype(BF16)

    def taps(ref, g, level):
        at, count = PADDED[g] * block, COLUMNS[g] * block
        shifted = [ref[at + d * block : at + d * block + count, :] for d in (-1, 0, 1)]
        return dot(
            jnp.concatenate(shifted, axis=1),
            spatial[3 * level * channels : 3 * (level + 1) * channels, :],
        )

    def put_groups(source, target):
        for g in range(3):
            count = COLUMNS[g] * block
            put(
                source.at[PADDED[g] * block : PADDED[g] * block + count],
                target.at[FIRST[g] * block : FIRST[g] * block + count],
            )

    for g in range(3):
        two[FIRST[g] : FIRST[g] + COLUMNS[g]] = taps(middle, g, 1).reshape(
            COLUMNS[g], 2, images, channels
        )
    put_groups(middle, middle_out)
    sums = jnp.zeros((1, channels), F32)
    squares = jnp.zeros((1, channels), F32)
    for g in range(3):
        halo_arrived(n, copies[g])
        at, count = PADDED[g] * block, COLUMNS[g] * block
        height = padded_rows(COLUMNS[g] * images)
        up = unpack_halo(above[starts[g] : starts[g] + height], COLUMNS[g], images)
        down = unpack_halo(below[starts[g] : starts[g] + height], COLUMNS[g], images)
        own = middle[at : at + count].astype(F32).reshape(COLUMNS[g], 2, images, channels)
        upper[at : at + count] = (
            jnp.stack([up, own[:, 0]], axis=1).reshape(count, channels).astype(BF16)
        )
        lower[at : at + count] = (
            jnp.stack([jnp.where(m[g] > 0.5, own[:, 1], down), down], axis=1)
            .reshape(count, channels)
            .astype(BF16)
        )
        c = taps(upper, g, 0) + taps(lower, g, 2)
        c = c.reshape(COLUMNS[g], 2, images, channels) + two[FIRST[g] : FIRST[g] + COLUMNS[g]]
        two[FIRST[g] : FIRST[g] + COLUMNS[g]] = c
        sums = sums + two_sums(c[:, 0], c[:, 1], m[g])
        squares = squares + two_sums(c[:, 0] * c[:, 0], c[:, 1] * c[:, 1], m[g])
    sum_two.begin(jnp.concatenate([sums, squares], axis=0))
    put(two, two_out)
    put_groups(upper, upper_out)
    put_groups(lower, lower_out)
    wide_copy.wait()
    half = wide_weight.shape[0] // 2
    square = jnp.zeros((8, wide_weight.shape[1]), F32)
    square = cast_rows(wide_weight.at[:half], expand, 0, square)
    sum_two.middle()
    square = cast_rows(wide_weight.at[half:], expand, half, square)
    square_expand[...] = jnp.sum(square, axis=0, keepdims=True)
    put(expand, expand_out)
    for g in range(3):
        halo_sent(n, copies[g])
    stats = sum_two.end()
    stat_two[...] = stats

    a, b, _, _ = forward_scale(stats, norm_params(gain_ref, bias_ref, 1, channels), number)
    for g in range(3):
        v = two[FIRST[g] : FIRST[g] + COLUMNS[g]] * a + b
        value = v * half_of(v)[0]
        both = jnp.stack([value[:, 0], value[:, 1] * m[g]], axis=1)
        hidden[FIRST[g] * block : (FIRST[g] + COLUMNS[g]) * block] = both.reshape(
            COLUMNS[g] * block, channels
        ).astype(BF16)
    put(hidden, hidden_out.at[:tail])
    sums, squares = [], []
    for part in range(three.shape[1] // 512):
        s = jnp.zeros((1, 512), F32)
        q = jnp.zeros((1, 512), F32)
        columns = slice(part * 512, (part + 1) * 512)
        for g in range(3):
            at = slice(FIRST[g] * block, (FIRST[g] + COLUMNS[g]) * block)
            c = dot(hidden[at, :], expand[:, columns])
            three[at, columns] = c.astype(BF16)
            s = s + jnp.sum(c, axis=0, keepdims=True)
            q = q + jnp.sum(c * c, axis=0, keepdims=True)
        put(three.at[:, columns], three_out.at[:, columns])
        sums.append(s)
        squares.append(q)
    sum_three.begin(
        jnp.concatenate(
            [jnp.concatenate(sums, axis=1), jnp.concatenate(squares, axis=1)], axis=0
        )
    )
    sum_three.middle()
    stat_three[...] = sum_three.end()
    for copy in outs:
        copy.wait()


DEPTH = 4


def top_kernel(
    number, inner, conv_ref, rows_ref, up_ref, stats_ref, gain_ref, bias_ref, counts_ref,
    out_ref, grad_ref, total,
    conv_ring, rows_ring, up_ring, out_ring, grad_ring, up_one, up_two, out_one, out_two, order, coefficients, sems,
):
    images = up_ref.shape[1]
    lanes = up_ref.shape[3] // 2
    block = 2 * images

    def rows_of(t):
        return pl.ds(pl.multiple_of(t * block, block), block)

    def copy(which, t):
        slot = lax.rem(t, DEPTH)
        g, j = place_of(t)
        source, target = (
            lambda: (conv_ref.at[rows_of(t)], conv_ring.at[slot]),
            lambda: (rows_ref.at[rows_of(t)], rows_ring.at[slot]),
            lambda: (up_ref.at[g, :, j], up_ring.at[slot]),
            lambda: (out_ring.at[slot], out_ref.at[g, :, j]),
            lambda: (grad_ring.at[slot], grad_ref.at[rows_of(t)]),
        )[which]()
        return pltpu.make_async_copy(source, target, sems.at[which, slot])

    def each(which, t, do):
        @pl.when((t >= 0) & (t < BLOCKS))
        def _():
            do(copy(which, t))

    def start(which, t):
        each(which, t, lambda c: c.start())

    def wait(which, t):
        each(which, t, lambda c: c.wait())

    for t in range(3):
        start(2, jnp.int32(t))
        if t < 2:
            start(0, jnp.int32(t))
            start(1, jnp.int32(t))
    total[...] = jnp.zeros(total.shape, F32)
    params = norm_params(gain_ref, bias_ref, 2, inner)
    a, b, scale, mean = forward_scale(stats_ref[...], params, number)
    coefficients[0:1] = a
    coefficients[1:2] = b
    order[0] = to_rows(lanes)
    order[1] = from_rows(lanes)
    out_two[...] = jnp.zeros(out_two.shape, F32)

    def enter(t, stage):
        slot = lax.rem(t, DEPTH)
        turn_in(
            order[0], lambda k: up_ring[slot, 8 * k : 8 * k + 8].reshape(16 * lanes, 128), stage
        )

    def leave(t, stage):
        slot = lax.rem(t + DEPTH, DEPTH)

        def store(k, value):
            out_ring[slot, 8 * k : 8 * k + 8] = value.reshape(8, 2 * lanes, 128)

        turn_out(order[1], stage, store)

    def work(t, stage_up, stage_out):
        slot = lax.rem(t, DEPTH)
        m = second_counts(counts_ref, place_of(t)[0])
        for c in range(lanes):
            at = slice(c * 128, (c + 1) * 128)
            raw = conv_ring[slot, :, at].astype(F32)
            v = raw * coefficients[0:1, at] + coefficients[1:2, at]
            v = v + rows_ring[slot, :, at].astype(F32)
            h, squared = half_of(v)
            out = v * h
            slope = h + out * (1.0 - h) * (2.0 * C0 + 6.0 * C1 * squared)
            put_staged(stage_out, c, 0, out[:images])
            put_staged(stage_out, c, 1, out[images:] * m)
            grad = jnp.concatenate(
                [
                    slope[:images] * staged(stage_up, c, 0),
                    slope[images:] * (staged(stage_up, c, 1) * m),
                ],
                axis=0,
            )
            grad_ring[slot, :, at] = grad.astype(BF16)
            total[0, :, at] += jnp.sum((grad * raw).reshape(block // 8, 8, 128), axis=0)
            total[1, :, at] += jnp.sum(grad.reshape(block // 8, 8, 128), axis=0)

    wait(2, jnp.int32(0))
    enter(jnp.int32(0), up_one)

    def pair(i, _):
        t = 2 * i
        for k in (2, 3):
            start(0, t + k)
            start(1, t + k)
            start(2, t + k + 1)
        for k in (0, 1):
            wait(0, t + k)
            wait(1, t + k)
            wait(2, t + k + 1)
            wait(3, t + k - 1 - DEPTH)
            wait(4, t + k - DEPTH)
        enter(t + 1, up_two)
        work(t, up_one, out_one)
        leave(t - 1, out_two)
        enter(t + 2, up_one)
        work(t + 1, up_two, out_two)
        leave(t, out_one)
        for k in (0, 1):
            start(3, t + k - 1)
            start(4, t + k)
        return 0

    lax.fori_loop(0, BLOCKS // 2, pair, 0)
    last = jnp.int32(BLOCKS - 1)
    wait(3, last - DEPTH)
    leave(last, out_two)
    start(3, last)
    for k in range(DEPTH):
        wait(3, last - k)
        wait(4, last - k)
    out_ring[0] = jnp.zeros(out_ring.shape[1:], BF16)
    copies = []
    for g in range(3):
        for j in range(COLUMNS[g], out_ref.shape[2]):
            copies.append(
                pltpu.make_async_copy(
                    out_ring.at[0], out_ref.at[g, :, j], sems.at[5, len(copies)]
                )
            )
            copies[-1].start()
    value = jnp.sum(total[...], axis=1)
    gains = scale * (value[0:1] - mean * value[1:2])
    total[0] = jnp.concatenate([gains, jnp.zeros((7, gains.shape[1]), F32)], axis=0)
    for copy in copies:
        copy.wait()


def unravel(index, sizes):
    digits = []
    for size in reversed(sizes):
        digits.append(index % size if isinstance(index, int) else lax.rem(index, size))
        index = index // size if isinstance(index, int) else lax.div(index, size)
    return digits[::-1]


def mesh_digits(n, w):
    if (n, w) == (4, 8):
        return (
            [("narrow", 2, 2), ("narrow", 1, 2), ("wide", 2, 4), ("wide", 1, 2)],
            [(1, 3, 0, 2), (1, 0, 3, 2)],
        )
    return [("narrow", 1, n), ("wide", 1, w)], [(0, 1), (0, 1)]


def digit_sizes(n, w):
    return [d[2] for d in mesh_digits(n, w)[0]]


def narrow_digits(n, w):
    return [d[2] for d in mesh_digits(n, w)[0] if d[0] == "narrow"]


def wide_digits(n, w):
    return [d[2] for d in mesh_digits(n, w)[0] if d[0] == "wide"]


def weight_parts(w, rows):
    share = rows // w
    if rows >= 4096 and share % 64 == 0:
        return 4
    return 2 if share % 32 == 0 else 1


def block_shapes(n, w, rows, columns):
    parts = weight_parts(w, rows)
    return [(*digit_sizes(n, w), rows // w // parts, columns // n)] * parts


def put_blocks(n, w, refs, value, row, rows, place_n=None, place_w=0, lane=0):
    share = rows // w
    part = share // len(refs)
    at, end = row, row + value.shape[0]
    columns = refs[0].shape[-1]
    while at < end:
        stop = min(end, (at // part + 1) * part)
        wide = at // share
        ref = refs[at // part % len(refs)]
        inside = slice(at % part, at % part + stop - at)
        piece = value[at - row : stop - row]
        wide = unravel(place_w + wide, wide_digits(n, w))
        if place_n is not None:
            lanes = slice(lane, lane + piece.shape[1])
            ref[(*unravel(place_n, narrow_digits(n, w)), *wide, inside, lanes)] = piece.astype(BF16)
        else:
            for k in range(n):
                ref[(*unravel(k, narrow_digits(n, w)), *wide, inside, slice(None))] = piece[
                    :, k * columns : (k + 1) * columns
                ].astype(BF16)
        at = stop


def scatter_scratch(n, w, rows, columns):
    digits, orders = mesh_digits(n, w)
    scratch = []
    for part, shape in enumerate(block_shapes(n, w, rows, columns)):
        left = list(range(len(digits)))
        for d in orders[part % 2]:
            left.remove(d)
            size = digits[d][2]
            scratch.append(VMEM((size - 1, *(digits[k][2] for k in left), *shape[-2:]), BF16))
            scratch.append(pltpu.SemaphoreType.DMA((size - 1,)))
            scratch.append(pltpu.SemaphoreType.DMA((size - 1,)))
    return scratch


class Scatter:
    def __init__(self, n, w, source, scratch, order):
        self.digits = mesh_digits(n, w)[0]
        self.order = order
        self.scratch = scratch
        self.sources = [source] + [scratch[3 * k].at[0] for k in range(len(order))]
        self.copies = []
        self.steps = len(order)

    def own(self, d):
        axis, stride, size = self.digits[d]
        return lax.rem(lax.div(lax.axis_index(axis), stride), size)

    def pick(self, ref, step, value):
        left = [d for d in range(len(self.digits)) if d not in self.order[:step]]
        return ref.at[tuple(value if d == self.order[step] else slice(None) for d in left)]

    def start(self, step):
        d = self.order[step]
        axis, stride, size = self.digits[d]
        landing, send, recv = self.scratch[3 * step : 3 * step + 3]
        mine = self.own(d)
        for k in range(1, size):
            other = lax.rem(mine + k, size)
            copy = pltpu.make_async_remote_copy(
                src_ref=self.pick(self.sources[step], step, other),
                dst_ref=landing.at[k - 1],
                send_sem=send.at[k - 1],
                recv_sem=recv.at[k - 1],
                device_id={axis: lax.axis_index(axis) + (other - mine) * stride},
                device_id_type=MESH,
            )
            copy.start()
            self.copies.append((step, copy))

    def finish(self, step):
        for at, copy in self.copies:
            if at == step:
                copy.wait_recv()
        d = self.order[step]
        size = self.digits[d][2]
        landing = self.scratch[3 * step]
        left = [k for k in range(len(self.digits)) if k not in self.order[: step + 1]]
        sizes = [self.digits[k][2] for k in left]
        mine = self.own(d)
        source = self.pick(self.sources[step], step, mine)

        def total(at):
            value = source[at].astype(F32)
            for k in range(size - 1):
                value = value + landing[(k, *at)].astype(F32)
            return value

        if step == self.steps - 1:
            return total((slice(None), slice(None)))
        count = 1
        for k in sizes:
            count *= k

        def add(index, _):
            at = tuple(unravel(index, sizes))
            landing[(0, *at)] = total(at).astype(BF16)
            return 0

        lax.fori_loop(0, count, add, 0)

    def done(self):
        for _, copy in self.copies:
            copy.wait_send()


def share_out(n, slots, value, send, recv):
    me = lax.axis_index("narrow")
    row = 0
    for piece in value:
        slots[me, row : row + piece.shape[0]] = piece.astype(BF16)
        row += piece.shape[0]
    copies = []
    for k in range(1, n):
        copy = pltpu.make_async_remote_copy(
            src_ref=slots.at[me],
            dst_ref=slots.at[me],
            send_sem=send.at[k],
            recv_sem=recv.at[k],
            device_id={"narrow": lax.rem(me + k, n)},
            device_id_type=MESH,
        )
        copy.start()
        copies.append(copy)
    return copies


BETA = 1.0 - STEP ** (-0.8)


class Refs:
    def __init__(self, refs):
        self.refs = list(refs)

    def take(self, count):
        taken, self.refs = self.refs[:count], self.refs[count:]
        return taken

    def one(self):
        return self.take(1)[0]


def backward_kernel(
    n, w, number, shapes, three_ref, grad_ref, hidden_ref, expand_ref, two_ref, spatial_ref,
    upper_ref, middle_ref, lower_ref, one_ref, rows_ref, reduce_ref, sums_ref, stat_one, stat_two, stat_three,
    gain_ref, bias_ref, counts_ref, reduce_rows_ref, spatial_rows_ref, expand_rows_ref, *refs,
):
    refs = Refs(refs)
    parts = [weight_parts(w, shape[0]) for shape in shapes]
    input_ref, columns_ref = refs.take(2)
    shares = refs.take(3)
    norm_one, norm_two, norm_three = refs.take(3)
    three, wide, hidden, turned, expand, spatial, two, one, u, coefficients = refs.take(10)
    backs = refs.take(2)
    ring, order, ring_sems = refs.take(3)
    to_before, to_after, from_after, from_before, halo_sems, in_sems = refs.take(6)
    gradients = [refs.take(parts[k]) for k in range(3)]
    orders = mesh_digits(n, w)[1]
    steps = len(orders[0])
    scatters = [
        [
            Scatter(n, w, gradients[k][p], refs.take(3 * steps), orders[p % 2])
            for p in range(parts[k])
        ]
        for k in range(3)
    ]
    share_sems = [refs.take(2) for _ in range(3)]
    sum_three = SumAll(n, w, refs.take(6))
    sum_two = SumAll(n, w, refs.take(6))
    sum_one = SumAll(n, w, refs.take(6))
    column_scratch = refs.take(3)

    images = two.shape[2]
    channels = two.shape[3]
    block = 2 * images
    tail = BLOCKS * block
    deep = three.shape[0]
    m = [second_counts(counts_ref, g) for g in range(3)]
    starts, _ = halo_rows(images)

    ins = {}

    def get(name, source, target):
        ins[name] = pltpu.make_async_copy(source, target, in_sems.at[len(ins)])
        ins[name].start()

    get("hidden", hidden_ref.at[:tail], hidden.at[:tail])
    get("three", three_ref, three.at[:tail])
    get("grad", grad_ref, wide.at[:tail])
    get("expand", expand_ref, expand)
    get("two", two_ref, two)
    get("spatial", spatial_ref, spatial)
    get("one", one_ref, one)
    greet(n, w)

    def norm_scale(which, stat, grads):
        params = norm_params(gain_ref, bias_ref, which, channels)
        return backward_scale(stat[...], params, grads, number)

    def turn(source, columns, target):
        for k in range(deep // 128):
            target[:, k * 128 : (k + 1) * 128] = source[k * 128 : (k + 1) * 128, columns].T

    sent = {}

    def advance(which, step, half=None):
        if step >= steps:
            return
        count = parts[which]
        if half is not None and count == 1:
            if half == 0:
                return
            half = None
        first = 0 if half is None else half * (count // 2)
        last = count if half is None else first + count // 2
        for scatter in scatters[which][first:last]:
            value = scatter.finish(step)
            if step < steps - 1:
                scatter.start(step + 1)
            else:
                sent.setdefault(which, []).append(value)
        if step == steps - 1 and last == count:
            sent[which] = share_out(n, shares[which], sent[which], *share_sems[which])

    def launch(which):
        for scatter in scatters[which]:
            scatter.start(0)

    value = jnp.concatenate(
        [sums_ref[0, 0:1], jnp.sum(sums_ref[1], axis=0, keepdims=True)],
        axis=0,
    )
    halo_edges(n, from_before, from_after)
    for back in backs:
        back[tail:] = jnp.zeros((deep - tail, back.shape[1]), BF16)
    hidden[tail:deep] = jnp.zeros((deep - tail, channels), BF16)
    met(n, w)
    sum_three.begin(value)
    ins["hidden"].wait()
    turn(hidden, slice(0, channels), turned.at[0])
    sum_three.middle()
    ins["three"].wait()
    ins["grad"].wait()
    ins["expand"].wait()
    grads = sum_three.end()
    norm_three[...] = grads
    a, b, c = norm_scale(2, stat_three, grads)
    coefficients[0:1] = a
    coefficients[1:2] = b
    coefficients[2:3] = c
    width = backs[0].shape[1]

    def back_three(k, back):
        at = slice(k * width, (k + 1) * width)
        a, b, c = coefficients[0:1, at], coefficients[1:2, at], coefficients[2:3, at]
        for g in range(3):
            rows = slice(FIRST[g] * block, (FIRST[g] + COLUMNS[g]) * block)
            up = wide[rows, at].astype(F32) * a
            raw = (three[rows, at].astype(F32) * b + c).reshape(COLUMNS[g], 2, images, width)
            raw = jnp.stack([raw[:, 0], raw[:, 1] * m[g]], axis=1).reshape(up.shape)
            back[rows, :] = (up - raw).astype(BF16)

    count = expand.shape[1] // width
    per = count // n
    back_three(0, backs[0])
    for k in range(count):
        back = backs[k % 2]
        if k + 1 < count:
            back_three(k + 1, backs[(k + 1) % 2])
        value = dot(turned[0], back[...])
        put_blocks(
            n, w, gradients[2], value, 0, channels, place_n=k // per, lane=k % per * width
        )
        for g in range(3):
            rows = slice(FIRST[g] * block, (FIRST[g] + COLUMNS[g]) * block)
            blocks = slice(FIRST[g], FIRST[g] + COLUMNS[g])
            value = dot_t(back[rows, :], expand[:, k * width : (k + 1) * width]).reshape(
                COLUMNS[g], 2, images, channels
            )
            u[blocks] = value if k == 0 else u[blocks] + value
    launch(2)
    for k, source in enumerate((upper_ref, middle_ref, lower_ref)):
        get(k, source.at[:tail], wide.at[:tail, k * channels : (k + 1) * channels])
    wide[tail:, :] = jnp.zeros((deep - tail, wide.shape[1]), BF16)

    ins["two"].wait()
    a, b, scale, mean = forward_scale(
        stat_two[...], norm_params(gain_ref, bias_ref, 1, channels), number
    )
    sums = jnp.zeros((1, channels), F32)
    gains = jnp.zeros((1, channels), F32)
    for g in range(3):
        blocks = slice(FIRST[g], FIRST[g] + COLUMNS[g])
        raw = two[blocks]
        v = raw * a + b
        value = slope_of(v, *half_of(v)) * u[blocks]
        value = jnp.stack([value[:, 0], value[:, 1] * m[g]], axis=1)
        u[blocks] = value
        sums = sums + jnp.sum(value, axis=(0, 1, 2))[None]
        gains = gains + jnp.sum(value * ((raw - mean) * scale), axis=(0, 1, 2))[None]
    sum_two.begin(jnp.concatenate([gains, sums], axis=0))
    for at in (0, PADDED[1] - 1, PADDED[2] - 1, PADDED_BLOCKS - 1):
        hidden[at * block : (at + 1) * block] = jnp.zeros((block, channels), BF16)
    ins[0].wait()
    turn(wide, slice(0, channels), turned.at[0])
    sum_two.middle()
    for k in (1, 2):
        ins[k].wait()
        turn(wide, slice(k * channels, (k + 1) * channels), turned.at[k])
    get("rows", rows_ref, wide)
    grads = sum_two.end()
    norm_two[...] = grads
    a, b, c = norm_scale(1, stat_two, grads)
    for g in range(3):
        blocks = slice(FIRST[g], FIRST[g] + COLUMNS[g])
        up = u[blocks] * a
        raw = two[blocks] * b + c
        value = jnp.stack([up[:, 0] - raw[:, 0], up[:, 1] - raw[:, 1] * m[g]], axis=1)
        hidden[PADDED[g] * block : (PADDED[g] + COLUMNS[g]) * block] = value.reshape(
            COLUMNS[g] * block, channels
        ).astype(BF16)
    three[tail:, :] = jnp.zeros((deep - tail, three.shape[1]), BF16)
    for offset in range(3):
        for g in range(3):
            start = (PADDED[g] - (offset - 1)) * block
            three[
                FIRST[g] * block : (FIRST[g] + COLUMNS[g]) * block,
                offset * channels : (offset + 1) * channels,
            ] = hidden[start : start + COLUMNS[g] * block, :]
    advance(2, 0)
    for level in range(3):
        for offset in range(3):
            value = dot(turned[level], three[:, offset * channels : (offset + 1) * channels])
            put_blocks(n, w, gradients[1], value, (3 * level + offset) * channels, shapes[1][0])
        advance(2, level + 1)
    launch(1)
    ins["spatial"].wait()

    def taps(g, level):
        at, count = PADDED[g] * block, COLUMNS[g] * block
        total = None
        for offset in range(3):
            start = at - (offset - 1) * block
            weight = spatial[(3 * level + offset) * channels : (3 * level + offset + 1) * channels, :]
            part = dot_t(hidden[start : start + count, :], weight)
            total = part if total is None else total + part
        return total.reshape(COLUMNS[g], 2, images, channels)

    copies = []
    for g in range(3):
        flag = m[g] > 0.5
        blocks = slice(FIRST[g], FIRST[g] + COLUMNS[g])
        rows = padded_rows(COLUMNS[g] * images)
        upper = taps(g, 0)
        lower = taps(g, 2)
        to_before[starts[g] : starts[g] + rows] = pack_halo(upper[:, 0])
        to_after[starts[g] : starts[g] + rows] = pack_halo(
            lower[:, 1] + jnp.where(flag, 0.0, lower[:, 0])
        )
        copies.append(
            halo_copies(
                n, g, rows, starts, to_after, from_before, to_before, from_after, halo_sems
            )
        )
        halo_start(n, copies[g])
        u[blocks] = jnp.stack([upper[:, 1], jnp.where(flag, lower[:, 0], 0.0)], axis=1)
    advance(1, 0)
    ins["one"].wait()

    a, b, scale, mean = forward_scale(stat_one[...], norm_params(gain_ref, bias_ref, 0, channels), number)
    sums = jnp.zeros((1, channels), F32)
    gains = jnp.zeros((1, channels), F32)
    for g in range(3):
        flag = m[g] > 0.5
        blocks = slice(FIRST[g], FIRST[g] + COLUMNS[g])
        middle = taps(g, 1)
        rows = padded_rows(COLUMNS[g] * images)
        halo_arrived(n, copies[g])
        before = unpack_halo(from_before[starts[g] : starts[g] + rows], COLUMNS[g], images)
        after = unpack_halo(from_after[starts[g] : starts[g] + rows], COLUMNS[g], images)
        first = u[blocks][:, 0] + middle[:, 0] + before + jnp.where(flag, 0.0, after)
        second = u[blocks][:, 1] + middle[:, 1] + jnp.where(flag, after, 0.0)
        raw = one[blocks]
        v = raw * a + b
        slope = slope_of(v, *half_of(v))
        value = jnp.stack([slope[:, 0] * first, slope[:, 1] * second * m[g]], axis=1)
        u[blocks] = value
        sums = sums + jnp.sum(value, axis=(0, 1, 2))[None]
        gains = gains + jnp.sum(value * ((raw - mean) * scale), axis=(0, 1, 2))[None]
    sum_one.begin(jnp.concatenate([gains, sums], axis=0))
    get("reduce", reduce_ref, spatial.at[: reduce_ref.shape[0]])
    order[...] = from_rows(wide.shape[1] // 128)
    hidden[tail:deep] = jnp.zeros((deep - tail, channels), BF16)
    sum_one.middle()
    for g in range(3):
        halo_sent(n, copies[g])
    grads = sum_one.end()
    norm_one[...] = grads
    a, b, c = norm_scale(0, stat_one, grads)
    for g in range(3):
        blocks = slice(FIRST[g], FIRST[g] + COLUMNS[g])
        up = u[blocks] * a
        raw = one[blocks] * b + c
        value = jnp.stack([up[:, 0] - raw[:, 0], up[:, 1] - raw[:, 1] * m[g]], axis=1)
        hidden[FIRST[g] * block : (FIRST[g] + COLUMNS[g]) * block] = value.reshape(
            COLUMNS[g] * block, channels
        ).astype(BF16)
    turn(hidden, slice(0, channels), turned.at[0])
    ins["rows"].wait()
    advance(1, 1, 0)
    per = 256 // (shapes[0][0] // w)

    def weight_step(k, _):
        at = pl.ds(pl.multiple_of(k * 256, 256), 256)
        value = dot(turned[0], wide[:, at]).T
        put_blocks(n, w, gradients[0], value, 0, shapes[0][0], place_w=k * per)
        return 0

    lax.fori_loop(0, shapes[0][0] // 256, weight_step, 0)
    launch(0)
    get("again", grad_ref, wide.at[:tail])
    advance(1, 1, 1)
    advance(1, 2, 0)
    ins["reduce"].wait()
    ins["again"].wait()

    def input_step(k, _):
        at = pl.ds(pl.multiple_of(k * 256, 256), 256)
        for g in range(3):
            rows = slice(FIRST[g] * block, (FIRST[g] + COLUMNS[g]) * block)
            value = dot_t(hidden[rows, :], spatial[at, :]) + wide[rows, at].astype(F32)
            three[rows, at] = value.astype(BF16)
        return 0

    lanes = wide.shape[1] // 128

    def out_copy(t):
        g, j = place_of(t)
        slot = lax.rem(t, 2)
        return pltpu.make_async_copy(ring.at[slot], input_ref.at[g, :, j], ring_sems.at[slot])

    def out_step(t, _):
        slot = lax.rem(t, 2)

        @pl.when(t >= 2)
        def _():
            out_copy(t - 2).wait()

        pieces = [[] for _ in range(images // 8)]
        row = pl.multiple_of(t * block, block)
        for c in range(lanes):
            value = three[pl.ds(row, block), c * 128 : (c + 1) * 128].astype(F32)
            for slots in range(2):
                for k in range(images // 8):
                    at = slots * images + 8 * k
                    pieces[k].append(value[at : at + 8])
        pieces = [jnp.concatenate(p, axis=0).astype(BF16) for p in pieces]
        for k in range(0, len(pieces), 2):
            value = dot(order[...], jnp.concatenate(pieces[k : k + 2], axis=1)).astype(BF16)
            for j in range(len(pieces[k : k + 2])):
                ring[slot, 8 * (k + j) : 8 * (k + j + 1)] = value[
                    :, 128 * j : 128 * (j + 1)
                ].reshape(8, 2 * lanes, 128)
        out_copy(t).start()
        return 0

    chunks = wide.shape[1] // 256
    lax.fori_loop(0, chunks // 4, input_step, 0)
    advance(0, 0)
    lax.fori_loop(chunks // 4, chunks, input_step, 0)
    advance(1, 2, 1)
    advance(0, 1)
    lax.fori_loop(0, BLOCKS // 2, out_step, 0)
    advance(1, 3, 0)
    advance(0, 2)
    lax.fori_loop(BLOCKS // 2, BLOCKS, out_step, 0)
    for t in (BLOCKS - 2, BLOCKS - 1):
        out_copy(jnp.int32(t)).wait()
    ring[0] = jnp.zeros(ring.shape[1:], BF16)
    empty = []
    for g in range(3):
        for j in range(COLUMNS[g], input_ref.shape[2]):
            empty.append(
                pltpu.make_async_copy(
                    ring.at[0], input_ref.at[g, :, j], in_sems.at[len(ins) + len(empty)]
                )
            )
            empty[-1].start()
    columns, totals = [None] * 3, [None] * 3

    def column_sums(which):
        for copy in sent[which]:
            copy.wait_recv()
        old = (reduce_rows_ref, spatial_rows_ref, expand_rows_ref)[which]
        by_column, total = [], None
        for k in range(n):
            value = shares[which][k].astype(F32)
            square = value * value + EPS_ONE
            by_column.append(jnp.sum(square, axis=0, keepdims=True))
            part = jnp.sum(by_column[-1], axis=1, keepdims=True)
            total = part if total is None else total + part
        columns[which] = jnp.concatenate(by_column, axis=1)
        total = BETA * jnp.sum(old[...].reshape(1, -1), axis=1, keepdims=True) + (
            1.0 - BETA
        ) / shapes[which][1] * total
        totals[which] = jnp.broadcast_to(total, (1, 128))

    column_sums(2)
    advance(1, 3, 1)
    advance(0, 3)
    column_sums(1)
    column_sums(0)
    columns_ref[...] = sum_over(
        "wide", w, jnp.concatenate(columns + totals, axis=1), *column_scratch
    )
    for which in range(3):
        for scatter in scatters[which]:
            scatter.done()
        for copy in sent[which]:
            copy.wait_send()
    for copy in empty:
        copy.wait()


def final_kernel(
    w, input_ref, sums_ref, reduce_share, spatial_share, expand_share,
    reduce_ref, spatial_ref, expand_ref, square_reduce, square_spatial, square_expand,
    reduce_rows, spatial_rows, expand_rows, reduce_cols, spatial_cols, expand_cols,
    one_ref, two_ref, three_ref, gain_ref, bias_ref, state_ref,
    out_ref, reduce_grad, spatial_grad, expand_grad, reduce_rows_next, reduce_cols_next, spatial_rows_next,
    spatial_cols_next, expand_rows_next, expand_cols_next, reduce_next, spatial_next, expand_next,
    norm_grads, norm_second, norm_next,
    held, reduce_own, spatial_own, expand_own, sems,
):
    me = lax.axis_index("wide")
    own_copies = []
    for k, (source, own) in enumerate(
        ((reduce_ref, reduce_own), (spatial_ref, spatial_own), (expand_ref, expand_own))
    ):
        size = own.shape[0]
        own_copies.append(
            pltpu.make_async_copy(source.at[pl.ds(me * size, size)], own, sems.at[k])
        )
        own_copies[-1].start()
    through = []
    images = input_ref.shape[1] // 4
    for g in range(3):
        for k in range(4):
            at, sem = (g, slice(k * images, (k + 1) * images)), sems.at[3 + len(through)]
            through.append(
                (
                    pltpu.make_async_copy(input_ref.at[at], held.at[at], sem),
                    pltpu.make_async_copy(held.at[at], out_ref.at[at], sem),
                )
            )
            through[-1][0].start()
    grads = jnp.concatenate([one_ref[...], two_ref[...], three_ref[...]], axis=1)
    norm_grads[...] = grads
    params = jnp.concatenate([gain_ref[...], bias_ref[...]], axis=0)
    second = BETA * state_ref[...] + (1.0 - BETA) * (grads * grads + EPS_ONE)
    norm_second[...] = second
    rate = 0.5 * jnp.maximum(
        jnp.sqrt(jnp.sum(params * params, axis=1, keepdims=True) / params.shape[1]), 0.001
    )
    norm_next[...] = params - rate * grads * lax.rsqrt(second)
    for into, out in through:
        into.wait()
        out.start()
    lane = 0
    weights = (
        (reduce_share, reduce_own, square_reduce, reduce_rows, reduce_cols, reduce_grad,
         reduce_rows_next, reduce_cols_next, reduce_next, reduce_ref),
        (spatial_share, spatial_own, square_spatial, spatial_rows, spatial_cols, spatial_grad,
         spatial_rows_next, spatial_cols_next, spatial_next, spatial_ref),
        (expand_share, expand_own, square_expand, expand_rows, expand_cols, expand_grad,
         expand_rows_next, expand_cols_next, expand_next, expand_ref),
    )
    at = 0
    for share, *_ in weights:
        at += share.shape[0] * share.shape[2]
    for which, (
        share, own, square, old_rows, old_cols, grad, next_rows, next_cols, next_w, full
    ) in enumerate(weights):
        n, height, width = share.shape
        all_rows = full.shape[0]
        rate = 0.5 * jnp.maximum(
            jnp.sqrt(
                jnp.sum(square[...], axis=1, keepdims=True) / (full.shape[0] * full.shape[1])
            ),
            0.001,
        )
        row_mean = sums_ref[0:1, at + 128 * which : at + 128 * which + 1] / all_rows
        total = jnp.zeros((height, 1), F32)
        for k in range(n):
            value = share[k].astype(F32)
            grad[:, k * width : (k + 1) * width] = value
            total = total + jnp.sum(value * value + EPS_ONE, axis=1, keepdims=True)
        old = jnp.broadcast_to(old_rows[...].reshape(1, height), (128, height)).T
        by_row = BETA * old + (1.0 - BETA) / (n * width) * total
        next_rows[...] = by_row.T[0:1].reshape(next_rows.shape)
        by_column = BETA * old_cols[...] + (1.0 - BETA) / all_rows * sums_ref[
            0:1, lane : lane + n * width
        ]
        next_cols[...] = by_column
        lane += n * width
        second = by_row[:, 0:1] * (by_column / row_mean)
        own_copies[which].wait()
        next_w[...] = own[...] - rate * grad[...] * lax.rsqrt(second)
    for _, out in through:
        out.wait()


def pixels_first(x):
    g, i, s, c, k = x.shape
    x = jnp.transpose(x, (0, 1, 3, 2, 4)).reshape(g, i, c, s, k // 128, 128)
    return jnp.transpose(x, (0, 1, 2, 4, 3, 5)).reshape(g, i, c, s * k // 128, 128)


def slots_first(x, slots):
    g, i, c, r, k = x.shape
    x = x.reshape(g, i, c, r // slots, slots, k)
    x = jnp.transpose(x, (0, 1, 2, 4, 3, 5)).reshape(g, i, c, slots, r // slots * k)
    return jnp.transpose(x, (0, 1, 3, 2, 4))


def call(kernel, outs, ins, scratch, collective_id=None, **more):
    params = dict(vmem_limit_bytes=LIMIT)
    if collective_id is not None:
        params.update(collective_id=collective_id, has_side_effects=True)
    smem = [x.ndim == 1 for x in ins]
    specs = dict(
        in_specs=[pl.BlockSpec(memory_space=pltpu.SMEM if s else VMEM) for s in smem],
        out_specs=tuple(pl.BlockSpec(memory_space=VMEM) for _ in outs),
    )
    specs.update(more)
    return pl.pallas_call(
        kernel,
        out_shape=tuple(jax.ShapeDtypeStruct(shape, dtype) for shape, dtype in outs),
        scratch_shapes=scratch,
        compiler_params=pltpu.CompilerParams(**params),
        **specs,
    )(*ins)


def shards(
    n, w, images, upstream, row_counts, w_reduce, w_spatial, w_expand, norm_gain, norm_bias,
    reduce_rows, reduce_cols, spatial_rows, spatial_cols, expand_rows, expand_cols, norm_state,
):
    groups, count, slots, across, outer = images.shape
    inner = w_reduce.shape[1]
    block = slots * count
    tail = BLOCKS * block
    deep = -(-tail // 256) * 256
    number = float(w * count * sum(c * c for c in COLUMNS))
    counts = row_counts.reshape(groups)
    x = pixels_first(images)
    up = pixels_first(upstream)
    params = (norm_gain.reshape(1, -1), norm_bias.reshape(1, -1))
    whole = (BLOCKS, slots, count, inner)
    narrow_sums = reduce_scratch(n, w, 2, inner)
    outer_sums = reduce_scratch(n, w, 2, outer)
    _, halo = halo_rows(count)
    halo_scratch = [VMEM((halo, inner), BF16)] * 4 + [pltpu.SemaphoreType.DMA((4, 3))]
    stage = VMEM((count // 8, slots * outer // 16, 128), F32)
    order = (slots * outer // 16, slots * outer // 16)

    weights = (w_reduce, w_spatial, w_expand)
    full = pl.BlockSpec(memory_space=VMEM)
    smem = pl.BlockSpec(memory_space=pltpu.SMEM)
    far = pl.BlockSpec(memory_space=pl.ANY)
    dma = pltpu.SemaphoreType.DMA
    padded = ((PADDED_BLOCKS * block, inner), BF16)
    compact = ((deep, inner), BF16)
    forward_arrays = [
        ((deep, outer), BF16), (whole, F32), (whole, F32), compact, compact, compact, compact,
        ((tail, outer), BF16), *[(v.shape, BF16) for v in weights],
    ]
    (
        rows, conv_one, conv_two, upper, middle, lower, hidden_two, conv_three, *rounded,
        stats_one, stats_two, stats_three, square_one, square_two, square_three,
    ) = call(
        functools.partial(forward_kernel, n, w, number),
        forward_arrays
        + [((2, v), F32) for v in (inner, inner, outer)]
        + [((1, v), F32) for v in (inner, inner, outer)],
        (x, *weights, *params, counts),
        [
            VMEM((RING, *x.shape[1:2], *x.shape[3:]), BF16),
            VMEM((deep, outer), BF16),
            VMEM((4, CHUNK, inner), F32),
            VMEM(w_expand.shape, F32),
            *[VMEM(v.shape, BF16) for v in weights],
            VMEM(whole, F32),
            VMEM(whole, F32),
            *[VMEM(*padded)] * 3,
            VMEM((tail, inner), BF16),
            VMEM((tail, outer), BF16),
            stage,
            stage,
            VMEM(order, BF16),
            *halo_scratch,
            dma((RING,)),
            dma((4,)),
            dma,
            dma((32,)),
        ]
        + narrow_sums
        + narrow_sums
        + outer_sums,
        0,
        in_specs=[far] * 4 + [full, full, smem],
        out_specs=(far,) * 11 + (full,) * 6,
    )
    row_ring = VMEM((DEPTH, block, outer), BF16)
    map_ring = VMEM((DEPTH, *x.shape[1:2], *x.shape[3:]), BF16)
    output, grad_summed, sums_three = call(
        functools.partial(top_kernel, number, inner),
        [(x.shape, BF16), ((tail, outer), BF16), ((2, 8, outer), F32)],
        (conv_three, rows, up, stats_three, *params, counts),
        [
            row_ring,
            row_ring,
            map_ring,
            map_ring,
            row_ring,
            *[stage] * 4,
            VMEM((2, *order), BF16),
            VMEM((2, outer), F32),
            dma((6, DEPTH)),
        ],
        in_specs=[far] * 3 + [full] * 3 + [smem],
        out_specs=(far, far, full),
    )
    blocks = [block_shapes(n, w, *weight.shape) for weight in weights]
    rows_old = [reduce_rows, spatial_rows, expand_rows]
    cols_old = [v.reshape(1, -1) for v in (reduce_cols, spatial_cols, expand_cols)]
    lanes = sum(v.shape[1] for v in weights) + 3 * 128
    scatter = []
    for weight in weights:
        scatter += scatter_scratch(n, w, *weight.shape)
    input_grad, sums, *more = call(
        functools.partial(backward_kernel, n, w, number, [v.shape for v in weights]),
        [(x.shape, BF16), ((1, lanes), F32)]
        + [((n, v.shape[0] // w, v.shape[1] // n), BF16) for v in weights]
        + [((2, v), F32) for v in (inner, inner, outer)],
        (
            conv_three, grad_summed, hidden_two, rounded[2], conv_two, rounded[1],
            upper, middle, lower, conv_one, rows, rounded[0], sums_three,
            stats_one, stats_two, stats_three, *params, counts, *rows_old,
        ),
        [
            VMEM((deep, outer), BF16),
            VMEM((deep, outer), BF16),
            VMEM(*padded),
            VMEM((3, inner, deep), BF16),
            VMEM(w_expand.shape, BF16),
            VMEM(w_spatial.shape, BF16),
            VMEM(whole, F32),
            VMEM(whole, F32),
            VMEM(whole, F32),
            VMEM((4, outer), F32),
            VMEM((deep, 256), BF16),
            VMEM((deep, 256), BF16),
            VMEM((2, *x.shape[1:2], *x.shape[3:]), BF16),
            VMEM(order, BF16),
            dma((2,)),
            *halo_scratch,
            dma((24,)),
            *[VMEM(shape, BF16) for which in range(3) for shape in blocks[which]],
        ]
        + scatter
        + [dma((n,))] * 6
        + outer_sums
        + narrow_sums
        + narrow_sums
        + [VMEM((w, 1, lanes), F32), dma((w,)), dma((w,))],
        1,
        in_specs=[far] * 12 + [full] * 6 + [smem] + [full] * 3,
        out_specs=(far,) + (full,) * 7,
    )
    shares, (grads_one, grads_two, grads_three) = more[:3], more[3:]
    heights = [v.shape[0] // w for v in weights]
    slabs = [((h, v.shape[1]), F32) for h, v in zip(heights, weights)]
    vectors = []
    for h, v in zip(heights, weights):
        vectors += [((h,), F32), ((1, v.shape[1]), F32)]
    outs = call(
        functools.partial(final_kernel, w),
        [(x.shape, BF16)] + slabs + vectors + slabs + [(norm_state.shape, F32)] * 3,
        (
            input_grad, sums, *shares, *weights, square_one, square_two, square_three,
            *rows_old, *cols_old, grads_one, grads_two, grads_three, *params, norm_state,
        ),
        [VMEM(x.shape, BF16), *[VMEM(shape, dtype) for shape, dtype in slabs], dma((16,))],
        in_specs=[far] + [full] * 4 + [far] * 3 + [full] * 15,
        out_specs=(far,) + (full,) * 15,
    )
    input_grad, *outs = outs
    for k in range(3, 9):
        outs[k] = outs[k].reshape(-1)
    return (slots_first(output, slots), slots_first(input_grad, slots), *outs)


def solution(mesh):
    maps = P(None, "wide", "narrow", None, None)
    in_specs = (
        maps, maps, P(None, "wide", "narrow"), P(), P(), P(), P(), P(),
        P("wide"), P(), P("wide"), P(), P("wide"), P(), P(),
    )
    out_specs = (
        maps, maps, P("wide", None), P("wide", None), P("wide", None),
        P("wide"), P(), P("wide"), P(), P("wide"), P(),
        P("wide", None), P("wide", None), P("wide", None), P(), P(), P(),
    )
    return jax.shard_map(
        functools.partial(shards, mesh.shape["narrow"], mesh.shape["wide"]),
        mesh=mesh,
        in_specs=in_specs,
        out_specs=out_specs,
        check_vma=False,
    )
```

```python
import functools

import jax
import jax.numpy as jnp
from jax import lax
from jax.experimental import pallas as pl
from jax.experimental.pallas import tpu as pltpu
from jax.sharding import PartitionSpec as P

MESH = pl.DeviceIdType.MESH
VMEM = pltpu.VMEM
F32 = jnp.float32
BF16 = jnp.bfloat16

STEP = 10
EPS = 1e-05
EPS_ONE = 1e-30
LIMIT = 63 * 1024 * 1024

COLUMNS = (5, 6, 7)
FIRST = (0, 5, 11)
PADDED = (1, 7, 14)
BLOCKS = 18
PADDED_BLOCKS = 22

C0 = 0.7978845608
C1 = C0 * 0.044715


def half_of(v):
    squared = v * v
    return 0.5 + 0.5 * jnp.tanh(v * (C0 + C1 * squared)), squared


def slope_of(v, h, squared):
    return h + v * h * (1.0 - h) * (2.0 * C0 + 6.0 * C1 * squared)


def dot(a, b):
    return jnp.dot(a, b, preferred_element_type=F32)


def dot_t(a, b):
    return lax.dot_general(a, b, (((1,), (1,)), ((), ())), preferred_element_type=F32)


def to_rows(lanes):
    size = 16 * lanes
    to = lax.broadcasted_iota(jnp.int32, (size, size), 0)
    at = lax.broadcasted_iota(jnp.int32, (size, size), 1)
    return (at == lax.rem(to, 8) * (2 * lanes) + to // 8).astype(F32).astype(BF16)


def from_rows(lanes):
    size = 16 * lanes
    to = lax.broadcasted_iota(jnp.int32, (size, size), 1)
    at = lax.broadcasted_iota(jnp.int32, (size, size), 0)
    return (at == lax.rem(to, 8) * (2 * lanes) + to // 8).astype(F32).astype(BF16)


def turn_in(order, load, stage):
    count = stage.shape[0]
    for k in range(0, count, 2):
        if k + 1 < count:
            both = dot(order, jnp.concatenate([load(k), load(k + 1)], axis=1))
            stage[k] = both[:, :128]
            stage[k + 1] = both[:, 128:]
        else:
            stage[k] = dot(order, load(k))


def turn_out(order, stage, store):
    count = stage.shape[0]
    for k in range(0, count, 2):
        if k + 1 < count:
            both = jnp.concatenate([stage[k].astype(BF16), stage[k + 1].astype(BF16)], axis=1)
            both = dot(order, both).astype(BF16)
            store(k, both[:, :128])
            store(k + 1, both[:, 128:])
        else:
            store(k, dot(order, stage[k].astype(BF16)).astype(BF16))


def staged(stage, c, slot):
    row = (2 * c + slot) * 8
    return jnp.concatenate([stage[k, row : row + 8, :] for k in range(stage.shape[0])], axis=0)


def put_staged(stage, c, slot, value):
    row = (2 * c + slot) * 8
    for k in range(stage.shape[0]):
        stage[k, row : row + 8, :] = value[8 * k : 8 * k + 8]


def cast_rows(value_ref, wb_ref, row, square):
    step = 64

    def add(k, square):
        value = value_ref[pl.ds(pl.multiple_of(k * step, step), step), :]
        wb_ref[pl.ds(pl.multiple_of(row + k * step, step), step), :] = value.astype(BF16)
        return square + jnp.sum((value * value).reshape(step // 8, 8, value.shape[1]), axis=0)

    return lax.fori_loop(0, value_ref.shape[0] // step, add, square)


def reduce_scratch(n, w, rows, channels):
    return [
        VMEM((n, rows, channels), F32),
        VMEM((w, rows, channels), F32),
        pltpu.SemaphoreType.DMA((n,)),
        pltpu.SemaphoreType.DMA((n,)),
        pltpu.SemaphoreType.DMA((w,)),
        pltpu.SemaphoreType.DMA((w,)),
    ]


def greet(n, w):
    me_n, me_w = lax.axis_index("narrow"), lax.axis_index("wide")
    barrier = pltpu.get_barrier_semaphore()
    for k in range(1, n):
        pl.semaphore_signal(
            barrier, inc=1, device_id={"narrow": lax.rem(me_n + k, n)}, device_id_type=MESH
        )
    for k in range(1, w):
        pl.semaphore_signal(
            barrier, inc=1, device_id={"wide": lax.rem(me_w + k, w)}, device_id_type=MESH
        )


def met(n, w):
    pl.semaphore_wait(pltpu.get_barrier_semaphore(), n + w - 2)


def sum_over(axis, size, value, slots, send, recv):
    me = lax.axis_index(axis)
    slots[me] = value
    copies = []
    for k in range(1, size):
        copy = pltpu.make_async_remote_copy(
            src_ref=slots.at[me],
            dst_ref=slots.at[me],
            send_sem=send.at[k],
            recv_sem=recv.at[k],
            device_id={axis: lax.rem(me + k, size)},
            device_id_type=MESH,
        )
        copy.start()
        copies.append(copy)
    for copy in copies:
        copy.wait_recv()
    total = slots[0]
    for k in range(1, size):
        total = total + slots[k]
    for copy in copies:
        copy.wait_send()
    return total


class SumAll:
    def __init__(self, n, w, scratch):
        self.axes = (("narrow", n, scratch[0], *scratch[2:4]), ("wide", w, scratch[1], *scratch[4:6]))
        self.copies = [[], []]

    def send(self, which, value):
        axis, size, slots, send, recv = self.axes[which]
        me = lax.axis_index(axis)
        slots[me] = value
        for k in range(1, size):
            copy = pltpu.make_async_remote_copy(
                src_ref=slots.at[me],
                dst_ref=slots.at[me],
                send_sem=send.at[k],
                recv_sem=recv.at[k],
                device_id={axis: lax.rem(me + k, size)},
                device_id_type=MESH,
            )
            copy.start()
            self.copies[which].append(copy)

    def total(self, which):
        _, size, slots, _, _ = self.axes[which]
        for copy in self.copies[which]:
            copy.wait_recv()
        total = slots[0]
        for k in range(1, size):
            total = total + slots[k]
        return total

    def begin(self, value):
        self.send(0, value)

    def middle(self):
        self.send(1, self.total(0))

    def end(self):
        total = self.total(1)
        for copies in self.copies:
            for copy in copies:
                copy.wait_send()
        return total


def forward_scale(stats, params, number):
    mean = stats[0:1] / number
    scale = lax.rsqrt(stats[1:2] / number - mean * mean + EPS)
    a = scale * params[0]
    return a, params[1] - mean * a, scale, mean


def backward_scale(stats, params, grads, number):
    mean = stats[0:1] / number
    scale = lax.rsqrt(stats[1:2] / number - mean * mean + EPS)
    a = scale * params[0]
    gain_grad, bias_grad = grads[0:1], grads[1:2]
    over = a / number
    return a, over * scale * gain_grad, over * (bias_grad - mean * scale * gain_grad)


def norm_params(gain_ref, bias_ref, which, inner):
    lane = (0, inner, 2 * inner, gain_ref.shape[1])
    at = slice(lane[which], lane[which + 1])
    return gain_ref[0:1, at], bias_ref[0:1, at]


def second_counts(counts_ref, g):
    return jnp.where(counts_ref[g] == 2, 1.0, 0.0)


def two_sums(first, second, m):
    return jnp.sum(first, axis=(0, 1))[None] + m * jnp.sum(second, axis=(0, 1))[None]


def padded_rows(count):
    return -(-count // 16) * 16


def halo_rows(images):
    starts, at = [], 0
    for g in range(3):
        starts.append(at)
        at += padded_rows(COLUMNS[g] * images)
    return starts, at


def pack_halo(value):
    count = value.shape[0] * value.shape[1]
    value = value.reshape(count, value.shape[2])
    extra = padded_rows(count) - count
    if extra:
        value = jnp.concatenate([value, jnp.zeros((extra, value.shape[1]), F32)], axis=0)
    return value.astype(BF16)


def unpack_halo(value, columns, images):
    return value.astype(F32)[: columns * images].reshape(columns, images, value.shape[1])


def halo_copies(n, g, count, starts, up_src, up_dst, down_src, down_dst, sems):
    me = lax.axis_index("narrow")
    rows = pl.ds(starts[g], count)
    forward = pltpu.make_async_remote_copy(
        src_ref=up_src.at[rows],
        dst_ref=up_dst.at[rows],
        send_sem=sems.at[0, g],
        recv_sem=sems.at[1, g],
        device_id={"narrow": lax.rem(me + 1, n)},
        device_id_type=MESH,
    )
    backward = pltpu.make_async_remote_copy(
        src_ref=down_src.at[rows],
        dst_ref=down_dst.at[rows],
        send_sem=sems.at[2, g],
        recv_sem=sems.at[3, g],
        device_id={"narrow": lax.rem(me + n - 1, n)},
        device_id_type=MESH,
    )
    return forward, backward


def halo_start(n, copies):
    me = lax.axis_index("narrow")

    @pl.when(me < n - 1)
    def _():
        copies[0].start()

    @pl.when(me > 0)
    def _():
        copies[1].start()


def halo_arrived(n, copies):
    me = lax.axis_index("narrow")

    @pl.when(me > 0)
    def _():
        copies[0].wait_recv()

    @pl.when(me < n - 1)
    def _():
        copies[1].wait_recv()


def halo_sent(n, copies):
    me = lax.axis_index("narrow")

    @pl.when(me < n - 1)
    def _():
        copies[0].wait_send()

    @pl.when(me > 0)
    def _():
        copies[1].wait_send()


def halo_edges(n, from_before, from_after):
    me = lax.axis_index("narrow")

    @pl.when(me == 0)
    def _():
        from_before[...] = jnp.zeros(from_before.shape, from_before.dtype)

    @pl.when(me == n - 1)
    def _():
        from_after[...] = jnp.zeros(from_after.shape, from_after.dtype)


RING = 6
CHUNK = 512


def place_of(t):
    g = (t >= FIRST[1]).astype(jnp.int32) + (t >= FIRST[2]).astype(jnp.int32)
    return g, t - jnp.where(g == 0, FIRST[0], jnp.where(g == 1, FIRST[1], FIRST[2]))


def forward_kernel(
    n, w, number, x_ref, reduce_ref, spatial_ref, expand_ref, gain_ref, bias_ref, counts_ref,
    rows_out, one_out, two_out, upper_out, middle_out, lower_out, hidden_out, three_out,
    reduce_out, spatial_out, expand_out,
    stat_one, stat_two, stat_three, square_reduce, square_spatial, square_expand,
    ring, rows, weight, wide_weight, reduce, spatial, expand, one, two, upper, middle, lower, hidden, three,
    stage_one, stage_two, order, last, first, above, below, halo_sems, ring_sems, weight_sems, wide_sem, out_sems,
    *scratch,
):
    m = [second_counts(counts_ref, g) for g in range(3)]
    stages = (stage_one, stage_two)
    sum_one = SumAll(n, w, scratch[:6])
    sum_two = SumAll(n, w, scratch[6:12])
    sum_three = SumAll(n, w, scratch[12:18])
    images = x_ref.shape[1]
    lanes = x_ref.shape[3] // 2
    channels = one.shape[3]
    block = 2 * images
    tail = BLOCKS * block
    starts, _ = halo_rows(images)
    outs = []

    def put(source, target):
        copy = pltpu.make_async_copy(source, target, out_sems.at[len(outs)])
        copy.start()
        outs.append(copy)

    def fetch(t):
        g, j = place_of(t)
        slot = lax.rem(t, RING)
        return pltpu.make_async_copy(x_ref.at[g, :, j], ring.at[slot], ring_sems.at[slot])

    sources = [reduce_ref.at[k : k + CHUNK] for k in range(0, reduce_ref.shape[0], CHUNK)]
    reduce_chunks = len(sources)
    sources += [spatial_ref.at[k : k + CHUNK] for k in range(0, spatial_ref.shape[0], CHUNK)]
    slots = weight.shape[0]

    def weight_copy(k):
        return pltpu.make_async_copy(sources[k], weight.at[k % slots], weight_sems.at[k % slots])

    for t in range(RING):
        fetch(jnp.int32(t)).start()
    for k in range(slots):
        weight_copy(k).start()
    wide_copy = pltpu.make_async_copy(expand_ref, wide_weight, wide_sem)
    wide_copy.start()
    greet(n, w)
    order[...] = to_rows(lanes)
    rows[tail:, :] = jnp.zeros((rows.shape[0] - tail, rows.shape[1]), BF16)
    for ref in (upper, middle, lower):
        for at in (0, PADDED[1] - 1, PADDED[2] - 1, PADDED_BLOCKS - 1):
            ref[at * block : (at + 1) * block] = jnp.zeros((block, channels), BF16)
    halo_edges(n, above, below)

    def cast_chunk(k, wb_ref, row, square):
        weight_copy(k).wait()
        square = cast_rows(weight.at[k % slots], wb_ref, row, square)
        if k + slots < len(sources):
            weight_copy(k + slots).start()
        return square

    def place(i, _):
        for k in range(2):
            fetch(2 * i + k).wait()
        for k, stage in enumerate(stages):
            slot = lax.rem(2 * i + k, RING)
            turn_in(
                order[...],
                lambda j, slot=slot: ring[slot, 8 * j : 8 * j + 8].reshape(16 * lanes, 128),
                stage,
            )
        for k, stage in enumerate(stages):
            row = pl.multiple_of((2 * i + k) * block, block)
            for c in range(lanes):
                rows[pl.ds(row, block), c * 128 : (c + 1) * 128] = jnp.concatenate(
                    [staged(stage, c, 0), staged(stage, c, 1)], axis=0
                ).astype(BF16)

        @pl.when(2 * i + RING < BLOCKS)
        def _():
            for k in range(2):
                fetch(2 * i + k + RING).start()

        return 0

    lax.fori_loop(0, BLOCKS // 2, place, 0)
    put(rows, rows_out)
    square = jnp.zeros((8, channels), F32)
    for k in range(reduce_chunks):
        square = cast_chunk(k, reduce, k * CHUNK, square)
    square_reduce[...] = jnp.sum(square, axis=0, keepdims=True)
    put(reduce, reduce_out)
    sums = jnp.zeros((1, channels), F32)
    squares = jnp.zeros((1, channels), F32)
    for g in range(3):
        at = slice(FIRST[g] * block, (FIRST[g] + COLUMNS[g]) * block)
        c = dot(rows[at, :], reduce[...]).reshape(COLUMNS[g], 2, images, channels)
        one[FIRST[g] : FIRST[g] + COLUMNS[g]] = c
        sums = sums + two_sums(c[:, 0], c[:, 1], m[g])
        squares = squares + two_sums(c[:, 0] * c[:, 0], c[:, 1] * c[:, 1], m[g])
    met(n, w)
    sum_one.begin(jnp.concatenate([sums, squares], axis=0))
    put(one, one_out)
    square = jnp.zeros((8, channels), F32)
    middle_chunk = (reduce_chunks + len(sources)) // 2
    for k in range(reduce_chunks, middle_chunk):
        square = cast_chunk(k, spatial, (k - reduce_chunks) * CHUNK, square)
    sum_one.middle()
    for k in range(middle_chunk, len(sources)):
        square = cast_chunk(k, spatial, (k - reduce_chunks) * CHUNK, square)
    square_spatial[...] = jnp.sum(square, axis=0, keepdims=True)
    put(spatial, spatial_out)
    stats = sum_one.end()
    stat_one[...] = stats

    a, b, _, _ = forward_scale(stats, norm_params(gain_ref, bias_ref, 0, channels), number)
    copies = []
    for g in range(3):
        v = one[FIRST[g] : FIRST[g] + COLUMNS[g]] * a + b
        value = v * half_of(v)[0]
        slot_one, slot_two = value[:, 0], value[:, 1] * m[g]
        count = padded_rows(COLUMNS[g] * images)
        first[starts[g] : starts[g] + count] = pack_halo(slot_one)
        last[starts[g] : starts[g] + count] = pack_halo(
            jnp.where(m[g] > 0.5, slot_two, slot_one)
        )
        copies.append(halo_copies(n, g, count, starts, last, above, first, below, halo_sems))
        halo_start(n, copies[g])
        both = jnp.stack([slot_one, slot_two], axis=1).reshape(COLUMNS[g] * block, channels)
        middle[PADDED[g] * block : (PADDED[g] + COLUMNS[g]) * block] = both.astype(BF16)

    def taps(ref, g, level):
        at, count = PADDED[g] * block, COLUMNS[g] * block
        shifted = [ref[at + d * block : at + d * block + count, :] for d in (-1, 0, 1)]
        return dot(
            jnp.concatenate(shifted, axis=1),
            spatial[3 * level * channels : 3 * (level + 1) * channels, :],
        )

    def put_groups(source, target):
        for g in range(3):
            count = COLUMNS[g] * block
            put(
                source.at[PADDED[g] * block : PADDED[g] * block + count],
                target.at[FIRST[g] * block : FIRST[g] * block + count],
            )

    for g in range(3):
        two[FIRST[g] : FIRST[g] + COLUMNS[g]] = taps(middle, g, 1).reshape(
            COLUMNS[g], 2, images, channels
        )
    put_groups(middle, middle_out)
    sums = jnp.zeros((1, channels), F32)
    squares = jnp.zeros((1, channels), F32)
    for g in range(3):
        halo_arrived(n, copies[g])
        at, count = PADDED[g] * block, COLUMNS[g] * block
        height = padded_rows(COLUMNS[g] * images)
        up = unpack_halo(above[starts[g] : starts[g] + height], COLUMNS[g], images)
        down = unpack_halo(below[starts[g] : starts[g] + height], COLUMNS[g], images)
        own = middle[at : at + count].astype(F32).reshape(COLUMNS[g], 2, images, channels)
        upper[at : at + count] = (
            jnp.stack([up, own[:, 0]], axis=1).reshape(count, channels).astype(BF16)
        )
        lower[at : at + count] = (
            jnp.stack([jnp.where(m[g] > 0.5, own[:, 1], down), down], axis=1)
            .reshape(count, channels)
            .astype(BF16)
        )
        c = taps(upper, g, 0) + taps(lower, g, 2)
        c = c.reshape(COLUMNS[g], 2, images, channels) + two[FIRST[g] : FIRST[g] + COLUMNS[g]]
        two[FIRST[g] : FIRST[g] + COLUMNS[g]] = c
        sums = sums + two_sums(c[:, 0], c[:, 1], m[g])
        squares = squares + two_sums(c[:, 0] * c[:, 0], c[:, 1] * c[:, 1], m[g])
    sum_two.begin(jnp.concatenate([sums, squares], axis=0))
    put(two, two_out)
    put_groups(upper, upper_out)
    put_groups(lower, lower_out)
    wide_copy.wait()
    half = wide_weight.shape[0] // 2
    square = jnp.zeros((8, wide_weight.shape[1]), F32)
    square = cast_rows(wide_weight.at[:half], expand, 0, square)
    sum_two.middle()
    square = cast_rows(wide_weight.at[half:], expand, half, square)
    square_expand[...] = jnp.sum(square, axis=0, keepdims=True)
    put(expand, expand_out)
    for g in range(3):
        halo_sent(n, copies[g])
    stats = sum_two.end()
    stat_two[...] = stats

    a, b, _, _ = forward_scale(stats, norm_params(gain_ref, bias_ref, 1, channels), number)
    for g in range(3):
        v = two[FIRST[g] : FIRST[g] + COLUMNS[g]] * a + b
        value = v * half_of(v)[0]
        both = jnp.stack([value[:, 0], value[:, 1] * m[g]], axis=1)
        hidden[FIRST[g] * block : (FIRST[g] + COLUMNS[g]) * block] = both.reshape(
            COLUMNS[g] * block, channels
        ).astype(BF16)
    put(hidden, hidden_out.at[:tail])
    sums, squares = [], []
    for part in range(three.shape[1] // 512):
        s = jnp.zeros((1, 512), F32)
        q = jnp.zeros((1, 512), F32)
        columns = slice(part * 512, (part + 1) * 512)
        for g in range(3):
            at = slice(FIRST[g] * block, (FIRST[g] + COLUMNS[g]) * block)
            c = dot(hidden[at, :], expand[:, columns])
            three[at, columns] = c.astype(BF16)
            s = s + jnp.sum(c, axis=0, keepdims=True)
            q = q + jnp.sum(c * c, axis=0, keepdims=True)
        put(three.at[:, columns], three_out.at[:, columns])
        sums.append(s)
        squares.append(q)
    sum_three.begin(
        jnp.concatenate(
            [jnp.concatenate(sums, axis=1), jnp.concatenate(squares, axis=1)], axis=0
        )
    )
    sum_three.middle()
    stat_three[...] = sum_three.end()
    for copy in outs:
        copy.wait()


DEPTH = 4


def top_kernel(
    number, inner, conv_ref, rows_ref, up_ref, stats_ref, gain_ref, bias_ref, counts_ref,
    out_ref, grad_ref, total,
    conv_ring, rows_ring, up_ring, out_ring, grad_ring, up_one, up_two, out_one, out_two, order, coefficients, sems,
):
    images = up_ref.shape[1]
    lanes = up_ref.shape[3] // 2
    block = 2 * images

    def rows_of(t):
        return pl.ds(pl.multiple_of(t * block, block), block)

    def copy(which, t):
        slot = lax.rem(t, DEPTH)
        g, j = place_of(t)
        source, target = (
            lambda: (conv_ref.at[rows_of(t)], conv_ring.at[slot]),
            lambda: (rows_ref.at[rows_of(t)], rows_ring.at[slot]),
            lambda: (up_ref.at[g, :, j], up_ring.at[slot]),
            lambda: (out_ring.at[slot], out_ref.at[g, :, j]),
            lambda: (grad_ring.at[slot], grad_ref.at[rows_of(t)]),
        )[which]()
        return pltpu.make_async_copy(source, target, sems.at[which, slot])

    def each(which, t, do):
        @pl.when((t >= 0) & (t < BLOCKS))
        def _():
            do(copy(which, t))

    def start(which, t):
        each(which, t, lambda c: c.start())

    def wait(which, t):
        each(which, t, lambda c: c.wait())

    for t in range(3):
        start(2, jnp.int32(t))
        if t < 2:
            start(0, jnp.int32(t))
            start(1, jnp.int32(t))
    total[...] = jnp.zeros(total.shape, F32)
    params = norm_params(gain_ref, bias_ref, 2, inner)
    a, b, scale, mean = forward_scale(stats_ref[...], params, number)
    coefficients[0:1] = a
    coefficients[1:2] = b
    order[0] = to_rows(lanes)
    order[1] = from_rows(lanes)
    out_two[...] = jnp.zeros(out_two.shape, F32)

    def enter(t, stage):
        slot = lax.rem(t, DEPTH)
        turn_in(
            order[0], lambda k: up_ring[slot, 8 * k : 8 * k + 8].reshape(16 * lanes, 128), stage
        )

    def leave(t, stage):
        slot = lax.rem(t + DEPTH, DEPTH)

        def store(k, value):
            out_ring[slot, 8 * k : 8 * k + 8] = value.reshape(8, 2 * lanes, 128)

        turn_out(order[1], stage, store)

    def work(t, stage_up, stage_out):
        slot = lax.rem(t, DEPTH)
        m = second_counts(counts_ref, place_of(t)[0])
        for c in range(lanes):
            at = slice(c * 128, (c + 1) * 128)
            raw = conv_ring[slot, :, at].astype(F32)
            v = raw * coefficients[0:1, at] + coefficients[1:2, at]
            v = v + rows_ring[slot, :, at].astype(F32)
            h, squared = half_of(v)
            out = v * h
            slope = h + out * (1.0 - h) * (2.0 * C0 + 6.0 * C1 * squared)
            put_staged(stage_out, c, 0, out[:images])
            put_staged(stage_out, c, 1, out[images:] * m)
            grad = jnp.concatenate(
                [
                    slope[:images] * staged(stage_up, c, 0),
                    slope[images:] * (staged(stage_up, c, 1) * m),
                ],
                axis=0,
            )
            grad_ring[slot, :, at] = grad.astype(BF16)
            total[0, :, at] += jnp.sum((grad * raw).reshape(block // 8, 8, 128), axis=0)
            total[1, :, at] += jnp.sum(grad.reshape(block // 8, 8, 128), axis=0)

    wait(2, jnp.int32(0))
    enter(jnp.int32(0), up_one)

    def pair(i, _):
        t = 2 * i
        for k in (2, 3):
            start(0, t + k)
            start(1, t + k)
            start(2, t + k + 1)
        for k in (0, 1):
            wait(0, t + k)
            wait(1, t + k)
            wait(2, t + k + 1)
            wait(3, t + k - 1 - DEPTH)
            wait(4, t + k - DEPTH)
        enter(t + 1, up_two)
        work(t, up_one, out_one)
        leave(t - 1, out_two)
        enter(t + 2, up_one)
        work(t + 1, up_two, out_two)
        leave(t, out_one)
        for k in (0, 1):
            start(3, t + k - 1)
            start(4, t + k)
        return 0

    lax.fori_loop(0, BLOCKS // 2, pair, 0)
    last = jnp.int32(BLOCKS - 1)
    wait(3, last - DEPTH)
    leave(last, out_two)
    start(3, last)
    for k in range(DEPTH):
        wait(3, last - k)
        wait(4, last - k)
    out_ring[0] = jnp.zeros(out_ring.shape[1:], BF16)
    copies = []
    for g in range(3):
        for j in range(COLUMNS[g], out_ref.shape[2]):
            copies.append(
                pltpu.make_async_copy(
                    out_ring.at[0], out_ref.at[g, :, j], sems.at[5, len(copies)]
                )
            )
            copies[-1].start()
    value = jnp.sum(total[...], axis=1)
    gains = scale * (value[0:1] - mean * value[1:2])
    total[0] = jnp.concatenate([gains, jnp.zeros((7, gains.shape[1]), F32)], axis=0)
    for copy in copies:
        copy.wait()


def unravel(index, sizes):
    digits = []
    for size in reversed(sizes):
        digits.append(index % size if isinstance(index, int) else lax.rem(index, size))
        index = index // size if isinstance(index, int) else lax.div(index, size)
    return digits[::-1]


def mesh_digits(n, w):
    if (n, w) == (4, 8):
        return (
            [("narrow", 2, 2), ("narrow", 1, 2), ("wide", 2, 4), ("wide", 1, 2)],
            [(1, 3, 0, 2), (1, 0, 3, 2)],
        )
    return [("narrow", 1, n), ("wide", 1, w)], [(0, 1), (0, 1)]


def digit_sizes(n, w):
    return [d[2] for d in mesh_digits(n, w)[0]]


def narrow_digits(n, w):
    return [d[2] for d in mesh_digits(n, w)[0] if d[0] == "narrow"]


def wide_digits(n, w):
    return [d[2] for d in mesh_digits(n, w)[0] if d[0] == "wide"]


def weight_parts(w, rows):
    share = rows // w
    if rows >= 4096 and share % 64 == 0:
        return 4
    return 2 if share % 32 == 0 else 1


def block_shapes(n, w, rows, columns):
    parts = weight_parts(w, rows)
    return [(*digit_sizes(n, w), rows // w // parts, columns // n)] * parts


def put_blocks(n, w, refs, value, row, rows, place_n=None, place_w=0, lane=0):
    share = rows // w
    part = share // len(refs)
    at, end = row, row + value.shape[0]
    columns = refs[0].shape[-1]
    while at < end:
        stop = min(end, (at // part + 1) * part)
        wide = at // share
        ref = refs[at // part % len(refs)]
        inside = slice(at % part, at % part + stop - at)
        piece = value[at - row : stop - row]
        wide = unravel(place_w + wide, wide_digits(n, w))
        if place_n is not None:
            lanes = slice(lane, lane + piece.shape[1])
            ref[(*unravel(place_n, narrow_digits(n, w)), *wide, inside, lanes)] = piece.astype(BF16)
        else:
            for k in range(n):
                ref[(*unravel(k, narrow_digits(n, w)), *wide, inside, slice(None))] = piece[
                    :, k * columns : (k + 1) * columns
                ].astype(BF16)
        at = stop


def scatter_scratch(n, w, rows, columns):
    digits, orders = mesh_digits(n, w)
    scratch = []
    for part, shape in enumerate(block_shapes(n, w, rows, columns)):
        left = list(range(len(digits)))
        for d in orders[part % 2]:
            left.remove(d)
            size = digits[d][2]
            scratch.append(VMEM((size - 1, *(digits[k][2] for k in left), *shape[-2:]), BF16))
            scratch.append(pltpu.SemaphoreType.DMA((size - 1,)))
            scratch.append(pltpu.SemaphoreType.DMA((size - 1,)))
    return scratch


class Scatter:
    def __init__(self, n, w, source, scratch, order):
        self.digits = mesh_digits(n, w)[0]
        self.order = order
        self.scratch = scratch
        self.sources = [source] + [scratch[3 * k].at[0] for k in range(len(order))]
        self.copies = []
        self.steps = len(order)

    def own(self, d):
        axis, stride, size = self.digits[d]
        return lax.rem(lax.div(lax.axis_index(axis), stride), size)

    def pick(self, ref, step, value):
        left = [d for d in range(len(self.digits)) if d not in self.order[:step]]
        return ref.at[tuple(value if d == self.order[step] else slice(None) for d in left)]

    def start(self, step):
        d = self.order[step]
        axis, stride, size = self.digits[d]
        landing, send, recv = self.scratch[3 * step : 3 * step + 3]
        mine = self.own(d)
        for k in range(1, size):
            other = lax.rem(mine + k, size)
            copy = pltpu.make_async_remote_copy(
                src_ref=self.pick(self.sources[step], step, other),
                dst_ref=landing.at[k - 1],
                send_sem=send.at[k - 1],
                recv_sem=recv.at[k - 1],
                device_id={axis: lax.axis_index(axis) + (other - mine) * stride},
                device_id_type=MESH,
            )
            copy.start()
            self.copies.append((step, copy))

    def finish(self, step):
        for at, copy in self.copies:
            if at == step:
                copy.wait_recv()
        d = self.order[step]
        size = self.digits[d][2]
        landing = self.scratch[3 * step]
        left = [k for k in range(len(self.digits)) if k not in self.order[: step + 1]]
        sizes = [self.digits[k][2] for k in left]
        mine = self.own(d)
        source = self.pick(self.sources[step], step, mine)

        def total(at):
            value = source[at].astype(F32)
            for k in range(size - 1):
                value = value + landing[(k, *at)].astype(F32)
            return value

        if step == self.steps - 1:
            return total((slice(None), slice(None)))
        count = 1
        for k in sizes:
            count *= k

        together = 4 if count % 4 == 0 else 1

        def add(index, _):
            for k in range(together):
                at = tuple(unravel(index * together + k, sizes))
                landing[(0, *at)] = total(at).astype(BF16)
            return 0

        lax.fori_loop(0, count // together, add, 0)

    def done(self):
        for _, copy in self.copies:
            copy.wait_send()


def share_out(n, slots, value, send, recv):
    me = lax.axis_index("narrow")
    row = 0
    for piece in value:
        slots[me, row : row + piece.shape[0]] = piece.astype(BF16)
        row += piece.shape[0]
    copies = []
    for k in range(1, n):
        copy = pltpu.make_async_remote_copy(
            src_ref=slots.at[me],
            dst_ref=slots.at[me],
            send_sem=send.at[k],
            recv_sem=recv.at[k],
            device_id={"narrow": lax.rem(me + k, n)},
            device_id_type=MESH,
        )
        copy.start()
        copies.append(copy)
    return copies


BETA = 1.0 - STEP ** (-0.8)


class Refs:
    def __init__(self, refs):
        self.refs = list(refs)

    def take(self, count):
        taken, self.refs = self.refs[:count], self.refs[count:]
        return taken

    def one(self):
        return self.take(1)[0]


def backward_kernel(
    n, w, number, shapes, three_ref, grad_ref, hidden_ref, expand_ref, two_ref, spatial_ref,
    upper_ref, middle_ref, lower_ref, one_ref, rows_ref, reduce_ref, sums_ref, stat_one, stat_two, stat_three,
    gain_ref, bias_ref, counts_ref, reduce_rows_ref, spatial_rows_ref, expand_rows_ref, *refs,
):
    refs = Refs(refs)
    parts = [weight_parts(w, shape[0]) for shape in shapes]
    input_ref, columns_ref = refs.take(2)
    shares = refs.take(3)
    norm_one, norm_two, norm_three = refs.take(3)
    three, wide, hidden, turned, expand, spatial, reduce, two, one, u, coefficients = refs.take(11)
    to_before, to_after, from_after, from_before, halo_sems, in_sems = refs.take(6)
    gradients = [refs.take(parts[k]) for k in range(3)]
    orders = mesh_digits(n, w)[1]
    steps = len(orders[0])
    scatters = [
        [
            Scatter(n, w, gradients[k][p], refs.take(3 * steps), orders[p % 2])
            for p in range(parts[k])
        ]
        for k in range(3)
    ]
    share_sems = [refs.take(2) for _ in range(3)]
    sum_three = SumAll(n, w, refs.take(6))
    sum_two = SumAll(n, w, refs.take(6))
    sum_one = SumAll(n, w, refs.take(6))
    column_scratch = refs.take(3)

    images = two.shape[2]
    channels = two.shape[3]
    block = 2 * images
    tail = BLOCKS * block
    deep = three.shape[0]
    m = [second_counts(counts_ref, g) for g in range(3)]
    starts, _ = halo_rows(images)

    ins = {}

    def get(name, source, target):
        ins[name] = pltpu.make_async_copy(source, target, in_sems.at[len(ins)])
        ins[name].start()

    get("hidden", hidden_ref.at[:tail], hidden.at[:tail])
    get("three", three_ref, three.at[:tail])
    get("grad", grad_ref, wide.at[:tail])
    get("expand", expand_ref, expand)
    get("two", two_ref, two)
    for tap in range(9):
        get(
            ("spatial", tap),
            spatial_ref.at[tap * channels : (tap + 1) * channels],
            spatial.at[tap // 3, :, tap % 3 * channels : (tap % 3 + 1) * channels],
        )
    get("one", one_ref, one)
    get("reduce", reduce_ref, reduce)
    greet(n, w)

    def norm_scale(which, stat, grads):
        params = norm_params(gain_ref, bias_ref, which, channels)
        return backward_scale(stat[...], params, grads, number)

    def turn(source, columns, target):
        for k in range(deep // 128):
            target[:, k * 128 : (k + 1) * 128] = source[k * 128 : (k + 1) * 128, columns].T

    sent = {}

    def advance(which, step, half=None):
        if step >= steps:
            return
        count = parts[which]
        if half is not None and count == 1:
            if half == 0:
                return
            half = None
        first = 0 if half is None else half * (count // 2)
        last = count if half is None else first + count // 2
        for scatter in scatters[which][first:last]:
            value = scatter.finish(step)
            if step < steps - 1:
                scatter.start(step + 1)
            else:
                sent.setdefault(which, []).append(value)
        if step == steps - 1 and last == count:
            sent[which] = share_out(n, shares[which], sent[which], *share_sems[which])

    def launch(which):
        for scatter in scatters[which]:
            scatter.start(0)

    value = jnp.concatenate(
        [sums_ref[0, 0:1], jnp.sum(sums_ref[1], axis=0, keepdims=True)],
        axis=0,
    )
    halo_edges(n, from_before, from_after)
    wide[tail:, :] = jnp.zeros((deep - tail, wide.shape[1]), BF16)
    hidden[tail:deep] = jnp.zeros((deep - tail, channels), BF16)
    met(n, w)
    sum_three.begin(value)
    ins["hidden"].wait()
    turn(hidden, slice(0, channels), turned.at[0])
    sum_three.middle()
    ins["three"].wait()
    ins["grad"].wait()
    ins["expand"].wait()
    grads = sum_three.end()
    norm_three[...] = grads
    a, b, c = norm_scale(2, stat_three, grads)
    coefficients[0:1] = a
    coefficients[1:2] = b
    coefficients[2:3] = c
    width = 256

    def back_three(k):
        at = slice(k * width, (k + 1) * width)
        a, b, c = coefficients[0:1, at], coefficients[1:2, at], coefficients[2:3, at]
        for g in range(3):
            rows = slice(FIRST[g] * block, (FIRST[g] + COLUMNS[g]) * block)
            up = wide[rows, at].astype(F32) * a
            raw = (three[rows, at].astype(F32) * b + c).reshape(COLUMNS[g], 2, images, width)
            raw = jnp.stack([raw[:, 0], raw[:, 1] * m[g]], axis=1).reshape(up.shape)
            wide[rows, at] = (up - raw).astype(BF16)

    count = expand.shape[1] // width
    per = count // n
    back_three(0)
    for k in range(count):
        if k + 1 < count:
            back_three(k + 1)
        value = dot(turned[0], wide[:, k * width : (k + 1) * width])
        put_blocks(
            n, w, gradients[2], value, 0, channels, place_n=k // per, lane=k % per * width
        )
    launch(2)

    ins["two"].wait()
    a, b, scale, mean = forward_scale(
        stat_two[...], norm_params(gain_ref, bias_ref, 1, channels), number
    )
    sums = jnp.zeros((1, channels), F32)
    gains = jnp.zeros((1, channels), F32)
    for g in range(3):
        blocks = slice(FIRST[g], FIRST[g] + COLUMNS[g])
        raw = two[blocks]
        v = raw * a + b
        rows = slice(FIRST[g] * block, (FIRST[g] + COLUMNS[g]) * block)
        value = slope_of(v, *half_of(v)) * dot_t(wide[rows, :], expand[...]).reshape(raw.shape)
        value = jnp.stack([value[:, 0], value[:, 1] * m[g]], axis=1)
        u[blocks] = value
        sums = sums + jnp.sum(value, axis=(0, 1, 2))[None]
        gains = gains + jnp.sum(value * ((raw - mean) * scale), axis=(0, 1, 2))[None]
    for k, source in enumerate((upper_ref, middle_ref, lower_ref)):
        get(k, source.at[:tail], wide.at[:tail, k * channels : (k + 1) * channels])
    sum_two.begin(jnp.concatenate([gains, sums], axis=0))
    for at in (0, PADDED[1] - 1, PADDED[2] - 1, PADDED_BLOCKS - 1):
        hidden[at * block : (at + 1) * block] = jnp.zeros((block, channels), BF16)
    ins[0].wait()
    turn(wide, slice(0, channels), turned.at[0])
    sum_two.middle()
    for k in (1, 2):
        ins[k].wait()
        turn(wide, slice(k * channels, (k + 1) * channels), turned.at[k])
    get("rows", rows_ref, wide)
    grads = sum_two.end()
    norm_two[...] = grads
    a, b, c = norm_scale(1, stat_two, grads)
    for g in range(3):
        blocks = slice(FIRST[g], FIRST[g] + COLUMNS[g])
        up = u[blocks] * a
        raw = two[blocks] * b + c
        value = jnp.stack([up[:, 0] - raw[:, 0], up[:, 1] - raw[:, 1] * m[g]], axis=1)
        hidden[PADDED[g] * block : (PADDED[g] + COLUMNS[g]) * block] = value.reshape(
            COLUMNS[g] * block, channels
        ).astype(BF16)
    three[tail:, :] = jnp.zeros((deep - tail, three.shape[1]), BF16)
    for offset in range(3):
        for g in range(3):
            start = (PADDED[g] - (offset - 1)) * block
            three[
                FIRST[g] * block : (FIRST[g] + COLUMNS[g]) * block,
                offset * channels : (offset + 1) * channels,
            ] = hidden[start : start + COLUMNS[g] * block, :]
    advance(2, 0)
    for level in range(3):
        for offset in range(3):
            value = dot(turned[level], three[:, offset * channels : (offset + 1) * channels])
            put_blocks(n, w, gradients[1], value, (3 * level + offset) * channels, shapes[1][0])
        if level > 0:
            advance(2, level)
    launch(1)
    for tap in range(9):
        ins["spatial", tap].wait()

    def taps(g, level):
        at, count = PADDED[g] * block, COLUMNS[g] * block
        shifted = [hidden[at - d * block : at - d * block + count, :] for d in (-1, 0, 1)]
        value = dot_t(jnp.concatenate(shifted, axis=1), spatial[level])
        return value.reshape(COLUMNS[g], 2, images, channels)

    copies = []
    for g in range(3):
        flag = m[g] > 0.5
        blocks = slice(FIRST[g], FIRST[g] + COLUMNS[g])
        rows = padded_rows(COLUMNS[g] * images)
        upper = taps(g, 0)
        lower = taps(g, 2)
        to_before[starts[g] : starts[g] + rows] = pack_halo(upper[:, 0])
        to_after[starts[g] : starts[g] + rows] = pack_halo(
            lower[:, 1] + jnp.where(flag, 0.0, lower[:, 0])
        )
        copies.append(
            halo_copies(
                n, g, rows, starts, to_after, from_before, to_before, from_after, halo_sems
            )
        )
        halo_start(n, copies[g])
        u[blocks] = jnp.stack([upper[:, 1], jnp.where(flag, lower[:, 0], 0.0)], axis=1)
    advance(1, 0)
    ins["one"].wait()

    a, b, scale, mean = forward_scale(stat_one[...], norm_params(gain_ref, bias_ref, 0, channels), number)
    sums = jnp.zeros((1, channels), F32)
    gains = jnp.zeros((1, channels), F32)
    for g in range(3):
        flag = m[g] > 0.5
        blocks = slice(FIRST[g], FIRST[g] + COLUMNS[g])
        middle = taps(g, 1)
        rows = padded_rows(COLUMNS[g] * images)
        halo_arrived(n, copies[g])
        before = unpack_halo(from_before[starts[g] : starts[g] + rows], COLUMNS[g], images)
        after = unpack_halo(from_after[starts[g] : starts[g] + rows], COLUMNS[g], images)
        first = u[blocks][:, 0] + middle[:, 0] + before + jnp.where(flag, 0.0, after)
        second = u[blocks][:, 1] + middle[:, 1] + jnp.where(flag, after, 0.0)
        raw = one[blocks]
        v = raw * a + b
        slope = slope_of(v, *half_of(v))
        value = jnp.stack([slope[:, 0] * first, slope[:, 1] * second * m[g]], axis=1)
        u[blocks] = value
        sums = sums + jnp.sum(value, axis=(0, 1, 2))[None]
        gains = gains + jnp.sum(value * ((raw - mean) * scale), axis=(0, 1, 2))[None]
    sum_one.begin(jnp.concatenate([gains, sums], axis=0))
    advance(2, 3)
    hidden[tail:deep] = jnp.zeros((deep - tail, channels), BF16)
    sum_one.middle()
    for g in range(3):
        halo_sent(n, copies[g])
    grads = sum_one.end()
    norm_one[...] = grads
    a, b, c = norm_scale(0, stat_one, grads)
    for g in range(3):
        blocks = slice(FIRST[g], FIRST[g] + COLUMNS[g])
        up = u[blocks] * a
        raw = one[blocks] * b + c
        value = jnp.stack([up[:, 0] - raw[:, 0], up[:, 1] - raw[:, 1] * m[g]], axis=1)
        hidden[FIRST[g] * block : (FIRST[g] + COLUMNS[g]) * block] = value.reshape(
            COLUMNS[g] * block, channels
        ).astype(BF16)
    turn(hidden, slice(0, channels), turned.at[0])
    ins["rows"].wait()
    advance(1, 1, 0)
    per = 256 // (shapes[0][0] // w)

    def weight_step(i, _):
        values = []
        for k in range(2):
            at = pl.ds(pl.multiple_of((2 * i + k) * 256, 256), 256)
            values.append(dot(turned[0], wide[:, at]))
        for k in range(2):
            place_w = (2 * i + k) * per
            put_blocks(n, w, gradients[0], values[k].T, 0, shapes[0][0], place_w=place_w)
        return 0

    lax.fori_loop(0, shapes[0][0] // 512, weight_step, 0)
    launch(0)
    get("again", grad_ref, wide.at[:tail])
    advance(1, 1, 1)
    advance(1, 2, 0)
    ins["reduce"].wait()
    ins["again"].wait()

    def input_step(k, _):
        at = pl.ds(pl.multiple_of(k * 256, 256), 256)
        for g in range(3):
            rows = slice(FIRST[g] * block, (FIRST[g] + COLUMNS[g]) * block)
            value = dot_t(hidden[rows, :], reduce[at, :]) + wide[rows, at].astype(F32)
            three[rows, at] = value.astype(BF16)
        return 0

    chunks = wide.shape[1] // 256
    lax.fori_loop(0, chunks // 4, input_step, 0)
    advance(0, 0)
    lax.fori_loop(chunks // 4, chunks, input_step, 0)
    get("out", three.at[:tail], input_ref)
    advance(1, 2, 1)
    advance(0, 1)
    advance(1, 3, 0)
    advance(0, 2)
    columns, totals = [None] * 3, [None] * 3

    def column_sums(which):
        for copy in sent[which]:
            copy.wait_recv()
        old = (reduce_rows_ref, spatial_rows_ref, expand_rows_ref)[which]
        by_column, total = [], None
        for k in range(n):
            value = shares[which][k].astype(F32)
            square = value * value + EPS_ONE
            by_column.append(jnp.sum(square, axis=0, keepdims=True))
            part = jnp.sum(by_column[-1], axis=1, keepdims=True)
            total = part if total is None else total + part
        columns[which] = jnp.concatenate(by_column, axis=1)
        total = BETA * jnp.sum(old[...].reshape(1, -1), axis=1, keepdims=True) + (
            1.0 - BETA
        ) / shapes[which][1] * total
        totals[which] = jnp.broadcast_to(total, (1, 128))

    column_sums(2)
    advance(1, 3, 1)
    advance(0, 3)
    column_sums(1)
    column_sums(0)
    columns_ref[...] = sum_over(
        "wide", w, jnp.concatenate(columns + totals, axis=1), *column_scratch
    )
    for which in range(3):
        for scatter in scatters[which]:
            scatter.done()
        for copy in sent[which]:
            copy.wait_send()
    ins["out"].wait()


def final_kernel(
    w, input_ref, sums_ref, reduce_share, spatial_share, expand_share,
    reduce_ref, spatial_ref, expand_ref, square_reduce, square_spatial, square_expand,
    reduce_rows, spatial_rows, expand_rows, reduce_cols, spatial_cols, expand_cols,
    one_ref, two_ref, three_ref, gain_ref, bias_ref, state_ref,
    out_ref, reduce_grad, spatial_grad, expand_grad, reduce_rows_next, reduce_cols_next, spatial_rows_next,
    spatial_cols_next, expand_rows_next, expand_cols_next, reduce_next, spatial_next, expand_next,
    norm_grads, norm_second, norm_next,
    row_ring, out_ring, zeros, order, reduce_own, spatial_own, expand_own, sems, ring_sems,
):
    me = lax.axis_index("wide")
    own_copies = []
    for k, (source, own) in enumerate(
        ((reduce_ref, reduce_own), (spatial_ref, spatial_own), (expand_ref, expand_own))
    ):
        size = own.shape[0]
        own_copies.append(
            pltpu.make_async_copy(source.at[pl.ds(me * size, size)], own, sems.at[k])
        )
        own_copies[-1].start()
    images = out_ref.shape[1]
    lanes = out_ref.shape[3] // 2
    block = 2 * images

    def copy(which, t):
        slot = lax.rem(t, DEPTH)
        if which == 0:
            rows = pl.ds(pl.multiple_of(t * block, block), block)
            return pltpu.make_async_copy(input_ref.at[rows], row_ring.at[slot], ring_sems.at[0, slot])
        g, j = place_of(t)
        return pltpu.make_async_copy(out_ring.at[slot], out_ref.at[g, :, j], ring_sems.at[1, slot])

    for t in range(DEPTH):
        copy(0, jnp.int32(t)).start()
    order[...] = from_rows(lanes)
    zeros[...] = jnp.zeros(zeros.shape, BF16)
    empty = []
    for g in range(3):
        for j in range(COLUMNS[g], out_ref.shape[2]):
            empty.append(
                pltpu.make_async_copy(zeros, out_ref.at[g, :, j], sems.at[3 + len(empty)])
            )
            empty[-1].start()

    def pair(i, _):
        for k in range(2):
            copy(0, 2 * i + k).wait()

        @pl.when(2 * i >= DEPTH)
        def _():
            for k in range(2):
                copy(1, 2 * i + k - DEPTH).wait()

        for k in range(2):
            slot = lax.rem(2 * i + k, DEPTH)
            pieces = [[] for _ in range(images // 8)]
            for c in range(lanes):
                value = row_ring[slot, :, c * 128 : (c + 1) * 128].astype(F32)
                for row in range(0, block, 8):
                    pieces[row % images // 8].append(value[row : row + 8])
            pieces = [jnp.concatenate(p, axis=0).astype(BF16) for p in pieces]
            for at in range(0, len(pieces), 2):
                value = dot(order[...], jnp.concatenate(pieces[at : at + 2], axis=1)).astype(BF16)
                for j in range(len(pieces[at : at + 2])):
                    out_ring[slot, 8 * (at + j) : 8 * (at + j + 1)] = value[
                        :, 128 * j : 128 * (j + 1)
                    ].reshape(8, 2 * lanes, 128)
        for k in range(2):
            copy(1, 2 * i + k).start()

        @pl.when(2 * i + DEPTH < BLOCKS)
        def _():
            for k in range(2):
                copy(0, 2 * i + k + DEPTH).start()

        return 0

    lax.fori_loop(0, BLOCKS // 2, pair, 0)
    grads = jnp.concatenate([one_ref[...], two_ref[...], three_ref[...]], axis=1)
    norm_grads[...] = grads
    params = jnp.concatenate([gain_ref[...], bias_ref[...]], axis=0)
    second = BETA * state_ref[...] + (1.0 - BETA) * (grads * grads + EPS_ONE)
    norm_second[...] = second
    rate = 0.5 * jnp.maximum(
        jnp.sqrt(jnp.sum(params * params, axis=1, keepdims=True) / params.shape[1]), 0.001
    )
    norm_next[...] = params - rate * grads * lax.rsqrt(second)
    lane = 0
    weights = (
        (reduce_share, reduce_own, square_reduce, reduce_rows, reduce_cols, reduce_grad,
         reduce_rows_next, reduce_cols_next, reduce_next, reduce_ref),
        (spatial_share, spatial_own, square_spatial, spatial_rows, spatial_cols, spatial_grad,
         spatial_rows_next, spatial_cols_next, spatial_next, spatial_ref),
        (expand_share, expand_own, square_expand, expand_rows, expand_cols, expand_grad,
         expand_rows_next, expand_cols_next, expand_next, expand_ref),
    )
    at = 0
    for share, *_ in weights:
        at += share.shape[0] * share.shape[2]
    for which, (
        share, own, square, old_rows, old_cols, grad, next_rows, next_cols, next_w, full
    ) in enumerate(weights):
        n, height, width = share.shape
        all_rows = full.shape[0]
        rate = 0.5 * jnp.maximum(
            jnp.sqrt(
                jnp.sum(square[...], axis=1, keepdims=True) / (full.shape[0] * full.shape[1])
            ),
            0.001,
        )
        row_mean = sums_ref[0:1, at + 128 * which : at + 128 * which + 1] / all_rows
        total = jnp.zeros((height, 1), F32)
        for k in range(n):
            value = share[k].astype(F32)
            grad[:, k * width : (k + 1) * width] = value
            total = total + jnp.sum(value * value + EPS_ONE, axis=1, keepdims=True)
        old = jnp.broadcast_to(old_rows[...].reshape(1, height), (128, height)).T
        by_row = BETA * old + (1.0 - BETA) / (n * width) * total
        next_rows[...] = by_row.T[0:1].reshape(next_rows.shape)
        by_column = BETA * old_cols[...] + (1.0 - BETA) / all_rows * sums_ref[
            0:1, lane : lane + n * width
        ]
        next_cols[...] = by_column
        lane += n * width
        second = by_row[:, 0:1] * (by_column / row_mean)
        own_copies[which].wait()
        next_w[...] = own[...] - rate * grad[...] * lax.rsqrt(second)
    for t in range(BLOCKS - DEPTH, BLOCKS):
        copy(1, jnp.int32(t)).wait()
    for done in empty:
        done.wait()


def pixels_first(x):
    g, i, s, c, k = x.shape
    x = jnp.transpose(x, (0, 1, 3, 2, 4)).reshape(g, i, c, s, k // 128, 128)
    return jnp.transpose(x, (0, 1, 2, 4, 3, 5)).reshape(g, i, c, s * k // 128, 128)


def slots_first(x, slots):
    g, i, c, r, k = x.shape
    x = x.reshape(g, i, c, r // slots, slots, k)
    x = jnp.transpose(x, (0, 1, 2, 4, 3, 5)).reshape(g, i, c, slots, r // slots * k)
    return jnp.transpose(x, (0, 1, 3, 2, 4))


def call(kernel, outs, ins, scratch, collective_id=None, **more):
    params = dict(vmem_limit_bytes=LIMIT)
    if collective_id is not None:
        params.update(collective_id=collective_id, has_side_effects=True)
    smem = [x.ndim == 1 for x in ins]
    specs = dict(
        in_specs=[pl.BlockSpec(memory_space=pltpu.SMEM if s else VMEM) for s in smem],
        out_specs=tuple(pl.BlockSpec(memory_space=VMEM) for _ in outs),
    )
    specs.update(more)
    return pl.pallas_call(
        kernel,
        out_shape=tuple(jax.ShapeDtypeStruct(shape, dtype) for shape, dtype in outs),
        scratch_shapes=scratch,
        compiler_params=pltpu.CompilerParams(**params),
        **specs,
    )(*ins)


def shards(
    n, w, images, upstream, row_counts, w_reduce, w_spatial, w_expand, norm_gain, norm_bias,
    reduce_rows, reduce_cols, spatial_rows, spatial_cols, expand_rows, expand_cols, norm_state,
):
    groups, count, slots, across, outer = images.shape
    inner = w_reduce.shape[1]
    block = slots * count
    tail = BLOCKS * block
    deep = -(-tail // 256) * 256
    number = float(w * count * sum(c * c for c in COLUMNS))
    counts = row_counts.reshape(groups)
    x = pixels_first(images)
    up = pixels_first(upstream)
    params = (norm_gain.reshape(1, -1), norm_bias.reshape(1, -1))
    whole = (BLOCKS, slots, count, inner)
    narrow_sums = reduce_scratch(n, w, 2, inner)
    outer_sums = reduce_scratch(n, w, 2, outer)
    _, halo = halo_rows(count)
    halo_scratch = [VMEM((halo, inner), BF16)] * 4 + [pltpu.SemaphoreType.DMA((4, 3))]
    stage = VMEM((count // 8, slots * outer // 16, 128), F32)
    order = (slots * outer // 16, slots * outer // 16)

    weights = (w_reduce, w_spatial, w_expand)
    full = pl.BlockSpec(memory_space=VMEM)
    smem = pl.BlockSpec(memory_space=pltpu.SMEM)
    far = pl.BlockSpec(memory_space=pl.ANY)
    dma = pltpu.SemaphoreType.DMA
    padded = ((PADDED_BLOCKS * block, inner), BF16)
    compact = ((deep, inner), BF16)
    forward_arrays = [
        ((deep, outer), BF16), (whole, F32), (whole, F32), compact, compact, compact, compact,
        ((tail, outer), BF16), *[(v.shape, BF16) for v in weights],
    ]
    (
        rows, conv_one, conv_two, upper, middle, lower, hidden_two, conv_three, *rounded,
        stats_one, stats_two, stats_three, square_one, square_two, square_three,
    ) = call(
        functools.partial(forward_kernel, n, w, number),
        forward_arrays
        + [((2, v), F32) for v in (inner, inner, outer)]
        + [((1, v), F32) for v in (inner, inner, outer)],
        (x, *weights, *params, counts),
        [
            VMEM((RING, *x.shape[1:2], *x.shape[3:]), BF16),
            VMEM((deep, outer), BF16),
            VMEM((4, CHUNK, inner), F32),
            VMEM(w_expand.shape, F32),
            *[VMEM(v.shape, BF16) for v in weights],
            VMEM(whole, F32),
            VMEM(whole, F32),
            *[VMEM(*padded)] * 3,
            VMEM((tail, inner), BF16),
            VMEM((tail, outer), BF16),
            stage,
            stage,
            VMEM(order, BF16),
            *halo_scratch,
            dma((RING,)),
            dma((4,)),
            dma,
            dma((32,)),
        ]
        + narrow_sums
        + narrow_sums
        + outer_sums,
        0,
        in_specs=[far] * 4 + [full, full, smem],
        out_specs=(far,) * 11 + (full,) * 6,
    )
    row_ring = VMEM((DEPTH, block, outer), BF16)
    map_ring = VMEM((DEPTH, *x.shape[1:2], *x.shape[3:]), BF16)
    output, grad_summed, sums_three = call(
        functools.partial(top_kernel, number, inner),
        [(x.shape, BF16), ((tail, outer), BF16), ((2, 8, outer), F32)],
        (conv_three, rows, up, stats_three, *params, counts),
        [
            row_ring,
            row_ring,
            map_ring,
            map_ring,
            row_ring,
            *[stage] * 4,
            VMEM((2, *order), BF16),
            VMEM((2, outer), F32),
            dma((6, DEPTH)),
        ],
        in_specs=[far] * 3 + [full] * 3 + [smem],
        out_specs=(far, far, full),
    )
    blocks = [block_shapes(n, w, *weight.shape) for weight in weights]
    rows_old = [reduce_rows, spatial_rows, expand_rows]
    cols_old = [v.reshape(1, -1) for v in (reduce_cols, spatial_cols, expand_cols)]
    lanes = sum(v.shape[1] for v in weights) + 3 * 128
    scatter = []
    for weight in weights:
        scatter += scatter_scratch(n, w, *weight.shape)
    input_grad, sums, *more = call(
        functools.partial(backward_kernel, n, w, number, [v.shape for v in weights]),
        [((tail, outer), BF16), ((1, lanes), F32)]
        + [((n, v.shape[0] // w, v.shape[1] // n), BF16) for v in weights]
        + [((2, v), F32) for v in (inner, inner, outer)],
        (
            conv_three, grad_summed, hidden_two, rounded[2], conv_two, rounded[1],
            upper, middle, lower, conv_one, rows, rounded[0], sums_three,
            stats_one, stats_two, stats_three, *params, counts, *rows_old,
        ),
        [
            VMEM((deep, outer), BF16),
            VMEM((deep, outer), BF16),
            VMEM(*padded),
            VMEM((3, inner, deep), BF16),
            VMEM(w_expand.shape, BF16),
            VMEM((3, inner, 3 * inner), BF16),
            VMEM(w_reduce.shape, BF16),
            VMEM(whole, F32),
            VMEM(whole, F32),
            VMEM(whole, F32),
            VMEM((4, outer), F32),
            *halo_scratch,
            dma((32,)),
            *[VMEM(shape, BF16) for which in range(3) for shape in blocks[which]],
        ]
        + scatter
        + [dma((n,))] * 6
        + outer_sums
        + narrow_sums
        + narrow_sums
        + [VMEM((w, 1, lanes), F32), dma((w,)), dma((w,))],
        1,
        in_specs=[far] * 12 + [full] * 6 + [smem] + [full] * 3,
        out_specs=(far,) + (full,) * 7,
    )
    shares, (grads_one, grads_two, grads_three) = more[:3], more[3:]
    heights = [v.shape[0] // w for v in weights]
    slabs = [((h, v.shape[1]), F32) for h, v in zip(heights, weights)]
    vectors = []
    for h, v in zip(heights, weights):
        vectors += [((h,), F32), ((1, v.shape[1]), F32)]
    outs = call(
        functools.partial(final_kernel, w),
        [(x.shape, BF16)] + slabs + vectors + slabs + [(norm_state.shape, F32)] * 3,
        (
            input_grad, sums, *shares, *weights, square_one, square_two, square_three,
            *rows_old, *cols_old, grads_one, grads_two, grads_three, *params, norm_state,
        ),
        [
            row_ring,
            map_ring,
            VMEM((*x.shape[1:2], *x.shape[3:]), BF16),
            VMEM(order, BF16),
            *[VMEM(shape, dtype) for shape, dtype in slabs],
            dma((16,)),
            dma((2, DEPTH)),
        ],
        in_specs=[far] + [full] * 4 + [far] * 3 + [full] * 15,
        out_specs=(far,) + (full,) * 15,
    )
    input_grad, *outs = outs
    for k in range(3, 9):
        outs[k] = outs[k].reshape(-1)
    return (slots_first(output, slots), slots_first(input_grad, slots), *outs)


def solution(mesh):
    maps = P(None, "wide", "narrow", None, None)
    in_specs = (
        maps, maps, P(None, "wide", "narrow"), P(), P(), P(), P(), P(),
        P("wide"), P(), P("wide"), P(), P("wide"), P(), P(),
    )
    out_specs = (
        maps, maps, P("wide", None), P("wide", None), P("wide", None),
        P("wide"), P(), P("wide"), P(), P("wide"), P(),
        P("wide", None), P("wide", None), P("wide", None), P(), P(), P(),
    )
    return jax.shard_map(
        functools.partial(shards, mesh.shape["narrow"], mesh.shape["wide"]),
        mesh=mesh,
        in_specs=in_specs,
        out_specs=out_specs,
        check_vma=False,
    )
```

```python
import functools

import jax
import jax.numpy as jnp
from jax import lax
from jax.experimental import pallas as pl
from jax.experimental.pallas import tpu as pltpu
from jax.sharding import PartitionSpec as P

MESH = pl.DeviceIdType.MESH
VMEM = pltpu.VMEM
F32 = jnp.float32
BF16 = jnp.bfloat16

STEP = 10
EPS = 1e-05
EPS_ONE = 1e-30
LIMIT = 63 * 1024 * 1024

COLUMNS = (5, 6, 7)
FIRST = (0, 5, 11)
PADDED = (1, 7, 14)
BLOCKS = 18
PADDED_BLOCKS = 22

C0 = 0.7978845608
C1 = C0 * 0.044715


def half_of(v):
    squared = v * v
    return 0.5 + 0.5 * jnp.tanh(v * (C0 + C1 * squared)), squared


def slope_of(v, h, squared):
    return h + v * h * (1.0 - h) * (2.0 * C0 + 6.0 * C1 * squared)


def dot(a, b):
    return jnp.dot(a, b, preferred_element_type=F32)


def dot_t(a, b):
    return lax.dot_general(a, b, (((1,), (1,)), ((), ())), preferred_element_type=F32)


def to_rows(lanes):
    size = 16 * lanes
    to = lax.broadcasted_iota(jnp.int32, (size, size), 0)
    at = lax.broadcasted_iota(jnp.int32, (size, size), 1)
    return (at == lax.rem(to, 8) * (2 * lanes) + to // 8).astype(F32).astype(BF16)


def from_rows(lanes):
    size = 16 * lanes
    to = lax.broadcasted_iota(jnp.int32, (size, size), 1)
    at = lax.broadcasted_iota(jnp.int32, (size, size), 0)
    return (at == lax.rem(to, 8) * (2 * lanes) + to // 8).astype(F32).astype(BF16)


def turn_in(order, load, stage):
    count = stage.shape[0]
    for k in range(0, count, 2):
        if k + 1 < count:
            both = dot(order, jnp.concatenate([load(k), load(k + 1)], axis=1))
            stage[k] = both[:, :128]
            stage[k + 1] = both[:, 128:]
        else:
            stage[k] = dot(order, load(k))


def turn_out(order, stage, store):
    count = stage.shape[0]
    for k in range(0, count, 2):
        if k + 1 < count:
            both = jnp.concatenate([stage[k].astype(BF16), stage[k + 1].astype(BF16)], axis=1)
            both = dot(order, both).astype(BF16)
            store(k, both[:, :128])
            store(k + 1, both[:, 128:])
        else:
            store(k, dot(order, stage[k].astype(BF16)).astype(BF16))


def staged(stage, c, slot):
    row = (2 * c + slot) * 8
    return jnp.concatenate([stage[k, row : row + 8, :] for k in range(stage.shape[0])], axis=0)


def put_staged(stage, c, slot, value):
    row = (2 * c + slot) * 8
    for k in range(stage.shape[0]):
        stage[k, row : row + 8, :] = value[8 * k : 8 * k + 8]


def cast_rows(value_ref, wb_ref, row, square):
    step = 64

    def add(k, square):
        value = value_ref[pl.ds(pl.multiple_of(k * step, step), step), :]
        wb_ref[pl.ds(pl.multiple_of(row + k * step, step), step), :] = value.astype(BF16)
        return square + jnp.sum((value * value).reshape(step // 8, 8, value.shape[1]), axis=0)

    return lax.fori_loop(0, value_ref.shape[0] // step, add, square)


def reduce_scratch(n, w, rows, channels):
    return [
        VMEM((n, rows, channels), F32),
        VMEM((w, rows, channels), F32),
        pltpu.SemaphoreType.DMA((n,)),
        pltpu.SemaphoreType.DMA((n,)),
        pltpu.SemaphoreType.DMA((w,)),
        pltpu.SemaphoreType.DMA((w,)),
    ]


def greet(n, w):
    me_n, me_w = lax.axis_index("narrow"), lax.axis_index("wide")
    barrier = pltpu.get_barrier_semaphore()
    for k in range(1, n):
        pl.semaphore_signal(
            barrier, inc=1, device_id={"narrow": lax.rem(me_n + k, n)}, device_id_type=MESH
        )
    for k in range(1, w):
        pl.semaphore_signal(
            barrier, inc=1, device_id={"wide": lax.rem(me_w + k, w)}, device_id_type=MESH
        )


def met(n, w):
    pl.semaphore_wait(pltpu.get_barrier_semaphore(), n + w - 2)


def sum_over(axis, size, value, slots, send, recv):
    me = lax.axis_index(axis)
    slots[me] = value
    copies = []
    for k in range(1, size):
        copy = pltpu.make_async_remote_copy(
            src_ref=slots.at[me],
            dst_ref=slots.at[me],
            send_sem=send.at[k],
            recv_sem=recv.at[k],
            device_id={axis: lax.rem(me + k, size)},
            device_id_type=MESH,
        )
        copy.start()
        copies.append(copy)
    for copy in copies:
        copy.wait_recv()
    total = slots[0]
    for k in range(1, size):
        total = total + slots[k]
    for copy in copies:
        copy.wait_send()
    return total


class SumAll:
    def __init__(self, n, w, scratch):
        self.axes = (("narrow", n, scratch[0], *scratch[2:4]), ("wide", w, scratch[1], *scratch[4:6]))
        self.copies = [[], []]

    def send(self, which, value):
        axis, size, slots, send, recv = self.axes[which]
        me = lax.axis_index(axis)
        slots[me] = value
        for k in range(1, size):
            copy = pltpu.make_async_remote_copy(
                src_ref=slots.at[me],
                dst_ref=slots.at[me],
                send_sem=send.at[k],
                recv_sem=recv.at[k],
                device_id={axis: lax.rem(me + k, size)},
                device_id_type=MESH,
            )
            copy.start()
            self.copies[which].append(copy)

    def total(self, which):
        _, size, slots, _, _ = self.axes[which]
        for copy in self.copies[which]:
            copy.wait_recv()
        total = slots[0]
        for k in range(1, size):
            total = total + slots[k]
        return total

    def begin(self, value):
        self.send(0, value)

    def middle(self):
        self.send(1, self.total(0))

    def end(self):
        total = self.total(1)
        for copies in self.copies:
            for copy in copies:
                copy.wait_send()
        return total


def forward_scale(stats, params, number):
    mean = stats[0:1] / number
    scale = lax.rsqrt(stats[1:2] / number - mean * mean + EPS)
    a = scale * params[0]
    return a, params[1] - mean * a, scale, mean


def backward_scale(stats, params, grads, number):
    mean = stats[0:1] / number
    scale = lax.rsqrt(stats[1:2] / number - mean * mean + EPS)
    a = scale * params[0]
    gain_grad, bias_grad = grads[0:1], grads[1:2]
    over = a / number
    return a, over * scale * gain_grad, over * (bias_grad - mean * scale * gain_grad)


def norm_params(gain_ref, bias_ref, which, inner):
    lane = (0, inner, 2 * inner, gain_ref.shape[1])
    at = slice(lane[which], lane[which + 1])
    return gain_ref[0:1, at], bias_ref[0:1, at]


def second_counts(counts_ref, g):
    return jnp.where(counts_ref[g] == 2, 1.0, 0.0)


def two_sums(first, second, m):
    return jnp.sum(first, axis=(0, 1))[None] + m * jnp.sum(second, axis=(0, 1))[None]


def padded_rows(count):
    return -(-count // 16) * 16


def halo_rows(images):
    starts, at = [], 0
    for g in range(3):
        starts.append(at)
        at += padded_rows(COLUMNS[g] * images)
    return starts, at


def pack_halo(value):
    count = value.shape[0] * value.shape[1]
    value = value.reshape(count, value.shape[2])
    extra = padded_rows(count) - count
    if extra:
        value = jnp.concatenate([value, jnp.zeros((extra, value.shape[1]), F32)], axis=0)
    return value.astype(BF16)


def unpack_halo(value, columns, images):
    return value.astype(F32)[: columns * images].reshape(columns, images, value.shape[1])


def halo_copies(n, g, count, starts, up_src, up_dst, down_src, down_dst, sems):
    me = lax.axis_index("narrow")
    rows = pl.ds(starts[g], count)
    forward = pltpu.make_async_remote_copy(
        src_ref=up_src.at[rows],
        dst_ref=up_dst.at[rows],
        send_sem=sems.at[0, g],
        recv_sem=sems.at[1, g],
        device_id={"narrow": lax.rem(me + 1, n)},
        device_id_type=MESH,
    )
    backward = pltpu.make_async_remote_copy(
        src_ref=down_src.at[rows],
        dst_ref=down_dst.at[rows],
        send_sem=sems.at[2, g],
        recv_sem=sems.at[3, g],
        device_id={"narrow": lax.rem(me + n - 1, n)},
        device_id_type=MESH,
    )
    return forward, backward


def halo_start(n, copies):
    me = lax.axis_index("narrow")

    @pl.when(me < n - 1)
    def _():
        copies[0].start()

    @pl.when(me > 0)
    def _():
        copies[1].start()


def halo_arrived(n, copies):
    me = lax.axis_index("narrow")

    @pl.when(me > 0)
    def _():
        copies[0].wait_recv()

    @pl.when(me < n - 1)
    def _():
        copies[1].wait_recv()


def halo_sent(n, copies):
    me = lax.axis_index("narrow")

    @pl.when(me < n - 1)
    def _():
        copies[0].wait_send()

    @pl.when(me > 0)
    def _():
        copies[1].wait_send()


def halo_edges(n, from_before, from_after):
    me = lax.axis_index("narrow")

    @pl.when(me == 0)
    def _():
        from_before[...] = jnp.zeros(from_before.shape, from_before.dtype)

    @pl.when(me == n - 1)
    def _():
        from_after[...] = jnp.zeros(from_after.shape, from_after.dtype)


RING = 6
CHUNK = 512


def turn(source, columns, target):
    for k in range(source.shape[0] // 128):
        target[:, k * 128 : (k + 1) * 128] = source[k * 128 : (k + 1) * 128, columns].T


def place_of(t):
    g = (t >= FIRST[1]).astype(jnp.int32) + (t >= FIRST[2]).astype(jnp.int32)
    return g, t - jnp.where(g == 0, FIRST[0], jnp.where(g == 1, FIRST[1], FIRST[2]))


def forward_kernel(
    n, w, number, x_ref, reduce_ref, spatial_ref, expand_ref, gain_ref, bias_ref, counts_ref,
    rows_out, one_out, two_out, upper_out, middle_out, lower_out, hidden_out, three_out, inner_out, outer_out,
    reduce_out, spatial_out, expand_out,
    stat_one, stat_two, stat_three, hidden_sum, square_reduce, square_spatial, square_expand,
    ring, rows, weight, wide_weight, reduce, spatial, expand, one, two, upper, middle, lower, hidden, three,
    turned, inner,
    stage_one, stage_two, order, last, first, above, below, halo_sems, ring_sems, weight_sems, wide_sem, out_sems,
    *scratch,
):
    m = [second_counts(counts_ref, g) for g in range(3)]
    stages = (stage_one, stage_two)
    sum_one = SumAll(n, w, scratch[:6])
    sum_two = SumAll(n, w, scratch[6:12])
    sum_three = SumAll(n, w, scratch[12:18])
    images = x_ref.shape[1]
    lanes = x_ref.shape[3] // 2
    channels = one.shape[3]
    block = 2 * images
    tail = BLOCKS * block
    starts, _ = halo_rows(images)
    outs = []

    def put(source, target):
        copy = pltpu.make_async_copy(source, target, out_sems.at[len(outs)])
        copy.start()
        outs.append(copy)

    def fetch(t):
        g, j = place_of(t)
        slot = lax.rem(t, RING)
        return pltpu.make_async_copy(x_ref.at[g, :, j], ring.at[slot], ring_sems.at[slot])

    sources = [reduce_ref.at[k : k + CHUNK] for k in range(0, reduce_ref.shape[0], CHUNK)]
    reduce_chunks = len(sources)
    sources += [spatial_ref.at[k : k + CHUNK] for k in range(0, spatial_ref.shape[0], CHUNK)]
    slots = weight.shape[0]

    def weight_copy(k):
        return pltpu.make_async_copy(sources[k], weight.at[k % slots], weight_sems.at[k % slots])

    for t in range(RING):
        fetch(jnp.int32(t)).start()
    for k in range(slots):
        weight_copy(k).start()
    wide_copy = pltpu.make_async_copy(expand_ref, wide_weight, wide_sem)
    wide_copy.start()
    greet(n, w)
    order[...] = to_rows(lanes)
    rows[tail:, :] = jnp.zeros((rows.shape[0] - tail, rows.shape[1]), BF16)
    three[tail:, :] = jnp.zeros((three.shape[0] - tail, three.shape[1]), BF16)
    for ref in (upper, middle, lower):
        for at in (0, PADDED[1] - 1, PADDED[2] - 1, PADDED_BLOCKS - 1):
            ref[at * block : (at + 1) * block] = jnp.zeros((block, channels), BF16)
    halo_edges(n, above, below)

    def cast_chunk(k, wb_ref, row, square):
        weight_copy(k).wait()
        square = cast_rows(weight.at[k % slots], wb_ref, row, square)
        if k + slots < len(sources):
            weight_copy(k + slots).start()
        return square

    def place(i, _):
        for k in range(2):
            fetch(2 * i + k).wait()
        for k, stage in enumerate(stages):
            slot = lax.rem(2 * i + k, RING)
            turn_in(
                order[...],
                lambda j, slot=slot: ring[slot, 8 * j : 8 * j + 8].reshape(16 * lanes, 128),
                stage,
            )
        for k, stage in enumerate(stages):
            row = pl.multiple_of((2 * i + k) * block, block)
            for c in range(lanes):
                rows[pl.ds(row, block), c * 128 : (c + 1) * 128] = jnp.concatenate(
                    [staged(stage, c, 0), staged(stage, c, 1)], axis=0
                ).astype(BF16)

        @pl.when(2 * i + RING < BLOCKS)
        def _():
            for k in range(2):
                fetch(2 * i + k + RING).start()

        return 0

    lax.fori_loop(0, BLOCKS // 2, place, 0)
    put(rows, rows_out)
    square = jnp.zeros((8, channels), F32)
    for k in range(reduce_chunks):
        square = cast_chunk(k, reduce, k * CHUNK, square)
    square_reduce[...] = jnp.sum(square, axis=0, keepdims=True)
    put(reduce, reduce_out)
    sums = jnp.zeros((1, channels), F32)
    squares = jnp.zeros((1, channels), F32)
    for g in range(3):
        at = slice(FIRST[g] * block, (FIRST[g] + COLUMNS[g]) * block)
        c = dot(rows[at, :], reduce[...]).reshape(COLUMNS[g], 2, images, channels)
        one[FIRST[g] : FIRST[g] + COLUMNS[g]] = c
        sums = sums + two_sums(c[:, 0], c[:, 1], m[g])
        squares = squares + two_sums(c[:, 0] * c[:, 0], c[:, 1] * c[:, 1], m[g])
    met(n, w)
    sum_one.begin(jnp.concatenate([sums, squares], axis=0))
    put(one, one_out)
    square = jnp.zeros((8, channels), F32)
    middle_chunk = (reduce_chunks + len(sources)) // 2
    for k in range(reduce_chunks, middle_chunk):
        square = cast_chunk(k, spatial, (k - reduce_chunks) * CHUNK, square)
    for g in range(3):
        value = one[FIRST[g] : FIRST[g] + COLUMNS[g]]
        value = jnp.stack([value[:, 0], value[:, 1] * m[g]], axis=1)
        hidden[FIRST[g] * block : (FIRST[g] + COLUMNS[g]) * block] = value.reshape(
            COLUMNS[g] * block, channels
        ).astype(BF16)
    hidden[tail:] = jnp.zeros((hidden.shape[0] - tail, channels), BF16)
    sum_one.middle()
    turn(hidden, slice(0, channels), turned.at[:channels])
    lane = lax.broadcasted_iota(jnp.int32, (16, turned.shape[1]), 1)
    place = lax.div(lane, block)
    flag = jnp.where(place < FIRST[1], m[0], jnp.where(place < FIRST[2], m[1], m[2]))
    flag = jnp.where(lax.rem(lane, block) < images, 1.0, flag)
    turned[channels:] = jnp.where(lane < tail, flag, 0.0).astype(BF16)

    def inner_chunk(k):
        at = slice(k * 256, (k + 1) * 256)
        inner[:, at] = dot(turned[...], rows[:, at])

    inner_chunks = rows.shape[1] // 256
    for k in range(middle_chunk, len(sources)):
        square = cast_chunk(k, spatial, (k - reduce_chunks) * CHUNK, square)
    for k in range(inner_chunks // 4):
        inner_chunk(k)
    square_spatial[...] = jnp.sum(square, axis=0, keepdims=True)
    put(spatial, spatial_out)
    stats = sum_one.end()
    stat_one[...] = stats

    a, b, _, _ = forward_scale(stats, norm_params(gain_ref, bias_ref, 0, channels), number)
    copies = []
    for g in range(3):
        v = one[FIRST[g] : FIRST[g] + COLUMNS[g]] * a + b
        value = v * half_of(v)[0]
        slot_one, slot_two = value[:, 0], value[:, 1] * m[g]
        count = padded_rows(COLUMNS[g] * images)
        first[starts[g] : starts[g] + count] = pack_halo(slot_one)
        last[starts[g] : starts[g] + count] = pack_halo(
            jnp.where(m[g] > 0.5, slot_two, slot_one)
        )
        copies.append(halo_copies(n, g, count, starts, last, above, first, below, halo_sems))
        halo_start(n, copies[g])
        both = jnp.stack([slot_one, slot_two], axis=1).reshape(COLUMNS[g] * block, channels)
        middle[PADDED[g] * block : (PADDED[g] + COLUMNS[g]) * block] = both.astype(BF16)

    def taps(ref, g, level):
        at, count = PADDED[g] * block, COLUMNS[g] * block
        shifted = [ref[at + d * block : at + d * block + count, :] for d in (-1, 0, 1)]
        return dot(
            jnp.concatenate(shifted, axis=1),
            spatial[3 * level * channels : 3 * (level + 1) * channels, :],
        )

    def put_groups(source, target):
        for g in range(3):
            count = COLUMNS[g] * block
            put(
                source.at[PADDED[g] * block : PADDED[g] * block + count],
                target.at[FIRST[g] * block : FIRST[g] * block + count],
            )

    for g in range(3):
        two[FIRST[g] : FIRST[g] + COLUMNS[g]] = taps(middle, g, 1).reshape(
            COLUMNS[g], 2, images, channels
        )
    put_groups(middle, middle_out)
    sums = jnp.zeros((1, channels), F32)
    squares = jnp.zeros((1, channels), F32)
    for g in range(3):
        halo_arrived(n, copies[g])
        at, count = PADDED[g] * block, COLUMNS[g] * block
        height = padded_rows(COLUMNS[g] * images)
        up = unpack_halo(above[starts[g] : starts[g] + height], COLUMNS[g], images)
        down = unpack_halo(below[starts[g] : starts[g] + height], COLUMNS[g], images)
        own = middle[at : at + count].astype(F32).reshape(COLUMNS[g], 2, images, channels)
        upper[at : at + count] = (
            jnp.stack([up, own[:, 0]], axis=1).reshape(count, channels).astype(BF16)
        )
        lower[at : at + count] = (
            jnp.stack([jnp.where(m[g] > 0.5, own[:, 1], down), down], axis=1)
            .reshape(count, channels)
            .astype(BF16)
        )
        c = taps(upper, g, 0) + taps(lower, g, 2)
        c = c.reshape(COLUMNS[g], 2, images, channels) + two[FIRST[g] : FIRST[g] + COLUMNS[g]]
        two[FIRST[g] : FIRST[g] + COLUMNS[g]] = c
        sums = sums + two_sums(c[:, 0], c[:, 1], m[g])
        squares = squares + two_sums(c[:, 0] * c[:, 0], c[:, 1] * c[:, 1], m[g])
    sum_two.begin(jnp.concatenate([sums, squares], axis=0))
    put(two, two_out)
    put_groups(upper, upper_out)
    put_groups(lower, lower_out)
    wide_copy.wait()
    half = wide_weight.shape[0] // 2
    square = jnp.zeros((8, wide_weight.shape[1]), F32)
    square = cast_rows(wide_weight.at[:half], expand, 0, square)
    for k in range(inner_chunks // 4, inner_chunks // 2):
        inner_chunk(k)
    sum_two.middle()
    square = cast_rows(wide_weight.at[half:], expand, half, square)
    square_expand[...] = jnp.sum(square, axis=0, keepdims=True)
    put(expand, expand_out)
    for k in range(inner_chunks // 2, inner_chunks):
        inner_chunk(k)
    put(inner, inner_out)
    inner_done = outs[-1]
    for g in range(3):
        halo_sent(n, copies[g])
    stats = sum_two.end()
    stat_two[...] = stats

    a, b, _, _ = forward_scale(stats, norm_params(gain_ref, bias_ref, 1, channels), number)
    sums = jnp.zeros((1, channels), F32)
    for g in range(3):
        v = two[FIRST[g] : FIRST[g] + COLUMNS[g]] * a + b
        value = v * half_of(v)[0]
        both = jnp.stack([value[:, 0], value[:, 1] * m[g]], axis=1)
        sums = sums + jnp.sum(both, axis=(0, 1, 2))[None]
        hidden[FIRST[g] * block : (FIRST[g] + COLUMNS[g]) * block] = both.reshape(
            COLUMNS[g] * block, channels
        ).astype(BF16)
    hidden_sum[...] = sums
    put(hidden.at[:tail], hidden_out.at[:tail])
    sums, squares = [], []
    for part in range(three.shape[1] // 512):
        s = jnp.zeros((1, 512), F32)
        q = jnp.zeros((1, 512), F32)
        columns = slice(part * 512, (part + 1) * 512)
        for g in range(3):
            at = slice(FIRST[g] * block, (FIRST[g] + COLUMNS[g]) * block)
            c = dot(hidden[at, :], expand[:, columns])
            three[at, columns] = c.astype(BF16)
            s = s + jnp.sum(c, axis=0, keepdims=True)
            q = q + jnp.sum(c * c, axis=0, keepdims=True)
        put(three.at[:tail, columns], three_out.at[:, columns])
        sums.append(s)
        squares.append(q)
    sum_three.begin(
        jnp.concatenate(
            [jnp.concatenate(sums, axis=1), jnp.concatenate(squares, axis=1)], axis=0
        )
    )
    turn(hidden, slice(0, channels), turned.at[:channels])
    inner_done.wait()
    outs = [copy for copy in outs if copy is not inner_done]

    def outer_chunk(k):
        at = slice(k * 256, (k + 1) * 256)
        inner[:channels, at] = dot(turned[:channels], three[:, at])

    for k in range(inner_chunks // 4):
        outer_chunk(k)
    sum_three.middle()
    for k in range(inner_chunks // 4, inner_chunks):
        outer_chunk(k)
    put_last = pltpu.make_async_copy(inner.at[:channels], outer_out, out_sems.at[31])
    put_last.start()
    stat_three[...] = sum_three.end()
    for copy in outs:
        copy.wait()
    put_last.wait()


DEPTH = 4


def top_kernel(
    number, inner, conv_ref, rows_ref, up_ref, stats_ref, gain_ref, bias_ref, counts_ref,
    out_ref, grad_ref, total,
    conv_ring, rows_ring, up_ring, out_ring, grad_ring, up_one, up_two, out_one, out_two, order, coefficients, sems,
):
    images = up_ref.shape[1]
    lanes = up_ref.shape[3] // 2
    block = 2 * images

    def rows_of(t):
        return pl.ds(pl.multiple_of(t * block, block), block)

    def copy(which, t):
        slot = lax.rem(t, DEPTH)
        g, j = place_of(t)
        source, target = (
            lambda: (conv_ref.at[rows_of(t)], conv_ring.at[slot]),
            lambda: (rows_ref.at[rows_of(t)], rows_ring.at[slot]),
            lambda: (up_ref.at[g, :, j], up_ring.at[slot]),
            lambda: (out_ring.at[slot], out_ref.at[g, :, j]),
            lambda: (grad_ring.at[slot], grad_ref.at[rows_of(t)]),
        )[which]()
        return pltpu.make_async_copy(source, target, sems.at[which, slot])

    def each(which, t, do):
        @pl.when((t >= 0) & (t < BLOCKS))
        def _():
            do(copy(which, t))

    def start(which, t):
        each(which, t, lambda c: c.start())

    def wait(which, t):
        each(which, t, lambda c: c.wait())

    for t in range(3):
        start(2, jnp.int32(t))
        if t < 2:
            start(0, jnp.int32(t))
            start(1, jnp.int32(t))
    total[...] = jnp.zeros(total.shape, F32)
    params = norm_params(gain_ref, bias_ref, 2, inner)
    a, b, scale, mean = forward_scale(stats_ref[...], params, number)
    coefficients[0:1] = a
    coefficients[1:2] = b
    order[0] = to_rows(lanes)
    order[1] = from_rows(lanes)
    out_two[...] = jnp.zeros(out_two.shape, F32)

    def enter(t, stage):
        slot = lax.rem(t, DEPTH)
        turn_in(
            order[0], lambda k: up_ring[slot, 8 * k : 8 * k + 8].reshape(16 * lanes, 128), stage
        )

    def leave(t, stage):
        slot = lax.rem(t + DEPTH, DEPTH)

        def store(k, value):
            out_ring[slot, 8 * k : 8 * k + 8] = value.reshape(8, 2 * lanes, 128)

        turn_out(order[1], stage, store)

    def work(t, stage_up, stage_out):
        slot = lax.rem(t, DEPTH)
        m = second_counts(counts_ref, place_of(t)[0])
        for c in range(lanes):
            at = slice(c * 128, (c + 1) * 128)
            raw = conv_ring[slot, :, at].astype(F32)
            v = raw * coefficients[0:1, at] + coefficients[1:2, at]
            v = v + rows_ring[slot, :, at].astype(F32)
            h, squared = half_of(v)
            out = v * h
            slope = h + out * (1.0 - h) * (2.0 * C0 + 6.0 * C1 * squared)
            put_staged(stage_out, c, 0, out[:images])
            put_staged(stage_out, c, 1, out[images:] * m)
            grad = jnp.concatenate(
                [
                    slope[:images] * staged(stage_up, c, 0),
                    slope[images:] * (staged(stage_up, c, 1) * m),
                ],
                axis=0,
            )
            grad_ring[slot, :, at] = grad.astype(BF16)
            total[0, :, at] += jnp.sum((grad * raw).reshape(block // 8, 8, 128), axis=0)
            total[1, :, at] += jnp.sum(grad.reshape(block // 8, 8, 128), axis=0)

    wait(2, jnp.int32(0))
    enter(jnp.int32(0), up_one)

    def pair(i, _):
        t = 2 * i
        for k in (2, 3):
            start(0, t + k)
            start(1, t + k)
            start(2, t + k + 1)
        for k in (0, 1):
            wait(0, t + k)
            wait(1, t + k)
            wait(2, t + k + 1)
            wait(3, t + k - 1 - DEPTH)
            wait(4, t + k - DEPTH)
        enter(t + 1, up_two)
        work(t, up_one, out_one)
        leave(t - 1, out_two)
        enter(t + 2, up_one)
        work(t + 1, up_two, out_two)
        leave(t, out_one)
        for k in (0, 1):
            start(3, t + k - 1)
            start(4, t + k)
        return 0

    lax.fori_loop(0, BLOCKS // 2, pair, 0)
    last = jnp.int32(BLOCKS - 1)
    wait(3, last - DEPTH)
    leave(last, out_two)
    start(3, last)
    for k in range(DEPTH):
        wait(3, last - k)
        wait(4, last - k)
    out_ring[0] = jnp.zeros(out_ring.shape[1:], BF16)
    copies = []
    for g in range(3):
        for j in range(COLUMNS[g], out_ref.shape[2]):
            copies.append(
                pltpu.make_async_copy(
                    out_ring.at[0], out_ref.at[g, :, j], sems.at[5, len(copies)]
                )
            )
            copies[-1].start()
    value = jnp.sum(total[...], axis=1)
    gains = scale * (value[0:1] - mean * value[1:2])
    total[0] = jnp.concatenate([gains, jnp.zeros((7, gains.shape[1]), F32)], axis=0)
    for copy in copies:
        copy.wait()


def unravel(index, sizes):
    digits = []
    for size in reversed(sizes):
        digits.append(index % size if isinstance(index, int) else lax.rem(index, size))
        index = index // size if isinstance(index, int) else lax.div(index, size)
    return digits[::-1]


def mesh_digits(n, w):
    if (n, w) == (4, 8):
        return (
            [("narrow", 2, 2), ("narrow", 1, 2), ("wide", 2, 4), ("wide", 1, 2)],
            [(1, 3, 0, 2), (1, 0, 3, 2)],
        )
    return [("narrow", 1, n), ("wide", 1, w)], [(0, 1), (0, 1)]


def digit_sizes(n, w):
    return [d[2] for d in mesh_digits(n, w)[0]]


def narrow_digits(n, w):
    return [d[2] for d in mesh_digits(n, w)[0] if d[0] == "narrow"]


def wide_digits(n, w):
    return [d[2] for d in mesh_digits(n, w)[0] if d[0] == "wide"]


def weight_parts(w, rows):
    share = rows // w
    if rows >= 4096 and share % 64 == 0:
        return 4
    return 2 if share % 32 == 0 else 1


def block_shapes(n, w, rows, columns):
    parts = weight_parts(w, rows)
    return [(*digit_sizes(n, w), rows // w // parts, columns // n)] * parts


def put_blocks(n, w, refs, value, row, rows, place_n=None, place_w=0, lane=0):
    share = rows // w
    part = share // len(refs)
    at, end = row, row + value.shape[0]
    columns = refs[0].shape[-1]
    while at < end:
        stop = min(end, (at // part + 1) * part)
        wide = at // share
        ref = refs[at // part % len(refs)]
        inside = slice(at % part, at % part + stop - at)
        piece = value[at - row : stop - row]
        wide = unravel(place_w + wide, wide_digits(n, w))
        if place_n is not None:
            lanes = slice(lane, lane + piece.shape[1])
            ref[(*unravel(place_n, narrow_digits(n, w)), *wide, inside, lanes)] = piece.astype(BF16)
        else:
            for k in range(n):
                ref[(*unravel(k, narrow_digits(n, w)), *wide, inside, slice(None))] = piece[
                    :, k * columns : (k + 1) * columns
                ].astype(BF16)
        at = stop


def scatter_scratch(n, w, rows, columns):
    digits, orders = mesh_digits(n, w)
    scratch = []
    for part, shape in enumerate(block_shapes(n, w, rows, columns)):
        left = list(range(len(digits)))
        for d in orders[part % 2]:
            left.remove(d)
            size = digits[d][2]
            scratch.append(VMEM((size - 1, *(digits[k][2] for k in left), *shape[-2:]), BF16))
            scratch.append(pltpu.SemaphoreType.DMA((size - 1,)))
            scratch.append(pltpu.SemaphoreType.DMA((size - 1,)))
    return scratch


class Scatter:
    def __init__(self, n, w, source, scratch, order):
        self.digits = mesh_digits(n, w)[0]
        self.order = order
        self.scratch = scratch
        self.sources = [source] + [scratch[3 * k].at[0] for k in range(len(order))]
        self.copies = []
        self.steps = len(order)

    def own(self, d):
        axis, stride, size = self.digits[d]
        return lax.rem(lax.div(lax.axis_index(axis), stride), size)

    def pick(self, ref, step, value):
        left = [d for d in range(len(self.digits)) if d not in self.order[:step]]
        return ref.at[tuple(value if d == self.order[step] else slice(None) for d in left)]

    def start(self, step):
        d = self.order[step]
        axis, stride, size = self.digits[d]
        landing, send, recv = self.scratch[3 * step : 3 * step + 3]
        mine = self.own(d)
        for k in range(1, size):
            other = lax.rem(mine + k, size)
            copy = pltpu.make_async_remote_copy(
                src_ref=self.pick(self.sources[step], step, other),
                dst_ref=landing.at[k - 1],
                send_sem=send.at[k - 1],
                recv_sem=recv.at[k - 1],
                device_id={axis: lax.axis_index(axis) + (other - mine) * stride},
                device_id_type=MESH,
            )
            copy.start()
            self.copies.append((step, copy))

    def finish(self, step):
        for at, copy in self.copies:
            if at == step:
                copy.wait_recv()
        d = self.order[step]
        size = self.digits[d][2]
        landing = self.scratch[3 * step]
        left = [k for k in range(len(self.digits)) if k not in self.order[: step + 1]]
        sizes = [self.digits[k][2] for k in left]
        mine = self.own(d)
        source = self.pick(self.sources[step], step, mine)

        def total(at):
            value = source[at].astype(F32)
            for k in range(size - 1):
                value = value + landing[(k, *at)].astype(F32)
            return value

        if step == self.steps - 1:
            return total((slice(None), slice(None)))
        count = 1
        for k in sizes:
            count *= k

        together = 4 if count % 4 == 0 else 1

        def add(index, _):
            for k in range(together):
                at = tuple(unravel(index * together + k, sizes))
                landing[(0, *at)] = total(at).astype(BF16)
            return 0

        lax.fori_loop(0, count // together, add, 0)

    def done(self):
        for _, copy in self.copies:
            copy.wait_send()


def share_out(n, slots, value, send, recv):
    me = lax.axis_index("narrow")
    row = 0
    for piece in value:
        slots[me, row : row + piece.shape[0]] = piece.astype(BF16)
        row += piece.shape[0]
    copies = []
    for k in range(1, n):
        copy = pltpu.make_async_remote_copy(
            src_ref=slots.at[me],
            dst_ref=slots.at[me],
            send_sem=send.at[k],
            recv_sem=recv.at[k],
            device_id={"narrow": lax.rem(me + k, n)},
            device_id_type=MESH,
        )
        copy.start()
        copies.append(copy)
    return copies


BETA = 1.0 - STEP ** (-0.8)


class Refs:
    def __init__(self, refs):
        self.refs = list(refs)

    def take(self, count):
        taken, self.refs = self.refs[:count], self.refs[count:]
        return taken

    def one(self):
        return self.take(1)[0]


def backward_kernel(
    n, w, number, shapes, three_ref, grad_ref, hidden_ref, expand_ref, two_ref, spatial_ref,
    upper_ref, middle_ref, lower_ref, one_ref, rows_ref, reduce_ref, inner_ref, outer_ref, sums_ref, hidden_sum, stat_one, stat_two, stat_three,
    gain_ref, bias_ref, counts_ref, reduce_rows_ref, spatial_rows_ref, expand_rows_ref, *refs,
):
    refs = Refs(refs)
    parts = [weight_parts(w, shape[0]) for shape in shapes]
    input_ref, columns_ref = refs.take(2)
    shares = refs.take(3)
    norm_one, norm_two, norm_three = refs.take(3)
    three, wide, hidden, turned, expand, spatial, two, one, u, coefficients = refs.take(10)
    inner_ring, inner_sems = refs.take(2)
    to_before, to_after, from_after, from_before, halo_sems, in_sems = refs.take(6)
    gradients = [refs.take(parts[k]) for k in range(3)]
    orders = mesh_digits(n, w)[1]
    steps = len(orders[0])
    scatters = [
        [
            Scatter(n, w, gradients[k][p], refs.take(3 * steps), orders[p % 2])
            for p in range(parts[k])
        ]
        for k in range(3)
    ]
    share_sems = [refs.take(2) for _ in range(3)]
    sum_three = SumAll(n, w, refs.take(6))
    sum_two = SumAll(n, w, refs.take(6))
    sum_one = SumAll(n, w, refs.take(6))
    column_scratch = refs.take(3)

    images = two.shape[2]
    channels = two.shape[3]
    block = 2 * images
    tail = BLOCKS * block
    deep = three.shape[0]
    m = [second_counts(counts_ref, g) for g in range(3)]
    starts, _ = halo_rows(images)

    ins = {}

    def get(name, source, target):
        ins[name] = pltpu.make_async_copy(source, target, in_sems.at[len(ins)])
        ins[name].start()

    get("hidden", hidden_ref.at[:tail], hidden.at[:tail])
    get("three", three_ref, three.at[:tail])
    get("grad", grad_ref, wide.at[:tail])
    get("expand", expand_ref, expand)
    get("two", two_ref, two)
    get("one", one_ref, one)
    greet(n, w)

    def norm_scale(which, stat, grads):
        params = norm_params(gain_ref, bias_ref, which, channels)
        return backward_scale(stat[...], params, grads, number)

    sent = {}

    def advance(which, step, half=None):
        if step >= steps:
            return
        count = parts[which]
        if half is not None and count == 1:
            if half == 0:
                return
            half = None
        first = 0 if half is None else half * (count // 2)
        last = count if half is None else first + count // 2
        for scatter in scatters[which][first:last]:
            value = scatter.finish(step)
            if step < steps - 1:
                scatter.start(step + 1)
            else:
                sent.setdefault(which, []).append(value)
        if step == steps - 1 and last == count:
            sent[which] = share_out(n, shares[which], sent[which], *share_sems[which])

    def launch(which):
        for scatter in scatters[which]:
            scatter.start(0)

    value = jnp.concatenate(
        [sums_ref[0, 0:1], jnp.sum(sums_ref[1], axis=0, keepdims=True)],
        axis=0,
    )
    halo_edges(n, from_before, from_after)
    wide[tail:, :] = jnp.zeros((deep - tail, wide.shape[1]), BF16)
    hidden[tail:deep] = jnp.zeros((deep - tail, channels), BF16)
    met(n, w)
    sum_three.begin(value)
    ins["hidden"].wait()
    turn(hidden.at[:deep], slice(0, channels), turned.at[0])
    ins["grad"].wait()

    def held(k):
        return (k // 6, slice(None), slice(k % 6 * 256, (k % 6 + 1) * 256))

    inner_chunks = wide.shape[1] // 256

    def raw_chunk(k):
        value = dot(turned[0], wide[:, k * 256 : (k + 1) * 256])
        high = value.astype(BF16)
        spatial[held(k)] = high
        spatial[held(inner_chunks + k)] = (value - high.astype(F32)).astype(BF16)

    def raw_value(k):
        return spatial[held(k)].astype(F32) + spatial[held(inner_chunks + k)].astype(F32)

    def inner_copy(ref, k):
        return pltpu.make_async_copy(
            ref.at[:, k * 256 : (k + 1) * 256],
            inner_ring.at[k % 2, : ref.shape[0]],
            inner_sems.at[k % 2],
        )

    def column(value):
        return jnp.broadcast_to(value, (128, channels)).T[:, 0:1]

    for k in range(2):
        raw_chunk(k)
    sum_three.middle()
    for k in range(2, inner_chunks):
        raw_chunk(k)
    for k in range(2):
        inner_copy(outer_ref, k).start()
    ins["three"].wait()
    ins["expand"].wait()
    grads = sum_three.end()
    norm_three[...] = grads
    a, b, c = norm_scale(2, stat_three, grads)
    coefficients[0:1] = a
    coefficients[1:2] = b
    coefficients[2:3] = c
    def back_three(g):
        rows = slice(FIRST[g] * block, (FIRST[g] + COLUMNS[g]) * block)
        for k in range(inner_chunks):
            at = slice(k * 256, (k + 1) * 256)
            a, b, c = coefficients[0:1, at], coefficients[1:2, at], coefficients[2:3, at]
            up = wide[rows, at].astype(F32) * a
            raw = (three[rows, at].astype(F32) * b + c).reshape(COLUMNS[g], 2, images, 256)
            raw = jnp.stack([raw[:, 0], raw[:, 1] * m[g]], axis=1).reshape(up.shape)
            wide[rows, at] = (up - raw).astype(BF16)

    ins["two"].wait()
    a, b, scale, mean = forward_scale(
        stat_two[...], norm_params(gain_ref, bias_ref, 1, channels), number
    )
    sums = jnp.zeros((1, channels), F32)
    gains = jnp.zeros((1, channels), F32)
    back_three(0)
    for g in range(3):
        if g < 2:
            back_three(g + 1)
        blocks = slice(FIRST[g], FIRST[g] + COLUMNS[g])
        raw = two[blocks]
        v = raw * a + b
        rows = slice(FIRST[g] * block, (FIRST[g] + COLUMNS[g]) * block)
        value = slope_of(v, *half_of(v)) * dot_t(wide[rows, :], expand[...]).reshape(raw.shape)
        value = jnp.stack([value[:, 0], value[:, 1] * m[g]], axis=1)
        u[blocks] = value
        sums = sums + jnp.sum(value, axis=(0, 1, 2))[None]
        gains = gains + jnp.sum(value * ((raw - mean) * scale), axis=(0, 1, 2))[None]
    for k, source in enumerate((upper_ref, middle_ref, lower_ref)):
        get(k, source.at[:tail], wide.at[:tail, k * channels : (k + 1) * channels])
    sum_two.begin(jnp.concatenate([gains, sums], axis=0))
    for at in (0, PADDED[1] - 1, PADDED[2] - 1, PADDED_BLOCKS - 1):
        hidden[at * block : (at + 1) * block] = jnp.zeros((block, channels), BF16)
    per = inner_chunks // n
    sum_column = column(hidden_sum[...])

    def expand_chunk(k):
        at = slice(k * 256, (k + 1) * 256)
        a, b, c = coefficients[0:1, at], coefficients[1:2, at], coefficients[2:3, at]
        inner_copy(outer_ref, k).wait()
        value = raw_value(k) * a - inner_ring[k % 2, :channels] * b - sum_column * c
        put_blocks(
            n, w, gradients[2], value, 0, channels, place_n=k // per, lane=k % per * 256
        )
        if k + 2 < inner_chunks:
            inner_copy(outer_ref, k + 2).start()

    for k in range(inner_chunks // 2):
        expand_chunk(k)
    sum_two.middle()
    for k in range(inner_chunks // 2, inner_chunks):
        expand_chunk(k)
    launch(2)
    for tap in range(9):
        get(
            ("spatial", tap),
            spatial_ref.at[tap * channels : (tap + 1) * channels],
            spatial.at[tap // 3, :, tap % 3 * channels : (tap % 3 + 1) * channels],
        )
    ins[0].wait()
    turn(wide, slice(0, channels), turned.at[0])
    for k in (1, 2):
        ins[k].wait()
        turn(wide, slice(k * channels, (k + 1) * channels), turned.at[k])
    get("rows", rows_ref, wide)
    grads = sum_two.end()
    norm_two[...] = grads
    a, b, c = norm_scale(1, stat_two, grads)
    for g in range(3):
        blocks = slice(FIRST[g], FIRST[g] + COLUMNS[g])
        up = u[blocks] * a
        raw = two[blocks] * b + c
        value = jnp.stack([up[:, 0] - raw[:, 0], up[:, 1] - raw[:, 1] * m[g]], axis=1)
        hidden[PADDED[g] * block : (PADDED[g] + COLUMNS[g]) * block] = value.reshape(
            COLUMNS[g] * block, channels
        ).astype(BF16)
    three[tail:, :] = jnp.zeros((deep - tail, three.shape[1]), BF16)
    for offset in range(3):
        for g in range(3):
            start = (PADDED[g] - (offset - 1)) * block
            three[
                FIRST[g] * block : (FIRST[g] + COLUMNS[g]) * block,
                offset * channels : (offset + 1) * channels,
            ] = hidden[start : start + COLUMNS[g] * block, :]
    advance(2, 0)
    for level in range(3):
        for offset in range(3):
            value = dot(turned[level], three[:, offset * channels : (offset + 1) * channels])
            put_blocks(n, w, gradients[1], value, (3 * level + offset) * channels, shapes[1][0])
        if level > 0:
            advance(2, level)
    launch(1)
    get("again", grad_ref, three.at[:tail])
    for tap in range(9):
        ins["spatial", tap].wait()

    def taps(g, level):
        at, count = PADDED[g] * block, COLUMNS[g] * block
        shifted = [hidden[at - d * block : at - d * block + count, :] for d in (-1, 0, 1)]
        value = dot_t(jnp.concatenate(shifted, axis=1), spatial[level])
        return value.reshape(COLUMNS[g], 2, images, channels)

    copies = []
    for g in range(3):
        flag = m[g] > 0.5
        blocks = slice(FIRST[g], FIRST[g] + COLUMNS[g])
        rows = padded_rows(COLUMNS[g] * images)
        upper = taps(g, 0)
        lower = taps(g, 2)
        to_before[starts[g] : starts[g] + rows] = pack_halo(upper[:, 0])
        to_after[starts[g] : starts[g] + rows] = pack_halo(
            lower[:, 1] + jnp.where(flag, 0.0, lower[:, 0])
        )
        copies.append(
            halo_copies(
                n, g, rows, starts, to_after, from_before, to_before, from_after, halo_sems
            )
        )
        halo_start(n, copies[g])
        u[blocks] = jnp.stack([upper[:, 1], jnp.where(flag, lower[:, 0], 0.0)], axis=1)
    advance(1, 0)
    ins["one"].wait()

    a, b, scale, mean = forward_scale(stat_one[...], norm_params(gain_ref, bias_ref, 0, channels), number)
    sums = jnp.zeros((1, channels), F32)
    gains = jnp.zeros((1, channels), F32)
    for g in range(3):
        flag = m[g] > 0.5
        blocks = slice(FIRST[g], FIRST[g] + COLUMNS[g])
        middle = taps(g, 1)
        rows = padded_rows(COLUMNS[g] * images)
        halo_arrived(n, copies[g])
        before = unpack_halo(from_before[starts[g] : starts[g] + rows], COLUMNS[g], images)
        after = unpack_halo(from_after[starts[g] : starts[g] + rows], COLUMNS[g], images)
        first = u[blocks][:, 0] + middle[:, 0] + before + jnp.where(flag, 0.0, after)
        second = u[blocks][:, 1] + middle[:, 1] + jnp.where(flag, after, 0.0)
        raw = one[blocks]
        v = raw * a + b
        slope = slope_of(v, *half_of(v))
        value = jnp.stack([slope[:, 0] * first, slope[:, 1] * second * m[g]], axis=1)
        u[blocks] = value
        sums = sums + jnp.sum(value, axis=(0, 1, 2))[None]
        gains = gains + jnp.sum(value * ((raw - mean) * scale), axis=(0, 1, 2))[None]
    sum_one.begin(jnp.concatenate([gains, sums], axis=0))
    for k in range(2):
        inner_copy(inner_ref, k).start()
    for g in range(3):
        hidden[FIRST[g] * block : (FIRST[g] + COLUMNS[g]) * block] = (
            u[FIRST[g] : FIRST[g] + COLUMNS[g]].reshape(COLUMNS[g] * block, channels).astype(BF16)
        )
    hidden[tail:deep] = jnp.zeros((deep - tail, channels), BF16)
    turn(hidden.at[:deep], slice(0, channels), turned.at[0])
    ins["rows"].wait()

    for k in range(2):
        raw_chunk(k)
    sum_one.middle()
    for k in range(2, inner_chunks):
        raw_chunk(k)
        if k == 4:
            advance(2, 3)
        if k == 5:
            advance(1, 1, 0)
    for k in range(4):
        at = slice(k * channels, (k + 1) * channels)
        get(("reduce", k), reduce_ref.at[at], wide.at[:channels, at])
    for g in range(3):
        halo_sent(n, copies[g])
    grads = sum_one.end()
    norm_one[...] = grads
    a, b, c = norm_scale(0, stat_one, grads)
    a_column, b_column, c_column = column(a), column(b), column(c)
    advance(1, 1, 1)
    per = 256 // (shapes[0][0] // w)
    for k in range(inner_chunks):
        inner_copy(inner_ref, k).wait()
        value = raw_value(k) * a_column - inner_ring[k % 2, :channels] * b_column
        value = value - inner_ring[k % 2, channels : channels + 1] * c_column
        put_blocks(n, w, gradients[0], value.T, 0, shapes[0][0], place_w=k * per)
        if k + 2 < inner_chunks:
            inner_copy(inner_ref, k + 2).start()
    launch(0)
    advance(1, 2, 0)
    advance(0, 0)
    for g in range(3):
        blocks = slice(FIRST[g], FIRST[g] + COLUMNS[g])
        up = u[blocks] * a
        raw = one[blocks] * b + c
        value = jnp.stack([up[:, 0] - raw[:, 0], up[:, 1] - raw[:, 1] * m[g]], axis=1)
        hidden[FIRST[g] * block : (FIRST[g] + COLUMNS[g]) * block] = value.reshape(
            COLUMNS[g] * block, channels
        ).astype(BF16)
    for k in range(4):
        ins["reduce", k].wait()
    ins["again"].wait()

    def input_step(k, _):
        at = pl.ds(pl.multiple_of(k * 256, 256), 256)
        weight = wide[
            pl.ds(pl.multiple_of(lax.rem(k, 2) * 256, 256), 256),
            pl.ds(pl.multiple_of(lax.div(k, 2) * channels, channels), channels),
        ]
        for g in range(3):
            rows = slice(FIRST[g] * block, (FIRST[g] + COLUMNS[g]) * block)
            value = dot_t(hidden[rows, :], weight) + three[rows, at].astype(F32)
            three[rows, at] = value.astype(BF16)
        return 0

    lax.fori_loop(0, inner_chunks // 2, input_step, 0)
    advance(1, 2, 1)
    advance(0, 1)
    lax.fori_loop(inner_chunks // 2, inner_chunks, input_step, 0)
    get("out", three.at[:tail], input_ref)
    advance(1, 3, 0)
    advance(0, 2)
    columns, totals = [None] * 3, [None] * 3

    def column_sums(which):
        for copy in sent[which]:
            copy.wait_recv()
        old = (reduce_rows_ref, spatial_rows_ref, expand_rows_ref)[which]
        by_column, total = [], None
        for k in range(n):
            value = shares[which][k].astype(F32)
            square = value * value + EPS_ONE
            by_column.append(jnp.sum(square, axis=0, keepdims=True))
            part = jnp.sum(by_column[-1], axis=1, keepdims=True)
            total = part if total is None else total + part
        columns[which] = jnp.concatenate(by_column, axis=1)
        total = BETA * jnp.sum(old[...].reshape(1, -1), axis=1, keepdims=True) + (
            1.0 - BETA
        ) / shapes[which][1] * total
        totals[which] = jnp.broadcast_to(total, (1, 128))

    column_sums(2)
    advance(1, 3, 1)
    advance(0, 3)
    column_sums(1)
    column_sums(0)
    columns_ref[...] = sum_over(
        "wide", w, jnp.concatenate(columns + totals, axis=1), *column_scratch
    )
    for which in range(3):
        for scatter in scatters[which]:
            scatter.done()
        for copy in sent[which]:
            copy.wait_send()
    ins["out"].wait()


def final_kernel(
    w, input_ref, sums_ref, reduce_share, spatial_share, expand_share,
    reduce_ref, spatial_ref, expand_ref, square_reduce, square_spatial, square_expand,
    reduce_rows, spatial_rows, expand_rows, reduce_cols, spatial_cols, expand_cols,
    one_ref, two_ref, three_ref, gain_ref, bias_ref, state_ref,
    out_ref, reduce_grad, spatial_grad, expand_grad, reduce_rows_next, reduce_cols_next, spatial_rows_next,
    spatial_cols_next, expand_rows_next, expand_cols_next, reduce_next, spatial_next, expand_next,
    norm_grads, norm_second, norm_next,
    row_ring, out_ring, zeros, order, reduce_own, spatial_own, expand_own, sems, ring_sems,
):
    me = lax.axis_index("wide")
    own_copies = []
    for k, (source, own) in enumerate(
        ((reduce_ref, reduce_own), (spatial_ref, spatial_own), (expand_ref, expand_own))
    ):
        size = own.shape[0]
        own_copies.append(
            pltpu.make_async_copy(source.at[pl.ds(me * size, size)], own, sems.at[k])
        )
        own_copies[-1].start()
    images = out_ref.shape[1]
    lanes = out_ref.shape[3] // 2
    block = 2 * images

    def copy(which, t):
        slot = lax.rem(t, DEPTH)
        if which == 0:
            rows = pl.ds(pl.multiple_of(t * block, block), block)
            return pltpu.make_async_copy(input_ref.at[rows], row_ring.at[slot], ring_sems.at[0, slot])
        g, j = place_of(t)
        return pltpu.make_async_copy(out_ring.at[slot], out_ref.at[g, :, j], ring_sems.at[1, slot])

    for t in range(DEPTH):
        copy(0, jnp.int32(t)).start()
    order[...] = from_rows(lanes)
    zeros[...] = jnp.zeros(zeros.shape, BF16)
    empty = []
    for g in range(3):
        for j in range(COLUMNS[g], out_ref.shape[2]):
            empty.append(
                pltpu.make_async_copy(zeros, out_ref.at[g, :, j], sems.at[3 + len(empty)])
            )
            empty[-1].start()

    def pair(i, _):
        for k in range(2):
            copy(0, 2 * i + k).wait()

        @pl.when(2 * i >= DEPTH)
        def _():
            for k in range(2):
                copy(1, 2 * i + k - DEPTH).wait()

        for k in range(2):
            slot = lax.rem(2 * i + k, DEPTH)
            pieces = [[] for _ in range(images // 8)]
            for c in range(lanes):
                value = row_ring[slot, :, c * 128 : (c + 1) * 128].astype(F32)
                for row in range(0, block, 8):
                    pieces[row % images // 8].append(value[row : row + 8])
            pieces = [jnp.concatenate(p, axis=0).astype(BF16) for p in pieces]
            for at in range(0, len(pieces), 2):
                value = dot(order[...], jnp.concatenate(pieces[at : at + 2], axis=1)).astype(BF16)
                for j in range(len(pieces[at : at + 2])):
                    out_ring[slot, 8 * (at + j) : 8 * (at + j + 1)] = value[
                        :, 128 * j : 128 * (j + 1)
                    ].reshape(8, 2 * lanes, 128)
        for k in range(2):
            copy(1, 2 * i + k).start()

        @pl.when(2 * i + DEPTH < BLOCKS)
        def _():
            for k in range(2):
                copy(0, 2 * i + k + DEPTH).start()

        return 0

    lax.fori_loop(0, BLOCKS // 2, pair, 0)
    grads = jnp.concatenate([one_ref[...], two_ref[...], three_ref[...]], axis=1)
    norm_grads[...] = grads
    params = jnp.concatenate([gain_ref[...], bias_ref[...]], axis=0)
    second = BETA * state_ref[...] + (1.0 - BETA) * (grads * grads + EPS_ONE)
    norm_second[...] = second
    rate = 0.5 * jnp.maximum(
        jnp.sqrt(jnp.sum(params * params, axis=1, keepdims=True) / params.shape[1]), 0.001
    )
    norm_next[...] = params - rate * grads * lax.rsqrt(second)
    lane = 0
    weights = (
        (reduce_share, reduce_own, square_reduce, reduce_rows, reduce_cols, reduce_grad,
         reduce_rows_next, reduce_cols_next, reduce_next, reduce_ref),
        (spatial_share, spatial_own, square_spatial, spatial_rows, spatial_cols, spatial_grad,
         spatial_rows_next, spatial_cols_next, spatial_next, spatial_ref),
        (expand_share, expand_own, square_expand, expand_rows, expand_cols, expand_grad,
         expand_rows_next, expand_cols_next, expand_next, expand_ref),
    )
    at = 0
    for share, *_ in weights:
        at += share.shape[0] * share.shape[2]
    for which, (
        share, own, square, old_rows, old_cols, grad, next_rows, next_cols, next_w, full
    ) in enumerate(weights):
        n, height, width = share.shape
        all_rows = full.shape[0]
        rate = 0.5 * jnp.maximum(
            jnp.sqrt(
                jnp.sum(square[...], axis=1, keepdims=True) / (full.shape[0] * full.shape[1])
            ),
            0.001,
        )
        row_mean = sums_ref[0:1, at + 128 * which : at + 128 * which + 1] / all_rows
        total = jnp.zeros((height, 1), F32)
        for k in range(n):
            value = share[k].astype(F32)
            grad[:, k * width : (k + 1) * width] = value
            total = total + jnp.sum(value * value + EPS_ONE, axis=1, keepdims=True)
        old = jnp.broadcast_to(old_rows[...].reshape(1, height), (128, height)).T
        by_row = BETA * old + (1.0 - BETA) / (n * width) * total
        next_rows[...] = by_row.T[0:1].reshape(next_rows.shape)
        by_column = BETA * old_cols[...] + (1.0 - BETA) / all_rows * sums_ref[
            0:1, lane : lane + n * width
        ]
        next_cols[...] = by_column
        lane += n * width
        second = by_row[:, 0:1] * (by_column / row_mean)
        own_copies[which].wait()
        next_w[...] = own[...] - rate * grad[...] * lax.rsqrt(second)
    for t in range(BLOCKS - DEPTH, BLOCKS):
        copy(1, jnp.int32(t)).wait()
    for done in empty:
        done.wait()


def pixels_first(x):
    g, i, s, c, k = x.shape
    x = jnp.transpose(x, (0, 1, 3, 2, 4)).reshape(g, i, c, s, k // 128, 128)
    return jnp.transpose(x, (0, 1, 2, 4, 3, 5)).reshape(g, i, c, s * k // 128, 128)


def slots_first(x, slots):
    g, i, c, r, k = x.shape
    x = x.reshape(g, i, c, r // slots, slots, k)
    x = jnp.transpose(x, (0, 1, 2, 4, 3, 5)).reshape(g, i, c, slots, r // slots * k)
    return jnp.transpose(x, (0, 1, 3, 2, 4))


def call(kernel, outs, ins, scratch, collective_id=None, **more):
    params = dict(vmem_limit_bytes=LIMIT)
    if collective_id is not None:
        params.update(collective_id=collective_id, has_side_effects=True)
    smem = [x.ndim == 1 for x in ins]
    specs = dict(
        in_specs=[pl.BlockSpec(memory_space=pltpu.SMEM if s else VMEM) for s in smem],
        out_specs=tuple(pl.BlockSpec(memory_space=VMEM) for _ in outs),
    )
    specs.update(more)
    return pl.pallas_call(
        kernel,
        out_shape=tuple(jax.ShapeDtypeStruct(shape, dtype) for shape, dtype in outs),
        scratch_shapes=scratch,
        compiler_params=pltpu.CompilerParams(**params),
        **specs,
    )(*ins)


def shards(
    n, w, images, upstream, row_counts, w_reduce, w_spatial, w_expand, norm_gain, norm_bias,
    reduce_rows, reduce_cols, spatial_rows, spatial_cols, expand_rows, expand_cols, norm_state,
):
    groups, count, slots, across, outer = images.shape
    inner = w_reduce.shape[1]
    block = slots * count
    tail = BLOCKS * block
    deep = -(-tail // 256) * 256
    number = float(w * count * sum(c * c for c in COLUMNS))
    counts = row_counts.reshape(groups)
    x = pixels_first(images)
    up = pixels_first(upstream)
    params = (norm_gain.reshape(1, -1), norm_bias.reshape(1, -1))
    whole = (BLOCKS, slots, count, inner)
    narrow_sums = reduce_scratch(n, w, 2, inner)
    outer_sums = reduce_scratch(n, w, 2, outer)
    _, halo = halo_rows(count)
    halo_scratch = [VMEM((halo, inner), BF16)] * 4 + [pltpu.SemaphoreType.DMA((4, 3))]
    stage = VMEM((count // 8, slots * outer // 16, 128), F32)
    order = (slots * outer // 16, slots * outer // 16)

    weights = (w_reduce, w_spatial, w_expand)
    full = pl.BlockSpec(memory_space=VMEM)
    smem = pl.BlockSpec(memory_space=pltpu.SMEM)
    far = pl.BlockSpec(memory_space=pl.ANY)
    dma = pltpu.SemaphoreType.DMA
    padded = ((PADDED_BLOCKS * block, inner), BF16)
    compact = ((deep, inner), BF16)
    inner_images = ((inner + 16, outer), F32)
    forward_arrays = [
        ((deep, outer), BF16), (whole, F32), (whole, F32), compact, compact, compact, compact,
        ((tail, outer), BF16), inner_images, (w_expand.shape, F32), *[(v.shape, BF16) for v in weights],
    ]
    (
        rows, conv_one, conv_two, upper, middle, lower, hidden_two, conv_three, one_images, two_three, *rounded,
        stats_one, stats_two, stats_three, hidden_sum, square_one, square_two, square_three,
    ) = call(
        functools.partial(forward_kernel, n, w, number),
        forward_arrays
        + [((2, v), F32) for v in (inner, inner, outer)]
        + [((1, v), F32) for v in (inner, inner, inner, outer)],
        (x, *weights, *params, counts),
        [
            VMEM((RING, *x.shape[1:2], *x.shape[3:]), BF16),
            VMEM((deep, outer), BF16),
            VMEM((4, CHUNK, inner), F32),
            VMEM(w_expand.shape, F32),
            *[VMEM(v.shape, BF16) for v in weights],
            VMEM(whole, F32),
            VMEM(whole, F32),
            *[VMEM(*padded)] * 3,
            VMEM((deep, inner), BF16),
            VMEM((deep, outer), BF16),
            VMEM((inner + 16, deep), BF16),
            VMEM(*inner_images),
            stage,
            stage,
            VMEM(order, BF16),
            *halo_scratch,
            dma((RING,)),
            dma((4,)),
            dma,
            dma((32,)),
        ]
        + narrow_sums
        + narrow_sums
        + outer_sums,
        0,
        in_specs=[far] * 4 + [full, full, smem],
        out_specs=(far,) * 13 + (full,) * 7,
    )
    row_ring = VMEM((DEPTH, block, outer), BF16)
    map_ring = VMEM((DEPTH, *x.shape[1:2], *x.shape[3:]), BF16)
    output, grad_summed, sums_three = call(
        functools.partial(top_kernel, number, inner),
        [(x.shape, BF16), ((tail, outer), BF16), ((2, 8, outer), F32)],
        (conv_three, rows, up, stats_three, *params, counts),
        [
            row_ring,
            row_ring,
            map_ring,
            map_ring,
            row_ring,
            *[stage] * 4,
            VMEM((2, *order), BF16),
            VMEM((2, outer), F32),
            dma((6, DEPTH)),
        ],
        in_specs=[far] * 3 + [full] * 3 + [smem],
        out_specs=(far, far, full),
    )
    blocks = [block_shapes(n, w, *weight.shape) for weight in weights]
    rows_old = [reduce_rows, spatial_rows, expand_rows]
    cols_old = [v.reshape(1, -1) for v in (reduce_cols, spatial_cols, expand_cols)]
    lanes = sum(v.shape[1] for v in weights) + 3 * 128
    scatter = []
    for weight in weights:
        scatter += scatter_scratch(n, w, *weight.shape)
    input_grad, sums, *more = call(
        functools.partial(backward_kernel, n, w, number, [v.shape for v in weights]),
        [((tail, outer), BF16), ((1, lanes), F32)]
        + [((n, v.shape[0] // w, v.shape[1] // n), BF16) for v in weights]
        + [((2, v), F32) for v in (inner, inner, outer)],
        (
            conv_three, grad_summed, hidden_two, rounded[2], conv_two, rounded[1],
            upper, middle, lower, conv_one, rows, rounded[0], one_images, two_three, sums_three, hidden_sum,
            stats_one, stats_two, stats_three, *params, counts, *rows_old,
        ),
        [
            VMEM((deep, outer), BF16),
            VMEM((deep, outer), BF16),
            VMEM(*padded),
            VMEM((3, inner, deep), BF16),
            VMEM(w_expand.shape, BF16),
            VMEM((3, inner, 3 * inner), BF16),
            VMEM(whole, F32),
            VMEM(whole, F32),
            VMEM(whole, F32),
            VMEM((4, outer), F32),
            VMEM((2, inner + 16, 256), F32),
            dma((2,)),
            *halo_scratch,
            dma((32,)),
            *[VMEM(shape, BF16) for which in range(3) for shape in blocks[which]],
        ]
        + scatter
        + [dma((n,))] * 6
        + outer_sums
        + narrow_sums
        + narrow_sums
        + [VMEM((w, 1, lanes), F32), dma((w,)), dma((w,))],
        1,
        in_specs=[far] * 14 + [full] * 7 + [smem] + [full] * 3,
        out_specs=(far,) + (full,) * 7,
    )
    shares, (grads_one, grads_two, grads_three) = more[:3], more[3:]
    heights = [v.shape[0] // w for v in weights]
    slabs = [((h, v.shape[1]), F32) for h, v in zip(heights, weights)]
    vectors = []
    for h, v in zip(heights, weights):
        vectors += [((h,), F32), ((1, v.shape[1]), F32)]
    outs = call(
        functools.partial(final_kernel, w),
        [(x.shape, BF16)] + slabs + vectors + slabs + [(norm_state.shape, F32)] * 3,
        (
            input_grad, sums, *shares, *weights, square_one, square_two, square_three,
            *rows_old, *cols_old, grads_one, grads_two, grads_three, *params, norm_state,
        ),
        [
            row_ring,
            map_ring,
            VMEM((*x.shape[1:2], *x.shape[3:]), BF16),
            VMEM(order, BF16),
            *[VMEM(shape, dtype) for shape, dtype in slabs],
            dma((16,)),
            dma((2, DEPTH)),
        ],
        in_specs=[far] + [full] * 4 + [far] * 3 + [full] * 15,
        out_specs=(far,) + (full,) * 15,
    )
    input_grad, *outs = outs
    for k in range(3, 9):
        outs[k] = outs[k].reshape(-1)
    return (slots_first(output, slots), slots_first(input_grad, slots), *outs)


def solution(mesh):
    maps = P(None, "wide", "narrow", None, None)
    in_specs = (
        maps, maps, P(None, "wide", "narrow"), P(), P(), P(), P(), P(),
        P("wide"), P(), P("wide"), P(), P("wide"), P(), P(),
    )
    out_specs = (
        maps, maps, P("wide", None), P("wide", None), P("wide", None),
        P("wide"), P(), P("wide"), P(), P("wide"), P(),
        P("wide", None), P("wide", None), P("wide", None), P(), P(), P(),
    )
    return jax.shard_map(
        functools.partial(shards, mesh.shape["narrow"], mesh.shape["wide"]),
        mesh=mesh,
        in_specs=in_specs,
        out_specs=out_specs,
        check_vma=False,
    )
```

```python
import functools

import jax
import jax.numpy as jnp
from jax import lax
from jax.experimental import pallas as pl
from jax.experimental.pallas import tpu as pltpu
from jax.sharding import PartitionSpec as P

MESH = pl.DeviceIdType.MESH
VMEM = pltpu.VMEM
F32 = jnp.float32
BF16 = jnp.bfloat16

STEP = 10
EPS = 1e-05
EPS_ONE = 1e-30
LIMIT = 63 * 1024 * 1024

COLUMNS = (5, 6, 7)
FIRST = (0, 5, 11)
PADDED = (1, 7, 14)
BLOCKS = 18
PADDED_BLOCKS = 22

C0 = 0.7978845608
C1 = C0 * 0.044715


def half_of(v):
    squared = v * v
    return 0.5 + 0.5 * jnp.tanh(v * (C0 + C1 * squared)), squared


def slope_of(v, h, squared):
    return h + v * h * (1.0 - h) * (2.0 * C0 + 6.0 * C1 * squared)


def dot(a, b):
    return jnp.dot(a, b, preferred_element_type=F32)


def dot_t(a, b):
    return lax.dot_general(a, b, (((1,), (1,)), ((), ())), preferred_element_type=F32)


def turned_in(load, count, group):
    pieces = [
        jnp.transpose(load(k)[:, 8 * group : 8 * group + 8].astype(F32), (1, 0, 2))
        for k in range(count)
    ]
    return [
        jnp.concatenate([piece[2 * c + slot] for slot in range(2) for piece in pieces], axis=0)
        for c in range(4)
    ]


def turned_out(blocks, k):
    images = blocks[0].shape[0] // 2
    rows = [
        block[slot * images + 8 * k : slot * images + 8 * k + 8]
        for block in blocks
        for slot in range(2)
    ]
    halves = [jnp.transpose(jnp.stack(rows[at : at + 8]), (1, 0, 2)) for at in (0, 8)]
    return jnp.concatenate(halves, axis=1)


def cast_rows(value_ref, wb_ref, row, square):
    step = 64

    def add(k, square):
        value = value_ref[pl.ds(pl.multiple_of(k * step, step), step), :]
        wb_ref[pl.ds(pl.multiple_of(row + k * step, step), step), :] = value.astype(BF16)
        return square + jnp.sum((value * value).reshape(step // 8, 8, value.shape[1]), axis=0)

    return lax.fori_loop(0, value_ref.shape[0] // step, add, square)


def reduce_scratch(n, w, rows, channels):
    return [
        VMEM((n, rows, channels), F32),
        VMEM((w, rows, channels), F32),
        pltpu.SemaphoreType.DMA((n,)),
        pltpu.SemaphoreType.DMA((n,)),
        pltpu.SemaphoreType.DMA((w,)),
        pltpu.SemaphoreType.DMA((w,)),
    ]


def greet(n, w):
    me_n, me_w = lax.axis_index("narrow"), lax.axis_index("wide")
    barrier = pltpu.get_barrier_semaphore()
    for k in range(1, n):
        pl.semaphore_signal(
            barrier, inc=1, device_id={"narrow": lax.rem(me_n + k, n)}, device_id_type=MESH
        )
    for k in range(1, w):
        pl.semaphore_signal(
            barrier, inc=1, device_id={"wide": lax.rem(me_w + k, w)}, device_id_type=MESH
        )


def met(n, w):
    pl.semaphore_wait(pltpu.get_barrier_semaphore(), n + w - 2)


def sum_over(axis, size, value, slots, send, recv):
    me = lax.axis_index(axis)
    slots[me] = value
    copies = []
    for k in range(1, size):
        copy = pltpu.make_async_remote_copy(
            src_ref=slots.at[me],
            dst_ref=slots.at[me],
            send_sem=send.at[k],
            recv_sem=recv.at[k],
            device_id={axis: lax.rem(me + k, size)},
            device_id_type=MESH,
        )
        copy.start()
        copies.append(copy)
    for copy in copies:
        copy.wait_recv()
    total = slots[0]
    for k in range(1, size):
        total = total + slots[k]
    for copy in copies:
        copy.wait_send()
    return total


class SumAll:
    def __init__(self, n, w, scratch):
        self.axes = (("narrow", n, scratch[0], *scratch[2:4]), ("wide", w, scratch[1], *scratch[4:6]))
        self.copies = [[], []]

    def send(self, which, value):
        axis, size, slots, send, recv = self.axes[which]
        me = lax.axis_index(axis)
        slots[me] = value
        for k in range(1, size):
            copy = pltpu.make_async_remote_copy(
                src_ref=slots.at[me],
                dst_ref=slots.at[me],
                send_sem=send.at[k],
                recv_sem=recv.at[k],
                device_id={axis: lax.rem(me + k, size)},
                device_id_type=MESH,
            )
            copy.start()
            self.copies[which].append(copy)

    def total(self, which):
        _, size, slots, _, _ = self.axes[which]
        for copy in self.copies[which]:
            copy.wait_recv()
        total = slots[0]
        for k in range(1, size):
            total = total + slots[k]
        return total

    def begin(self, value):
        self.send(0, value)

    def middle(self):
        self.send(1, self.total(0))

    def end(self):
        total = self.total(1)
        for copies in self.copies:
            for copy in copies:
                copy.wait_send()
        return total


def forward_scale(stats, params, number):
    mean = stats[0:1] / number
    scale = lax.rsqrt(stats[1:2] / number - mean * mean + EPS)
    a = scale * params[0]
    return a, params[1] - mean * a, scale, mean


def backward_scale(stats, params, grads, number):
    mean = stats[0:1] / number
    scale = lax.rsqrt(stats[1:2] / number - mean * mean + EPS)
    a = scale * params[0]
    gain_grad, bias_grad = grads[0:1], grads[1:2]
    over = a / number
    return a, over * scale * gain_grad, over * (bias_grad - mean * scale * gain_grad)


def norm_params(gain_ref, bias_ref, which, inner):
    lane = (0, inner, 2 * inner, gain_ref.shape[1])
    at = slice(lane[which], lane[which + 1])
    return gain_ref[0:1, at], bias_ref[0:1, at]


def second_counts(counts_ref, g):
    return jnp.where(counts_ref[g] == 2, 1.0, 0.0)


def two_sums(first, second, m):
    return jnp.sum(first, axis=(0, 1))[None] + m * jnp.sum(second, axis=(0, 1))[None]


def padded_rows(count):
    return -(-count // 16) * 16


def halo_rows(images):
    starts, at = [], 0
    for g in range(3):
        starts.append(at)
        at += padded_rows(COLUMNS[g] * images)
    return starts, at


def pack_halo(value):
    count = value.shape[0] * value.shape[1]
    value = value.reshape(count, value.shape[2])
    extra = padded_rows(count) - count
    if extra:
        value = jnp.concatenate([value, jnp.zeros((extra, value.shape[1]), F32)], axis=0)
    return value.astype(BF16)


def unpack_halo(value, columns, images):
    return value.astype(F32)[: columns * images].reshape(columns, images, value.shape[1])


def halo_copies(n, g, count, starts, up_src, up_dst, down_src, down_dst, sems):
    me = lax.axis_index("narrow")
    rows = pl.ds(starts[g], count)
    forward = pltpu.make_async_remote_copy(
        src_ref=up_src.at[rows],
        dst_ref=up_dst.at[rows],
        send_sem=sems.at[0, g],
        recv_sem=sems.at[1, g],
        device_id={"narrow": lax.rem(me + 1, n)},
        device_id_type=MESH,
    )
    backward = pltpu.make_async_remote_copy(
        src_ref=down_src.at[rows],
        dst_ref=down_dst.at[rows],
        send_sem=sems.at[2, g],
        recv_sem=sems.at[3, g],
        device_id={"narrow": lax.rem(me + n - 1, n)},
        device_id_type=MESH,
    )
    return forward, backward


def halo_start(n, copies):
    me = lax.axis_index("narrow")

    @pl.when(me < n - 1)
    def _():
        copies[0].start()

    @pl.when(me > 0)
    def _():
        copies[1].start()


def halo_arrived(n, copies):
    me = lax.axis_index("narrow")

    @pl.when(me > 0)
    def _():
        copies[0].wait_recv()

    @pl.when(me < n - 1)
    def _():
        copies[1].wait_recv()


def halo_sent(n, copies):
    me = lax.axis_index("narrow")

    @pl.when(me < n - 1)
    def _():
        copies[0].wait_send()

    @pl.when(me > 0)
    def _():
        copies[1].wait_send()


def halo_edges(n, from_before, from_after):
    me = lax.axis_index("narrow")

    @pl.when(me == 0)
    def _():
        from_before[...] = jnp.zeros(from_before.shape, from_before.dtype)

    @pl.when(me == n - 1)
    def _():
        from_after[...] = jnp.zeros(from_after.shape, from_after.dtype)


RING = 6
CHUNK = 512


def turn(source, columns, target):
    for k in range(source.shape[0] // 128):
        target[:, k * 128 : (k + 1) * 128] = source[k * 128 : (k + 1) * 128, columns].T


def place_of(t):
    g = (t >= FIRST[1]).astype(jnp.int32) + (t >= FIRST[2]).astype(jnp.int32)
    return g, t - jnp.where(g == 0, FIRST[0], jnp.where(g == 1, FIRST[1], FIRST[2]))


def forward_kernel(
    n, w, number, x_ref, reduce_ref, spatial_ref, expand_ref, gain_ref, bias_ref, counts_ref,
    rows_out, one_out, two_out, upper_out, middle_out, lower_out, hidden_out, three_out, inner_out, outer_out,
    reduce_out, spatial_out, expand_out,
    stat_one, stat_two, stat_three, hidden_sum, square_reduce, square_spatial, square_expand,
    ring, rows, weight, wide_weight, reduce, spatial, expand, one, two, upper, middle, lower, hidden, three,
    turned, inner,
    last, first, above, below, halo_sems, ring_sems, weight_sems, wide_sem, out_sems,
    *scratch,
):
    m = [second_counts(counts_ref, g) for g in range(3)]
    sum_one = SumAll(n, w, scratch[:6])
    sum_two = SumAll(n, w, scratch[6:12])
    sum_three = SumAll(n, w, scratch[12:18])
    images = x_ref.shape[1]
    lanes = x_ref.shape[3] // 2
    channels = one.shape[3]
    block = 2 * images
    tail = BLOCKS * block
    starts, _ = halo_rows(images)
    outs = []

    def put(source, target):
        copy = pltpu.make_async_copy(source, target, out_sems.at[len(outs)])
        copy.start()
        outs.append(copy)

    def fetch(t):
        g, j = place_of(t)
        slot = lax.rem(t, RING)
        return pltpu.make_async_copy(x_ref.at[g, :, j], ring.at[slot], ring_sems.at[slot])

    sources = [reduce_ref.at[k : k + CHUNK] for k in range(0, reduce_ref.shape[0], CHUNK)]
    reduce_chunks = len(sources)
    sources += [spatial_ref.at[k : k + CHUNK] for k in range(0, spatial_ref.shape[0], CHUNK)]
    slots = weight.shape[0]

    def weight_copy(k):
        return pltpu.make_async_copy(sources[k], weight.at[k % slots], weight_sems.at[k % slots])

    for t in range(RING):
        fetch(jnp.int32(t)).start()
    for k in range(slots):
        weight_copy(k).start()
    wide_copy = pltpu.make_async_copy(expand_ref, wide_weight, wide_sem)
    wide_copy.start()
    greet(n, w)
    rows[tail:, :] = jnp.zeros((rows.shape[0] - tail, rows.shape[1]), BF16)
    three[tail:, :] = jnp.zeros((three.shape[0] - tail, three.shape[1]), BF16)
    for ref in (upper, middle, lower):
        for at in (0, PADDED[1] - 1, PADDED[2] - 1, PADDED_BLOCKS - 1):
            ref[at * block : (at + 1) * block] = jnp.zeros((block, channels), BF16)
    halo_edges(n, above, below)

    def cast_chunk(k, wb_ref, row, square):
        weight_copy(k).wait()
        square = cast_rows(weight.at[k % slots], wb_ref, row, square)
        if k + slots < len(sources):
            weight_copy(k + slots).start()
        return square

    def place(i, _):
        for k in range(2):
            fetch(2 * i + k).wait()
        for k in range(2):
            slot = lax.rem(2 * i + k, RING)
            row = pl.multiple_of((2 * i + k) * block, block)
            for group in range(lanes // 4):
                values = turned_in(lambda j: ring[slot, 8 * j : 8 * j + 8], images // 8, group)
                for c in range(4):
                    at = (4 * group + c) * 128
                    rows[pl.ds(row, block), at : at + 128] = values[c].astype(BF16)

        @pl.when(2 * i + RING < BLOCKS)
        def _():
            for k in range(2):
                fetch(2 * i + k + RING).start()

        return 0

    lax.fori_loop(0, BLOCKS // 2, place, 0)
    put(rows, rows_out)
    square = jnp.zeros((8, channels), F32)
    for k in range(reduce_chunks):
        square = cast_chunk(k, reduce, k * CHUNK, square)
    square_reduce[...] = jnp.sum(square, axis=0, keepdims=True)
    put(reduce, reduce_out)
    sums = jnp.zeros((1, channels), F32)
    squares = jnp.zeros((1, channels), F32)
    for g in range(3):
        at = slice(FIRST[g] * block, (FIRST[g] + COLUMNS[g]) * block)
        c = dot(rows[at, :], reduce[...]).reshape(COLUMNS[g], 2, images, channels)
        one[FIRST[g] : FIRST[g] + COLUMNS[g]] = c
        sums = sums + two_sums(c[:, 0], c[:, 1], m[g])
        squares = squares + two_sums(c[:, 0] * c[:, 0], c[:, 1] * c[:, 1], m[g])
    met(n, w)
    sum_one.begin(jnp.concatenate([sums, squares], axis=0))
    put(one, one_out)
    square = jnp.zeros((8, channels), F32)
    middle_chunk = (reduce_chunks + len(sources)) // 2
    for k in range(reduce_chunks, middle_chunk):
        square = cast_chunk(k, spatial, (k - reduce_chunks) * CHUNK, square)
    for g in range(3):
        value = one[FIRST[g] : FIRST[g] + COLUMNS[g]]
        value = jnp.stack([value[:, 0], value[:, 1] * m[g]], axis=1)
        hidden[FIRST[g] * block : (FIRST[g] + COLUMNS[g]) * block] = value.reshape(
            COLUMNS[g] * block, channels
        ).astype(BF16)
    hidden[tail:] = jnp.zeros((hidden.shape[0] - tail, channels), BF16)
    sum_one.middle()
    turn(hidden, slice(0, channels), turned.at[:channels])
    lane = lax.broadcasted_iota(jnp.int32, (16, turned.shape[1]), 1)
    place = lax.div(lane, block)
    flag = jnp.where(place < FIRST[1], m[0], jnp.where(place < FIRST[2], m[1], m[2]))
    flag = jnp.where(lax.rem(lane, block) < images, 1.0, flag)
    turned[channels:] = jnp.where(lane < tail, flag, 0.0).astype(BF16)

    def inner_chunk(k):
        at = slice(k * 256, (k + 1) * 256)
        inner[:, at] = dot(turned[...], rows[:, at])

    inner_chunks = rows.shape[1] // 256
    for k in range(middle_chunk, len(sources)):
        square = cast_chunk(k, spatial, (k - reduce_chunks) * CHUNK, square)
    for k in range(inner_chunks // 4):
        inner_chunk(k)
    square_spatial[...] = jnp.sum(square, axis=0, keepdims=True)
    put(spatial, spatial_out)
    stats = sum_one.end()
    stat_one[...] = stats

    a, b, _, _ = forward_scale(stats, norm_params(gain_ref, bias_ref, 0, channels), number)
    copies = []
    for g in range(3):
        v = one[FIRST[g] : FIRST[g] + COLUMNS[g]] * a + b
        value = v * half_of(v)[0]
        slot_one, slot_two = value[:, 0], value[:, 1] * m[g]
        count = padded_rows(COLUMNS[g] * images)
        first[starts[g] : starts[g] + count] = pack_halo(slot_one)
        last[starts[g] : starts[g] + count] = pack_halo(
            jnp.where(m[g] > 0.5, slot_two, slot_one)
        )
        copies.append(halo_copies(n, g, count, starts, last, above, first, below, halo_sems))
        halo_start(n, copies[g])
        both = jnp.stack([slot_one, slot_two], axis=1).reshape(COLUMNS[g] * block, channels)
        middle[PADDED[g] * block : (PADDED[g] + COLUMNS[g]) * block] = both.astype(BF16)

    def taps(ref, g, level):
        at, count = PADDED[g] * block, COLUMNS[g] * block
        shifted = [ref[at + d * block : at + d * block + count, :] for d in (-1, 0, 1)]
        return dot(
            jnp.concatenate(shifted, axis=1),
            spatial[3 * level * channels : 3 * (level + 1) * channels, :],
        )

    def put_groups(source, target):
        for g in range(3):
            count = COLUMNS[g] * block
            put(
                source.at[PADDED[g] * block : PADDED[g] * block + count],
                target.at[FIRST[g] * block : FIRST[g] * block + count],
            )

    for g in range(3):
        two[FIRST[g] : FIRST[g] + COLUMNS[g]] = taps(middle, g, 1).reshape(
            COLUMNS[g], 2, images, channels
        )
    put_groups(middle, middle_out)
    sums = jnp.zeros((1, channels), F32)
    squares = jnp.zeros((1, channels), F32)
    for g in range(3):
        halo_arrived(n, copies[g])
        at, count = PADDED[g] * block, COLUMNS[g] * block
        height = padded_rows(COLUMNS[g] * images)
        up = unpack_halo(above[starts[g] : starts[g] + height], COLUMNS[g], images)
        down = unpack_halo(below[starts[g] : starts[g] + height], COLUMNS[g], images)
        own = middle[at : at + count].astype(F32).reshape(COLUMNS[g], 2, images, channels)
        upper[at : at + count] = (
            jnp.stack([up, own[:, 0]], axis=1).reshape(count, channels).astype(BF16)
        )
        lower[at : at + count] = (
            jnp.stack([jnp.where(m[g] > 0.5, own[:, 1], down), down], axis=1)
            .reshape(count, channels)
            .astype(BF16)
        )
        c = taps(upper, g, 0) + taps(lower, g, 2)
        c = c.reshape(COLUMNS[g], 2, images, channels) + two[FIRST[g] : FIRST[g] + COLUMNS[g]]
        two[FIRST[g] : FIRST[g] + COLUMNS[g]] = c
        sums = sums + two_sums(c[:, 0], c[:, 1], m[g])
        squares = squares + two_sums(c[:, 0] * c[:, 0], c[:, 1] * c[:, 1], m[g])
    sum_two.begin(jnp.concatenate([sums, squares], axis=0))
    put(two, two_out)
    put_groups(upper, upper_out)
    put_groups(lower, lower_out)
    wide_copy.wait()
    half = wide_weight.shape[0] // 2
    square = jnp.zeros((8, wide_weight.shape[1]), F32)
    square = cast_rows(wide_weight.at[:half], expand, 0, square)
    for k in range(inner_chunks // 4, inner_chunks // 2):
        inner_chunk(k)
    sum_two.middle()
    square = cast_rows(wide_weight.at[half:], expand, half, square)
    square_expand[...] = jnp.sum(square, axis=0, keepdims=True)
    put(expand, expand_out)
    for k in range(inner_chunks // 2, inner_chunks):
        inner_chunk(k)
    put(inner, inner_out)
    inner_done = outs[-1]
    for g in range(3):
        halo_sent(n, copies[g])
    stats = sum_two.end()
    stat_two[...] = stats

    a, b, _, _ = forward_scale(stats, norm_params(gain_ref, bias_ref, 1, channels), number)
    sums = jnp.zeros((1, channels), F32)
    for g in range(3):
        v = two[FIRST[g] : FIRST[g] + COLUMNS[g]] * a + b
        value = v * half_of(v)[0]
        both = jnp.stack([value[:, 0], value[:, 1] * m[g]], axis=1)
        sums = sums + jnp.sum(both, axis=(0, 1, 2))[None]
        hidden[FIRST[g] * block : (FIRST[g] + COLUMNS[g]) * block] = both.reshape(
            COLUMNS[g] * block, channels
        ).astype(BF16)
    hidden_sum[...] = sums
    put(hidden.at[:tail], hidden_out.at[:tail])
    sums, squares = [], []
    for part in range(three.shape[1] // 512):
        s = jnp.zeros((1, 512), F32)
        q = jnp.zeros((1, 512), F32)
        columns = slice(part * 512, (part + 1) * 512)
        for g in range(3):
            at = slice(FIRST[g] * block, (FIRST[g] + COLUMNS[g]) * block)
            c = dot(hidden[at, :], expand[:, columns])
            three[at, columns] = c.astype(BF16)
            s = s + jnp.sum(c, axis=0, keepdims=True)
            q = q + jnp.sum(c * c, axis=0, keepdims=True)
        put(three.at[:tail, columns], three_out.at[:, columns])
        sums.append(s)
        squares.append(q)
    sum_three.begin(
        jnp.concatenate(
            [jnp.concatenate(sums, axis=1), jnp.concatenate(squares, axis=1)], axis=0
        )
    )
    turn(hidden, slice(0, channels), turned.at[:channels])
    inner_done.wait()
    outs = [copy for copy in outs if copy is not inner_done]

    def outer_chunk(k):
        at = slice(k * 256, (k + 1) * 256)
        inner[:channels, at] = dot(turned[:channels], three[:, at])

    for k in range(inner_chunks // 4):
        outer_chunk(k)
    sum_three.middle()
    for k in range(inner_chunks // 4, inner_chunks):
        outer_chunk(k)
    put_last = pltpu.make_async_copy(inner.at[:channels], outer_out, out_sems.at[31])
    put_last.start()
    stat_three[...] = sum_three.end()
    for copy in outs:
        copy.wait()
    put_last.wait()


DEPTH = 4


def top_kernel(
    number, inner, conv_ref, rows_ref, up_ref, stats_ref, gain_ref, bias_ref, counts_ref,
    out_ref, grad_ref, total,
    conv_ring, rows_ring, up_ring, out_ring, grad_ring, up_one, up_two, out_one, out_two, coefficients, sems,
):
    images = up_ref.shape[1]
    lanes = up_ref.shape[3] // 2
    block = 2 * images

    def rows_of(t):
        return pl.ds(pl.multiple_of(t * block, block), block)

    def copy(which, t):
        slot = lax.rem(t, DEPTH)
        g, j = place_of(t)
        source, target = (
            lambda: (conv_ref.at[rows_of(t)], conv_ring.at[slot]),
            lambda: (rows_ref.at[rows_of(t)], rows_ring.at[slot]),
            lambda: (up_ref.at[g, :, j], up_ring.at[slot]),
            lambda: (out_ring.at[slot], out_ref.at[g, :, j]),
            lambda: (grad_ring.at[slot], grad_ref.at[rows_of(t)]),
        )[which]()
        return pltpu.make_async_copy(source, target, sems.at[which, slot])

    def each(which, t, do):
        @pl.when((t >= 0) & (t < BLOCKS))
        def _():
            do(copy(which, t))

    def start(which, t):
        each(which, t, lambda c: c.start())

    def wait(which, t):
        each(which, t, lambda c: c.wait())

    for t in range(3):
        start(2, jnp.int32(t))
        if t < 2:
            start(0, jnp.int32(t))
            start(1, jnp.int32(t))
    total[...] = jnp.zeros(total.shape, F32)
    params = norm_params(gain_ref, bias_ref, 2, inner)
    a, b, scale, mean = forward_scale(stats_ref[...], params, number)
    coefficients[0:1] = a
    coefficients[1:2] = b
    out_two[...] = jnp.zeros(out_two.shape, F32)

    def enter(t, stage):
        slot = lax.rem(t, DEPTH)
        for group in range(lanes // 4):
            values = turned_in(lambda j: up_ring[slot, 8 * j : 8 * j + 8], images // 8, group)
            for c in range(4):
                stage[4 * group + c] = values[c]

    def leave(t, stage):
        slot = lax.rem(t + DEPTH, DEPTH)
        for group in range(lanes // 8):
            blocks = [stage[8 * group + c] for c in range(8)]
            for k in range(images // 8):
                out_ring[slot, 8 * k : 8 * k + 8, 16 * group : 16 * group + 16] = turned_out(
                    blocks, k
                ).astype(BF16)

    def work(t, stage_up, stage_out):
        slot = lax.rem(t, DEPTH)
        m = second_counts(counts_ref, place_of(t)[0])
        for c in range(lanes):
            at = slice(c * 128, (c + 1) * 128)
            raw = conv_ring[slot, :, at].astype(F32)
            v = raw * coefficients[0:1, at] + coefficients[1:2, at]
            v = v + rows_ring[slot, :, at].astype(F32)
            h, squared = half_of(v)
            out = v * h
            slope = h + out * (1.0 - h) * (2.0 * C0 + 6.0 * C1 * squared)
            stage_out[c, :images] = out[:images]
            stage_out[c, images:] = out[images:] * m
            up = stage_up[c]
            grad = jnp.concatenate(
                [slope[:images] * up[:images], slope[images:] * (up[images:] * m)], axis=0
            )
            grad_ring[slot, :, at] = grad.astype(BF16)
            total[0, :, at] += jnp.sum((grad * raw).reshape(block // 8, 8, 128), axis=0)
            total[1, :, at] += jnp.sum(grad.reshape(block // 8, 8, 128), axis=0)

    wait(2, jnp.int32(0))
    enter(jnp.int32(0), up_one)

    def pair(i, _):
        t = 2 * i
        for k in (2, 3):
            start(0, t + k)
            start(1, t + k)
            start(2, t + k + 1)
        for k in (0, 1):
            wait(0, t + k)
            wait(1, t + k)
            wait(2, t + k + 1)
            wait(3, t + k - 1 - DEPTH)
            wait(4, t + k - DEPTH)
        enter(t + 1, up_two)
        work(t, up_one, out_one)
        leave(t - 1, out_two)
        enter(t + 2, up_one)
        work(t + 1, up_two, out_two)
        leave(t, out_one)
        for k in (0, 1):
            start(3, t + k - 1)
            start(4, t + k)
        return 0

    lax.fori_loop(0, BLOCKS // 2, pair, 0)
    last = jnp.int32(BLOCKS - 1)
    wait(3, last - DEPTH)
    leave(last, out_two)
    start(3, last)
    for k in range(DEPTH):
        wait(3, last - k)
        wait(4, last - k)
    out_ring[0] = jnp.zeros(out_ring.shape[1:], BF16)
    copies = []
    for g in range(3):
        for j in range(COLUMNS[g], out_ref.shape[2]):
            copies.append(
                pltpu.make_async_copy(
                    out_ring.at[0], out_ref.at[g, :, j], sems.at[5, len(copies)]
                )
            )
            copies[-1].start()
    value = jnp.sum(total[...], axis=1)
    gains = scale * (value[0:1] - mean * value[1:2])
    total[0] = jnp.concatenate([gains, jnp.zeros((7, gains.shape[1]), F32)], axis=0)
    for copy in copies:
        copy.wait()


def unravel(index, sizes):
    digits = []
    for size in reversed(sizes):
        digits.append(index % size if isinstance(index, int) else lax.rem(index, size))
        index = index // size if isinstance(index, int) else lax.div(index, size)
    return digits[::-1]


def mesh_digits(n, w):
    if (n, w) == (4, 8):
        return (
            [("narrow", 2, 2), ("narrow", 1, 2), ("wide", 2, 4), ("wide", 1, 2)],
            [(1, 3, 0, 2), (1, 0, 3, 2)],
        )
    return [("narrow", 1, n), ("wide", 1, w)], [(0, 1), (0, 1)]


def digit_sizes(n, w):
    return [d[2] for d in mesh_digits(n, w)[0]]


def narrow_digits(n, w):
    return [d[2] for d in mesh_digits(n, w)[0] if d[0] == "narrow"]


def wide_digits(n, w):
    return [d[2] for d in mesh_digits(n, w)[0] if d[0] == "wide"]


def weight_parts(w, rows):
    share = rows // w
    if rows >= 4096 and share % 64 == 0:
        return 4
    return 2 if share % 32 == 0 else 1


def block_shapes(n, w, rows, columns):
    parts = weight_parts(w, rows)
    return [(*digit_sizes(n, w), rows // w // parts, columns // n)] * parts


def put_blocks(n, w, refs, value, row, rows, place_n=None, place_w=0, lane=0):
    share = rows // w
    part = share // len(refs)
    at, end = row, row + value.shape[0]
    columns = refs[0].shape[-1]
    while at < end:
        stop = min(end, (at // part + 1) * part)
        wide = at // share
        ref = refs[at // part % len(refs)]
        inside = slice(at % part, at % part + stop - at)
        piece = value[at - row : stop - row]
        wide = unravel(place_w + wide, wide_digits(n, w))
        if place_n is not None:
            lanes = slice(lane, lane + piece.shape[1])
            ref[(*unravel(place_n, narrow_digits(n, w)), *wide, inside, lanes)] = piece.astype(BF16)
        else:
            for k in range(n):
                ref[(*unravel(k, narrow_digits(n, w)), *wide, inside, slice(None))] = piece[
                    :, k * columns : (k + 1) * columns
                ].astype(BF16)
        at = stop


def scatter_scratch(n, w, rows, columns):
    digits, orders = mesh_digits(n, w)
    scratch = []
    for part, shape in enumerate(block_shapes(n, w, rows, columns)):
        left = list(range(len(digits)))
        for d in orders[part % 2]:
            left.remove(d)
            size = digits[d][2]
            scratch.append(VMEM((size - 1, *(digits[k][2] for k in left), *shape[-2:]), BF16))
            scratch.append(pltpu.SemaphoreType.DMA((size - 1,)))
            scratch.append(pltpu.SemaphoreType.DMA((size - 1,)))
    return scratch


class Scatter:
    def __init__(self, n, w, source, scratch, order):
        self.digits = mesh_digits(n, w)[0]
        self.order = order
        self.scratch = scratch
        self.sources = [source] + [scratch[3 * k].at[0] for k in range(len(order))]
        self.copies = []
        self.steps = len(order)

    def own(self, d):
        axis, stride, size = self.digits[d]
        return lax.rem(lax.div(lax.axis_index(axis), stride), size)

    def pick(self, ref, step, value):
        left = [d for d in range(len(self.digits)) if d not in self.order[:step]]
        return ref.at[tuple(value if d == self.order[step] else slice(None) for d in left)]

    def start(self, step):
        d = self.order[step]
        axis, stride, size = self.digits[d]
        landing, send, recv = self.scratch[3 * step : 3 * step + 3]
        mine = self.own(d)
        for k in range(1, size):
            other = lax.rem(mine + k, size)
            copy = pltpu.make_async_remote_copy(
                src_ref=self.pick(self.sources[step], step, other),
                dst_ref=landing.at[k - 1],
                send_sem=send.at[k - 1],
                recv_sem=recv.at[k - 1],
                device_id={axis: lax.axis_index(axis) + (other - mine) * stride},
                device_id_type=MESH,
            )
            copy.start()
            self.copies.append((step, copy))

    def finish(self, step):
        for at, copy in self.copies:
            if at == step:
                copy.wait_recv()
        d = self.order[step]
        size = self.digits[d][2]
        landing = self.scratch[3 * step]
        left = [k for k in range(len(self.digits)) if k not in self.order[: step + 1]]
        sizes = [self.digits[k][2] for k in left]
        mine = self.own(d)
        source = self.pick(self.sources[step], step, mine)

        def total(at):
            value = source[at].astype(F32)
            for k in range(size - 1):
                value = value + landing[(k, *at)].astype(F32)
            return value

        if step == self.steps - 1:
            return total((slice(None), slice(None)))
        count = 1
        for k in sizes:
            count *= k

        together = 4 if count % 4 == 0 else 1

        def add(index, _):
            for k in range(together):
                at = tuple(unravel(index * together + k, sizes))
                landing[(0, *at)] = total(at).astype(BF16)
            return 0

        lax.fori_loop(0, count // together, add, 0)

    def done(self):
        for _, copy in self.copies:
            copy.wait_send()


def share_out(n, slots, value, send, recv):
    me = lax.axis_index("narrow")
    row = 0
    for piece in value:
        slots[me, row : row + piece.shape[0]] = piece.astype(BF16)
        row += piece.shape[0]
    copies = []
    for k in range(1, n):
        copy = pltpu.make_async_remote_copy(
            src_ref=slots.at[me],
            dst_ref=slots.at[me],
            send_sem=send.at[k],
            recv_sem=recv.at[k],
            device_id={"narrow": lax.rem(me + k, n)},
            device_id_type=MESH,
        )
        copy.start()
        copies.append(copy)
    return copies


BETA = 1.0 - STEP ** (-0.8)


class Refs:
    def __init__(self, refs):
        self.refs = list(refs)

    def take(self, count):
        taken, self.refs = self.refs[:count], self.refs[count:]
        return taken

    def one(self):
        return self.take(1)[0]


def backward_kernel(
    n, w, number, shapes, three_ref, grad_ref, hidden_ref, expand_ref, two_ref, spatial_ref,
    upper_ref, middle_ref, lower_ref, one_ref, rows_ref, reduce_ref, inner_ref, outer_ref, sums_ref, hidden_sum, stat_one, stat_two, stat_three,
    gain_ref, bias_ref, counts_ref, reduce_rows_ref, spatial_rows_ref, expand_rows_ref, *refs,
):
    refs = Refs(refs)
    parts = [weight_parts(w, shape[0]) for shape in shapes]
    input_ref, columns_ref = refs.take(2)
    shares = refs.take(3)
    norm_one, norm_two, norm_three = refs.take(3)
    three, wide, hidden, turned, expand, spatial, two, one, u, coefficients = refs.take(10)
    inner_ring, inner_sems = refs.take(2)
    to_before, to_after, from_after, from_before, halo_sems, in_sems = refs.take(6)
    gradients = [refs.take(parts[k]) for k in range(3)]
    orders = mesh_digits(n, w)[1]
    steps = len(orders[0])
    scatters = [
        [
            Scatter(n, w, gradients[k][p], refs.take(3 * steps), orders[p % 2])
            for p in range(parts[k])
        ]
        for k in range(3)
    ]
    share_sems = [refs.take(2) for _ in range(3)]
    sum_three = SumAll(n, w, refs.take(6))
    sum_two = SumAll(n, w, refs.take(6))
    sum_one = SumAll(n, w, refs.take(6))
    column_scratch = refs.take(3)

    images = two.shape[2]
    channels = two.shape[3]
    block = 2 * images
    tail = BLOCKS * block
    deep = three.shape[0]
    m = [second_counts(counts_ref, g) for g in range(3)]
    starts, _ = halo_rows(images)

    ins = {}

    def get(name, source, target):
        ins[name] = pltpu.make_async_copy(source, target, in_sems.at[len(ins)])
        ins[name].start()

    get("hidden", hidden_ref.at[:tail], hidden.at[:tail])
    get("three", three_ref, three.at[:tail])
    get("grad", grad_ref, wide.at[:tail])
    get("expand", expand_ref, expand)
    get("two", two_ref, two)
    get("one", one_ref, one)
    greet(n, w)

    def norm_scale(which, stat, grads):
        params = norm_params(gain_ref, bias_ref, which, channels)
        return backward_scale(stat[...], params, grads, number)

    sent = {}

    def advance(which, step, half=None):
        if step >= steps:
            return
        count = parts[which]
        if half is not None and count == 1:
            if half == 0:
                return
            half = None
        first = 0 if half is None else half * (count // 2)
        last = count if half is None else first + count // 2
        for scatter in scatters[which][first:last]:
            value = scatter.finish(step)
            if step < steps - 1:
                scatter.start(step + 1)
            else:
                sent.setdefault(which, []).append(value)
        if step == steps - 1 and last == count:
            sent[which] = share_out(n, shares[which], sent[which], *share_sems[which])

    def launch(which):
        for scatter in scatters[which]:
            scatter.start(0)

    value = jnp.concatenate(
        [sums_ref[0, 0:1], jnp.sum(sums_ref[1], axis=0, keepdims=True)],
        axis=0,
    )
    halo_edges(n, from_before, from_after)
    wide[tail:, :] = jnp.zeros((deep - tail, wide.shape[1]), BF16)
    hidden[tail:deep] = jnp.zeros((deep - tail, channels), BF16)
    met(n, w)
    sum_three.begin(value)
    ins["hidden"].wait()
    turn(hidden.at[:deep], slice(0, channels), turned.at[0])
    ins["grad"].wait()

    def held(k):
        return (k // 6, slice(None), slice(k % 6 * 256, (k % 6 + 1) * 256))

    inner_chunks = wide.shape[1] // 256

    def raw_chunk(k):
        value = dot(turned[0], wide[:, k * 256 : (k + 1) * 256])
        high = value.astype(BF16)
        spatial[held(k)] = high
        spatial[held(inner_chunks + k)] = (value - high.astype(F32)).astype(BF16)

    def raw_value(k):
        return spatial[held(k)].astype(F32) + spatial[held(inner_chunks + k)].astype(F32)

    def inner_copy(ref, k):
        return pltpu.make_async_copy(
            ref.at[:, k * 256 : (k + 1) * 256],
            inner_ring.at[k % 2, : ref.shape[0]],
            inner_sems.at[k % 2],
        )

    def column(value):
        return jnp.broadcast_to(value, (128, channels)).T[:, 0:1]

    for k in range(2):
        raw_chunk(k)
    sum_three.middle()
    for k in range(2, inner_chunks):
        raw_chunk(k)
    for k in range(2):
        inner_copy(outer_ref, k).start()
    ins["three"].wait()
    ins["expand"].wait()
    grads = sum_three.end()
    norm_three[...] = grads
    a, b, c = norm_scale(2, stat_three, grads)
    coefficients[0:1] = a
    coefficients[1:2] = b
    coefficients[2:3] = c
    def back_three(g):
        rows = slice(FIRST[g] * block, (FIRST[g] + COLUMNS[g]) * block)
        for k in range(inner_chunks):
            at = slice(k * 256, (k + 1) * 256)
            a, b, c = coefficients[0:1, at], coefficients[1:2, at], coefficients[2:3, at]
            up = wide[rows, at].astype(F32) * a
            raw = (three[rows, at].astype(F32) * b + c).reshape(COLUMNS[g], 2, images, 256)
            raw = jnp.stack([raw[:, 0], raw[:, 1] * m[g]], axis=1).reshape(up.shape)
            wide[rows, at] = (up - raw).astype(BF16)

    ins["two"].wait()
    a, b, scale, mean = forward_scale(
        stat_two[...], norm_params(gain_ref, bias_ref, 1, channels), number
    )
    sums = jnp.zeros((1, channels), F32)
    gains = jnp.zeros((1, channels), F32)
    back_three(0)
    for g in range(3):
        if g < 2:
            back_three(g + 1)
        blocks = slice(FIRST[g], FIRST[g] + COLUMNS[g])
        raw = two[blocks]
        v = raw * a + b
        rows = slice(FIRST[g] * block, (FIRST[g] + COLUMNS[g]) * block)
        value = slope_of(v, *half_of(v)) * dot_t(wide[rows, :], expand[...]).reshape(raw.shape)
        value = jnp.stack([value[:, 0], value[:, 1] * m[g]], axis=1)
        u[blocks] = value
        sums = sums + jnp.sum(value, axis=(0, 1, 2))[None]
        gains = gains + jnp.sum(value * ((raw - mean) * scale), axis=(0, 1, 2))[None]
    for k, source in enumerate((upper_ref, middle_ref, lower_ref)):
        get(k, source.at[:tail], wide.at[:tail, k * channels : (k + 1) * channels])
    sum_two.begin(jnp.concatenate([gains, sums], axis=0))
    for at in (0, PADDED[1] - 1, PADDED[2] - 1, PADDED_BLOCKS - 1):
        hidden[at * block : (at + 1) * block] = jnp.zeros((block, channels), BF16)
    per = inner_chunks // n
    sum_column = column(hidden_sum[...])

    def expand_chunk(k):
        at = slice(k * 256, (k + 1) * 256)
        a, b, c = coefficients[0:1, at], coefficients[1:2, at], coefficients[2:3, at]
        inner_copy(outer_ref, k).wait()
        value = raw_value(k) * a - inner_ring[k % 2, :channels] * b - sum_column * c
        put_blocks(
            n, w, gradients[2], value, 0, channels, place_n=k // per, lane=k % per * 256
        )
        if k + 2 < inner_chunks:
            inner_copy(outer_ref, k + 2).start()

    for k in range(inner_chunks // 2):
        expand_chunk(k)
    sum_two.middle()
    for k in range(inner_chunks // 2, inner_chunks):
        expand_chunk(k)
    launch(2)
    for tap in range(9):
        get(
            ("spatial", tap),
            spatial_ref.at[tap * channels : (tap + 1) * channels],
            spatial.at[tap // 3, :, tap % 3 * channels : (tap % 3 + 1) * channels],
        )
    ins[0].wait()
    turn(wide, slice(0, channels), turned.at[0])
    for k in (1, 2):
        ins[k].wait()
        turn(wide, slice(k * channels, (k + 1) * channels), turned.at[k])
    get("rows", rows_ref, wide)
    grads = sum_two.end()
    norm_two[...] = grads
    a, b, c = norm_scale(1, stat_two, grads)
    for g in range(3):
        blocks = slice(FIRST[g], FIRST[g] + COLUMNS[g])
        up = u[blocks] * a
        raw = two[blocks] * b + c
        value = jnp.stack([up[:, 0] - raw[:, 0], up[:, 1] - raw[:, 1] * m[g]], axis=1)
        hidden[PADDED[g] * block : (PADDED[g] + COLUMNS[g]) * block] = value.reshape(
            COLUMNS[g] * block, channels
        ).astype(BF16)
    three[tail:, :] = jnp.zeros((deep - tail, three.shape[1]), BF16)
    for offset in range(3):
        for g in range(3):
            start = (PADDED[g] - (offset - 1)) * block
            three[
                FIRST[g] * block : (FIRST[g] + COLUMNS[g]) * block,
                offset * channels : (offset + 1) * channels,
            ] = hidden[start : start + COLUMNS[g] * block, :]
    advance(2, 0)
    for level in range(3):
        for offset in range(3):
            value = dot(turned[level], three[:, offset * channels : (offset + 1) * channels])
            put_blocks(n, w, gradients[1], value, (3 * level + offset) * channels, shapes[1][0])
        if level > 0:
            advance(2, level)
    launch(1)
    get("again", grad_ref, three.at[:tail])
    for tap in range(9):
        ins["spatial", tap].wait()

    def taps(g, level):
        at, count = PADDED[g] * block, COLUMNS[g] * block
        shifted = [hidden[at - d * block : at - d * block + count, :] for d in (-1, 0, 1)]
        value = dot_t(jnp.concatenate(shifted, axis=1), spatial[level])
        return value.reshape(COLUMNS[g], 2, images, channels)

    copies = []
    for g in range(3):
        flag = m[g] > 0.5
        blocks = slice(FIRST[g], FIRST[g] + COLUMNS[g])
        rows = padded_rows(COLUMNS[g] * images)
        upper = taps(g, 0)
        lower = taps(g, 2)
        to_before[starts[g] : starts[g] + rows] = pack_halo(upper[:, 0])
        to_after[starts[g] : starts[g] + rows] = pack_halo(
            lower[:, 1] + jnp.where(flag, 0.0, lower[:, 0])
        )
        copies.append(
            halo_copies(
                n, g, rows, starts, to_after, from_before, to_before, from_after, halo_sems
            )
        )
        halo_start(n, copies[g])
        u[blocks] = jnp.stack([upper[:, 1], jnp.where(flag, lower[:, 0], 0.0)], axis=1)
        if g > 0:
            advance(1, 0, g - 1)
    ins["one"].wait()

    a, b, scale, mean = forward_scale(stat_one[...], norm_params(gain_ref, bias_ref, 0, channels), number)
    sums = jnp.zeros((1, channels), F32)
    gains = jnp.zeros((1, channels), F32)
    for g in range(3):
        flag = m[g] > 0.5
        blocks = slice(FIRST[g], FIRST[g] + COLUMNS[g])
        middle = taps(g, 1)
        rows = padded_rows(COLUMNS[g] * images)
        halo_arrived(n, copies[g])
        before = unpack_halo(from_before[starts[g] : starts[g] + rows], COLUMNS[g], images)
        after = unpack_halo(from_after[starts[g] : starts[g] + rows], COLUMNS[g], images)
        first = u[blocks][:, 0] + middle[:, 0] + before + jnp.where(flag, 0.0, after)
        second = u[blocks][:, 1] + middle[:, 1] + jnp.where(flag, after, 0.0)
        raw = one[blocks]
        v = raw * a + b
        slope = slope_of(v, *half_of(v))
        value = jnp.stack([slope[:, 0] * first, slope[:, 1] * second * m[g]], axis=1)
        u[blocks] = value
        sums = sums + jnp.sum(value, axis=(0, 1, 2))[None]
        gains = gains + jnp.sum(value * ((raw - mean) * scale), axis=(0, 1, 2))[None]
    sum_one.begin(jnp.concatenate([gains, sums], axis=0))
    for k in range(2):
        inner_copy(inner_ref, k).start()
    for g in range(3):
        hidden[FIRST[g] * block : (FIRST[g] + COLUMNS[g]) * block] = (
            u[FIRST[g] : FIRST[g] + COLUMNS[g]].reshape(COLUMNS[g] * block, channels).astype(BF16)
        )
    hidden[tail:deep] = jnp.zeros((deep - tail, channels), BF16)
    turn(hidden.at[:deep], slice(0, channels), turned.at[0])
    ins["rows"].wait()

    for k in range(2):
        raw_chunk(k)
    sum_one.middle()
    for k in range(2, inner_chunks):
        raw_chunk(k)
        if k == 3:
            advance(1, 1, 0)
        if k == 4:
            advance(2, 3)
        if k == 6:
            advance(1, 1, 1)
    for k in range(4):
        at = slice(k * channels, (k + 1) * channels)
        get(("reduce", k), reduce_ref.at[at], wide.at[:channels, at])
    for g in range(3):
        halo_sent(n, copies[g])
    grads = sum_one.end()
    norm_one[...] = grads
    a, b, c = norm_scale(0, stat_one, grads)
    a_column, b_column, c_column = column(a), column(b), column(c)
    advance(1, 2, 0)
    per = 256 // (shapes[0][0] // w)
    for k in range(inner_chunks):
        inner_copy(inner_ref, k).wait()
        value = raw_value(k) * a_column - inner_ring[k % 2, :channels] * b_column
        value = value - inner_ring[k % 2, channels : channels + 1] * c_column
        put_blocks(n, w, gradients[0], value.T, 0, shapes[0][0], place_w=k * per)
        if k + 2 < inner_chunks:
            inner_copy(inner_ref, k + 2).start()
    launch(0)
    advance(1, 2, 1)
    advance(0, 0)
    for g in range(3):
        blocks = slice(FIRST[g], FIRST[g] + COLUMNS[g])
        up = u[blocks] * a
        raw = one[blocks] * b + c
        value = jnp.stack([up[:, 0] - raw[:, 0], up[:, 1] - raw[:, 1] * m[g]], axis=1)
        hidden[FIRST[g] * block : (FIRST[g] + COLUMNS[g]) * block] = value.reshape(
            COLUMNS[g] * block, channels
        ).astype(BF16)
    for k in range(4):
        ins["reduce", k].wait()
    ins["again"].wait()

    def input_step(k, _):
        at = pl.ds(pl.multiple_of(k * 256, 256), 256)
        weight = wide[
            pl.ds(pl.multiple_of(lax.rem(k, 2) * 256, 256), 256),
            pl.ds(pl.multiple_of(lax.div(k, 2) * channels, channels), channels),
        ]
        for g in range(3):
            rows = slice(FIRST[g] * block, (FIRST[g] + COLUMNS[g]) * block)
            value = dot_t(hidden[rows, :], weight) + three[rows, at].astype(F32)
            three[rows, at] = value.astype(BF16)
        return 0

    lax.fori_loop(0, inner_chunks // 2, input_step, 0)
    advance(0, 1)
    lax.fori_loop(inner_chunks // 2, inner_chunks, input_step, 0)
    get("out", three.at[:tail], input_ref)
    advance(1, 3, 0)
    advance(0, 2)
    columns, totals = [None] * 3, [None] * 3

    def column_sums(which):
        for copy in sent[which]:
            copy.wait_recv()
        old = (reduce_rows_ref, spatial_rows_ref, expand_rows_ref)[which]
        by_column, total = [], None
        for k in range(n):
            value = shares[which][k].astype(F32)
            square = value * value + EPS_ONE
            by_column.append(jnp.sum(square, axis=0, keepdims=True))
            part = jnp.sum(by_column[-1], axis=1, keepdims=True)
            total = part if total is None else total + part
        columns[which] = jnp.concatenate(by_column, axis=1)
        total = BETA * jnp.sum(old[...].reshape(1, -1), axis=1, keepdims=True) + (
            1.0 - BETA
        ) / shapes[which][1] * total
        totals[which] = jnp.broadcast_to(total, (1, 128))

    column_sums(2)
    advance(1, 3, 1)
    advance(0, 3)
    column_sums(1)
    column_sums(0)
    columns_ref[...] = sum_over(
        "wide", w, jnp.concatenate(columns + totals, axis=1), *column_scratch
    )
    for which in range(3):
        for scatter in scatters[which]:
            scatter.done()
        for copy in sent[which]:
            copy.wait_send()
    ins["out"].wait()


def final_kernel(
    w, input_ref, sums_ref, reduce_share, spatial_share, expand_share,
    reduce_ref, spatial_ref, expand_ref, square_reduce, square_spatial, square_expand,
    reduce_rows, spatial_rows, expand_rows, reduce_cols, spatial_cols, expand_cols,
    one_ref, two_ref, three_ref, gain_ref, bias_ref, state_ref,
    out_ref, reduce_grad, spatial_grad, expand_grad, reduce_rows_next, reduce_cols_next, spatial_rows_next,
    spatial_cols_next, expand_rows_next, expand_cols_next, reduce_next, spatial_next, expand_next,
    norm_grads, norm_second, norm_next,
    row_ring, out_ring, zeros, reduce_own, spatial_own, expand_own, sems, ring_sems,
):
    me = lax.axis_index("wide")
    own_copies = []
    for k, (source, own) in enumerate(
        ((reduce_ref, reduce_own), (spatial_ref, spatial_own), (expand_ref, expand_own))
    ):
        size = own.shape[0]
        own_copies.append(
            pltpu.make_async_copy(source.at[pl.ds(me * size, size)], own, sems.at[k])
        )
        own_copies[-1].start()
    images = out_ref.shape[1]
    lanes = out_ref.shape[3] // 2
    block = 2 * images

    def copy(which, t):
        slot = lax.rem(t, DEPTH)
        if which == 0:
            rows = pl.ds(pl.multiple_of(t * block, block), block)
            return pltpu.make_async_copy(input_ref.at[rows], row_ring.at[slot], ring_sems.at[0, slot])
        g, j = place_of(t)
        return pltpu.make_async_copy(out_ring.at[slot], out_ref.at[g, :, j], ring_sems.at[1, slot])

    for t in range(DEPTH):
        copy(0, jnp.int32(t)).start()
    zeros[...] = jnp.zeros(zeros.shape, BF16)
    empty = []
    for g in range(3):
        for j in range(COLUMNS[g], out_ref.shape[2]):
            empty.append(
                pltpu.make_async_copy(zeros, out_ref.at[g, :, j], sems.at[3 + len(empty)])
            )
            empty[-1].start()

    def pair(i, _):
        for k in range(2):
            copy(0, 2 * i + k).wait()

        @pl.when(2 * i >= DEPTH)
        def _():
            for k in range(2):
                copy(1, 2 * i + k - DEPTH).wait()

        for k in range(2):
            slot = lax.rem(2 * i + k, DEPTH)
            for group in range(lanes // 8):
                blocks = [
                    row_ring[slot, :, c * 128 : (c + 1) * 128].astype(F32)
                    for c in range(8 * group, 8 * group + 8)
                ]
                for j in range(images // 8):
                    out_ring[slot, 8 * j : 8 * j + 8, 16 * group : 16 * group + 16] = turned_out(
                        blocks, j
                    ).astype(BF16)
        for k in range(2):
            copy(1, 2 * i + k).start()

        @pl.when(2 * i + DEPTH < BLOCKS)
        def _():
            for k in range(2):
                copy(0, 2 * i + k + DEPTH).start()

        return 0

    lax.fori_loop(0, BLOCKS // 2, pair, 0)
    grads = jnp.concatenate([one_ref[...], two_ref[...], three_ref[...]], axis=1)
    norm_grads[...] = grads
    params = jnp.concatenate([gain_ref[...], bias_ref[...]], axis=0)
    second = BETA * state_ref[...] + (1.0 - BETA) * (grads * grads + EPS_ONE)
    norm_second[...] = second
    rate = 0.5 * jnp.maximum(
        jnp.sqrt(jnp.sum(params * params, axis=1, keepdims=True) / params.shape[1]), 0.001
    )
    norm_next[...] = params - rate * grads * lax.rsqrt(second)
    lane = 0
    weights = (
        (reduce_share, reduce_own, square_reduce, reduce_rows, reduce_cols, reduce_grad,
         reduce_rows_next, reduce_cols_next, reduce_next, reduce_ref),
        (spatial_share, spatial_own, square_spatial, spatial_rows, spatial_cols, spatial_grad,
         spatial_rows_next, spatial_cols_next, spatial_next, spatial_ref),
        (expand_share, expand_own, square_expand, expand_rows, expand_cols, expand_grad,
         expand_rows_next, expand_cols_next, expand_next, expand_ref),
    )
    at = 0
    for share, *_ in weights:
        at += share.shape[0] * share.shape[2]
    for which, (
        share, own, square, old_rows, old_cols, grad, next_rows, next_cols, next_w, full
    ) in enumerate(weights):
        n, height, width = share.shape
        all_rows = full.shape[0]
        rate = 0.5 * jnp.maximum(
            jnp.sqrt(
                jnp.sum(square[...], axis=1, keepdims=True) / (full.shape[0] * full.shape[1])
            ),
            0.001,
        )
        row_mean = sums_ref[0:1, at + 128 * which : at + 128 * which + 1] / all_rows
        total = jnp.zeros((height, 1), F32)
        for k in range(n):
            value = share[k].astype(F32)
            grad[:, k * width : (k + 1) * width] = value
            total = total + jnp.sum(value * value + EPS_ONE, axis=1, keepdims=True)
        old = jnp.broadcast_to(old_rows[...].reshape(1, height), (128, height)).T
        by_row = BETA * old + (1.0 - BETA) / (n * width) * total
        next_rows[...] = by_row.T[0:1].reshape(next_rows.shape)
        by_column = BETA * old_cols[...] + (1.0 - BETA) / all_rows * sums_ref[
            0:1, lane : lane + n * width
        ]
        next_cols[...] = by_column
        lane += n * width
        second = by_row[:, 0:1] * (by_column / row_mean)
        own_copies[which].wait()
        next_w[...] = own[...] - rate * grad[...] * lax.rsqrt(second)
    for t in range(BLOCKS - DEPTH, BLOCKS):
        copy(1, jnp.int32(t)).wait()
    for done in empty:
        done.wait()


def pixels_first(x):
    g, i, s, c, k = x.shape
    x = jnp.transpose(x, (0, 1, 3, 2, 4)).reshape(g, i, c, s, k // 128, 128)
    return jnp.transpose(x, (0, 1, 2, 4, 3, 5)).reshape(g, i, c, s * k // 128, 128)


def slots_first(x, slots):
    g, i, c, r, k = x.shape
    x = x.reshape(g, i, c, r // slots, slots, k)
    x = jnp.transpose(x, (0, 1, 2, 4, 3, 5)).reshape(g, i, c, slots, r // slots * k)
    return jnp.transpose(x, (0, 1, 3, 2, 4))


def call(kernel, outs, ins, scratch, collective_id=None, **more):
    params = dict(vmem_limit_bytes=LIMIT)
    if collective_id is not None:
        params.update(collective_id=collective_id, has_side_effects=True)
    smem = [x.ndim == 1 for x in ins]
    specs = dict(
        in_specs=[pl.BlockSpec(memory_space=pltpu.SMEM if s else VMEM) for s in smem],
        out_specs=tuple(pl.BlockSpec(memory_space=VMEM) for _ in outs),
    )
    specs.update(more)
    return pl.pallas_call(
        kernel,
        out_shape=tuple(jax.ShapeDtypeStruct(shape, dtype) for shape, dtype in outs),
        scratch_shapes=scratch,
        compiler_params=pltpu.CompilerParams(**params),
        **specs,
    )(*ins)


def shards(
    n, w, images, upstream, row_counts, w_reduce, w_spatial, w_expand, norm_gain, norm_bias,
    reduce_rows, reduce_cols, spatial_rows, spatial_cols, expand_rows, expand_cols, norm_state,
):
    groups, count, slots, across, outer = images.shape
    inner = w_reduce.shape[1]
    block = slots * count
    tail = BLOCKS * block
    deep = -(-tail // 256) * 256
    number = float(w * count * sum(c * c for c in COLUMNS))
    counts = row_counts.reshape(groups)
    x = pixels_first(images)
    up = pixels_first(upstream)
    params = (norm_gain.reshape(1, -1), norm_bias.reshape(1, -1))
    whole = (BLOCKS, slots, count, inner)
    narrow_sums = reduce_scratch(n, w, 2, inner)
    outer_sums = reduce_scratch(n, w, 2, outer)
    _, halo = halo_rows(count)
    halo_scratch = [VMEM((halo, inner), BF16)] * 4 + [pltpu.SemaphoreType.DMA((4, 3))]
    stage = VMEM((outer // 128, block, 128), F32)

    weights = (w_reduce, w_spatial, w_expand)
    full = pl.BlockSpec(memory_space=VMEM)
    smem = pl.BlockSpec(memory_space=pltpu.SMEM)
    far = pl.BlockSpec(memory_space=pl.ANY)
    dma = pltpu.SemaphoreType.DMA
    padded = ((PADDED_BLOCKS * block, inner), BF16)
    compact = ((deep, inner), BF16)
    inner_images = ((inner + 16, outer), F32)
    forward_arrays = [
        ((deep, outer), BF16), (whole, F32), (whole, F32), compact, compact, compact, compact,
        ((tail, outer), BF16), inner_images, (w_expand.shape, F32), *[(v.shape, BF16) for v in weights],
    ]
    (
        rows, conv_one, conv_two, upper, middle, lower, hidden_two, conv_three, one_images, two_three, *rounded,
        stats_one, stats_two, stats_three, hidden_sum, square_one, square_two, square_three,
    ) = call(
        functools.partial(forward_kernel, n, w, number),
        forward_arrays
        + [((2, v), F32) for v in (inner, inner, outer)]
        + [((1, v), F32) for v in (inner, inner, inner, outer)],
        (x, *weights, *params, counts),
        [
            VMEM((RING, *x.shape[1:2], *x.shape[3:]), BF16),
            VMEM((deep, outer), BF16),
            VMEM((4, CHUNK, inner), F32),
            VMEM(w_expand.shape, F32),
            *[VMEM(v.shape, BF16) for v in weights],
            VMEM(whole, F32),
            VMEM(whole, F32),
            *[VMEM(*padded)] * 3,
            VMEM((deep, inner), BF16),
            VMEM((deep, outer), BF16),
            VMEM((inner + 16, deep), BF16),
            VMEM(*inner_images),
            *halo_scratch,
            dma((RING,)),
            dma((4,)),
            dma,
            dma((32,)),
        ]
        + narrow_sums
        + narrow_sums
        + outer_sums,
        0,
        in_specs=[far] * 4 + [full, full, smem],
        out_specs=(far,) * 13 + (full,) * 7,
    )
    row_ring = VMEM((DEPTH, block, outer), BF16)
    map_ring = VMEM((DEPTH, *x.shape[1:2], *x.shape[3:]), BF16)
    output, grad_summed, sums_three = call(
        functools.partial(top_kernel, number, inner),
        [(x.shape, BF16), ((tail, outer), BF16), ((2, 8, outer), F32)],
        (conv_three, rows, up, stats_three, *params, counts),
        [
            row_ring,
            row_ring,
            map_ring,
            map_ring,
            row_ring,
            *[stage] * 4,
            VMEM((2, outer), F32),
            dma((6, DEPTH)),
        ],
        in_specs=[far] * 3 + [full] * 3 + [smem],
        out_specs=(far, far, full),
    )
    blocks = [block_shapes(n, w, *weight.shape) for weight in weights]
    rows_old = [reduce_rows, spatial_rows, expand_rows]
    cols_old = [v.reshape(1, -1) for v in (reduce_cols, spatial_cols, expand_cols)]
    lanes = sum(v.shape[1] for v in weights) + 3 * 128
    scatter = []
    for weight in weights:
        scatter += scatter_scratch(n, w, *weight.shape)
    input_grad, sums, *more = call(
        functools.partial(backward_kernel, n, w, number, [v.shape for v in weights]),
        [((tail, outer), BF16), ((1, lanes), F32)]
        + [((n, v.shape[0] // w, v.shape[1] // n), BF16) for v in weights]
        + [((2, v), F32) for v in (inner, inner, outer)],
        (
            conv_three, grad_summed, hidden_two, rounded[2], conv_two, rounded[1],
            upper, middle, lower, conv_one, rows, rounded[0], one_images, two_three, sums_three, hidden_sum,
            stats_one, stats_two, stats_three, *params, counts, *rows_old,
        ),
        [
            VMEM((deep, outer), BF16),
            VMEM((deep, outer), BF16),
            VMEM(*padded),
            VMEM((3, inner, deep), BF16),
            VMEM(w_expand.shape, BF16),
            VMEM((3, inner, 3 * inner), BF16),
            VMEM(whole, F32),
            VMEM(whole, F32),
            VMEM(whole, F32),
            VMEM((4, outer), F32),
            VMEM((2, inner + 16, 256), F32),
            dma((2,)),
            *halo_scratch,
            dma((32,)),
            *[VMEM(shape, BF16) for which in range(3) for shape in blocks[which]],
        ]
        + scatter
        + [dma((n,))] * 6
        + outer_sums
        + narrow_sums
        + narrow_sums
        + [VMEM((w, 1, lanes), F32), dma((w,)), dma((w,))],
        1,
        in_specs=[far] * 14 + [full] * 7 + [smem] + [full] * 3,
        out_specs=(far,) + (full,) * 7,
    )
    shares, (grads_one, grads_two, grads_three) = more[:3], more[3:]
    heights = [v.shape[0] // w for v in weights]
    slabs = [((h, v.shape[1]), F32) for h, v in zip(heights, weights)]
    vectors = []
    for h, v in zip(heights, weights):
        vectors += [((h,), F32), ((1, v.shape[1]), F32)]
    outs = call(
        functools.partial(final_kernel, w),
        [(x.shape, BF16)] + slabs + vectors + slabs + [(norm_state.shape, F32)] * 3,
        (
            input_grad, sums, *shares, *weights, square_one, square_two, square_three,
            *rows_old, *cols_old, grads_one, grads_two, grads_three, *params, norm_state,
        ),
        [
            row_ring,
            map_ring,
            VMEM((*x.shape[1:2], *x.shape[3:]), BF16),
            *[VMEM(shape, dtype) for shape, dtype in slabs],
            dma((16,)),
            dma((2, DEPTH)),
        ],
        in_specs=[far] + [full] * 4 + [far] * 3 + [full] * 15,
        out_specs=(far,) + (full,) * 15,
    )
    input_grad, *outs = outs
    for k in range(3, 9):
        outs[k] = outs[k].reshape(-1)
    return (slots_first(output, slots), slots_first(input_grad, slots), *outs)


def solution(mesh):
    maps = P(None, "wide", "narrow", None, None)
    in_specs = (
        maps, maps, P(None, "wide", "narrow"), P(), P(), P(), P(), P(),
        P("wide"), P(), P("wide"), P(), P("wide"), P(), P(),
    )
    out_specs = (
        maps, maps, P("wide", None), P("wide", None), P("wide", None),
        P("wide"), P(), P("wide"), P(), P("wide"), P(),
        P("wide", None), P("wide", None), P("wide", None), P(), P(), P(),
    )
    return jax.shard_map(
        functools.partial(shards, mesh.shape["narrow"], mesh.shape["wide"]),
        mesh=mesh,
        in_specs=in_specs,
        out_specs=out_specs,
        check_vma=False,
    )
```

```python
import functools

import jax
import jax.numpy as jnp
from jax import lax
from jax.experimental import pallas as pl
from jax.experimental.pallas import tpu as pltpu
from jax.sharding import PartitionSpec as P

MESH = pl.DeviceIdType.MESH
VMEM = pltpu.VMEM
F32 = jnp.float32
BF16 = jnp.bfloat16

STEP = 10
EPS = 1e-05
EPS_ONE = 1e-30
LIMIT = 63 * 1024 * 1024

COLUMNS = (5, 6, 7)
FIRST = (0, 5, 11)
PADDED = (1, 7, 14)
BLOCKS = 18
PADDED_BLOCKS = 22

C0 = 0.7978845608
C1 = C0 * 0.044715


def half_of(v):
    squared = v * v
    return 0.5 + 0.5 * jnp.tanh(v * (C0 + C1 * squared)), squared


def slope_of(v, h, squared):
    return h + v * h * (1.0 - h) * (2.0 * C0 + 6.0 * C1 * squared)


def dot(a, b):
    return jnp.dot(a, b, preferred_element_type=F32)


def dot_t(a, b):
    return lax.dot_general(a, b, (((1,), (1,)), ((), ())), preferred_element_type=F32)


def turned_in(load, count, group):
    pieces = [
        jnp.transpose(load(k)[:, 8 * group : 8 * group + 8].astype(F32), (1, 0, 2))
        for k in range(count)
    ]
    return [
        jnp.concatenate([piece[2 * c + slot] for slot in range(2) for piece in pieces], axis=0)
        for c in range(4)
    ]


def turned_out(blocks, k):
    images = blocks[0].shape[0] // 2
    rows = [
        block[slot * images + 8 * k : slot * images + 8 * k + 8]
        for block in blocks
        for slot in range(2)
    ]
    halves = [jnp.transpose(jnp.stack(rows[at : at + 8]), (1, 0, 2)) for at in (0, 8)]
    return jnp.concatenate(halves, axis=1)


def to_rows(lanes):
    size = 16 * lanes
    to = lax.broadcasted_iota(jnp.int32, (size, size), 0)
    at = lax.broadcasted_iota(jnp.int32, (size, size), 1)
    return (at == lax.rem(to, 8) * (2 * lanes) + to // 8).astype(F32).astype(BF16)


def from_rows(lanes):
    size = 16 * lanes
    to = lax.broadcasted_iota(jnp.int32, (size, size), 1)
    at = lax.broadcasted_iota(jnp.int32, (size, size), 0)
    return (at == lax.rem(to, 8) * (2 * lanes) + to // 8).astype(F32).astype(BF16)


def turn_in(order, load, stage):
    count = stage.shape[0]
    for k in range(0, count, 2):
        if k + 1 < count:
            both = dot(order, jnp.concatenate([load(k), load(k + 1)], axis=1))
            stage[k] = both[:, :128]
            stage[k + 1] = both[:, 128:]
        else:
            stage[k] = dot(order, load(k))


def turn_out(order, stage, store):
    count = stage.shape[0]
    for k in range(0, count, 2):
        if k + 1 < count:
            both = jnp.concatenate([stage[k].astype(BF16), stage[k + 1].astype(BF16)], axis=1)
            both = dot(order, both).astype(BF16)
            store(k, both[:, :128])
            store(k + 1, both[:, 128:])
        else:
            store(k, dot(order, stage[k].astype(BF16)).astype(BF16))


def staged(stage, c, slot):
    row = (2 * c + slot) * 8
    return jnp.concatenate([stage[k, row : row + 8, :] for k in range(stage.shape[0])], axis=0)


def put_staged(stage, c, slot, value):
    row = (2 * c + slot) * 8
    for k in range(stage.shape[0]):
        stage[k, row : row + 8, :] = value[8 * k : 8 * k + 8]


def cast_rows(value_ref, wb_ref, row, square):
    step = 64

    def add(k, square):
        value = value_ref[pl.ds(pl.multiple_of(k * step, step), step), :]
        wb_ref[pl.ds(pl.multiple_of(row + k * step, step), step), :] = value.astype(BF16)
        return square + jnp.sum((value * value).reshape(step // 8, 8, value.shape[1]), axis=0)

    return lax.fori_loop(0, value_ref.shape[0] // step, add, square)


def reduce_scratch(n, w, rows, channels):
    return [
        VMEM((n, rows, channels), F32),
        VMEM((w, rows, channels), F32),
        pltpu.SemaphoreType.DMA((n,)),
        pltpu.SemaphoreType.DMA((n,)),
        pltpu.SemaphoreType.DMA((w,)),
        pltpu.SemaphoreType.DMA((w,)),
    ]


def greet(n, w):
    me_n, me_w = lax.axis_index("narrow"), lax.axis_index("wide")
    barrier = pltpu.get_barrier_semaphore()
    for k in range(1, n):
        pl.semaphore_signal(
            barrier, inc=1, device_id={"narrow": lax.rem(me_n + k, n)}, device_id_type=MESH
        )
    for k in range(1, w):
        pl.semaphore_signal(
            barrier, inc=1, device_id={"wide": lax.rem(me_w + k, w)}, device_id_type=MESH
        )


def met(n, w):
    pl.semaphore_wait(pltpu.get_barrier_semaphore(), n + w - 2)


def sum_over(axis, size, value, slots, send, recv):
    me = lax.axis_index(axis)
    slots[me] = value
    copies = []
    for k in range(1, size):
        copy = pltpu.make_async_remote_copy(
            src_ref=slots.at[me],
            dst_ref=slots.at[me],
            send_sem=send.at[k],
            recv_sem=recv.at[k],
            device_id={axis: lax.rem(me + k, size)},
            device_id_type=MESH,
        )
        copy.start()
        copies.append(copy)
    for copy in copies:
        copy.wait_recv()
    total = slots[0]
    for k in range(1, size):
        total = total + slots[k]
    for copy in copies:
        copy.wait_send()
    return total


class SumAll:
    def __init__(self, n, w, scratch):
        self.axes = (("narrow", n, scratch[0], *scratch[2:4]), ("wide", w, scratch[1], *scratch[4:6]))
        self.copies = [[], []]

    def send(self, which, value):
        axis, size, slots, send, recv = self.axes[which]
        me = lax.axis_index(axis)
        slots[me] = value
        for k in range(1, size):
            copy = pltpu.make_async_remote_copy(
                src_ref=slots.at[me],
                dst_ref=slots.at[me],
                send_sem=send.at[k],
                recv_sem=recv.at[k],
                device_id={axis: lax.rem(me + k, size)},
                device_id_type=MESH,
            )
            copy.start()
            self.copies[which].append(copy)

    def total(self, which):
        _, size, slots, _, _ = self.axes[which]
        for copy in self.copies[which]:
            copy.wait_recv()
        total = slots[0]
        for k in range(1, size):
            total = total + slots[k]
        return total

    def begin(self, value):
        self.send(0, value)

    def middle(self):
        self.send(1, self.total(0))

    def end(self):
        total = self.total(1)
        for copies in self.copies:
            for copy in copies:
                copy.wait_send()
        return total


def forward_scale(stats, params, number):
    mean = stats[0:1] / number
    scale = lax.rsqrt(stats[1:2] / number - mean * mean + EPS)
    a = scale * params[0]
    return a, params[1] - mean * a, scale, mean


def backward_scale(stats, params, grads, number):
    mean = stats[0:1] / number
    scale = lax.rsqrt(stats[1:2] / number - mean * mean + EPS)
    a = scale * params[0]
    gain_grad, bias_grad = grads[0:1], grads[1:2]
    over = a / number
    return a, over * scale * gain_grad, over * (bias_grad - mean * scale * gain_grad)


def norm_params(gain_ref, bias_ref, which, inner):
    lane = (0, inner, 2 * inner, gain_ref.shape[1])
    at = slice(lane[which], lane[which + 1])
    return gain_ref[0:1, at], bias_ref[0:1, at]


def second_counts(counts_ref, g):
    return jnp.where(counts_ref[g] == 2, 1.0, 0.0)


def two_sums(first, second, m):
    return jnp.sum(first, axis=(0, 1))[None] + m * jnp.sum(second, axis=(0, 1))[None]


def padded_rows(count):
    return -(-count // 16) * 16


def halo_rows(images):
    starts, at = [], 0
    for g in range(3):
        starts.append(at)
        at += padded_rows(COLUMNS[g] * images)
    return starts, at


def pack_halo(value):
    count = value.shape[0] * value.shape[1]
    value = value.reshape(count, value.shape[2])
    extra = padded_rows(count) - count
    if extra:
        value = jnp.concatenate([value, jnp.zeros((extra, value.shape[1]), F32)], axis=0)
    return value.astype(BF16)


def unpack_halo(value, columns, images):
    return value.astype(F32)[: columns * images].reshape(columns, images, value.shape[1])


def halo_copies(n, g, count, starts, up_src, up_dst, down_src, down_dst, sems):
    me = lax.axis_index("narrow")
    rows = pl.ds(starts[g], count)
    forward = pltpu.make_async_remote_copy(
        src_ref=up_src.at[rows],
        dst_ref=up_dst.at[rows],
        send_sem=sems.at[0, g],
        recv_sem=sems.at[1, g],
        device_id={"narrow": lax.rem(me + 1, n)},
        device_id_type=MESH,
    )
    backward = pltpu.make_async_remote_copy(
        src_ref=down_src.at[rows],
        dst_ref=down_dst.at[rows],
        send_sem=sems.at[2, g],
        recv_sem=sems.at[3, g],
        device_id={"narrow": lax.rem(me + n - 1, n)},
        device_id_type=MESH,
    )
    return forward, backward


def halo_start(n, copies):
    me = lax.axis_index("narrow")

    @pl.when(me < n - 1)
    def _():
        copies[0].start()

    @pl.when(me > 0)
    def _():
        copies[1].start()


def halo_arrived(n, copies):
    me = lax.axis_index("narrow")

    @pl.when(me > 0)
    def _():
        copies[0].wait_recv()

    @pl.when(me < n - 1)
    def _():
        copies[1].wait_recv()


def halo_sent(n, copies):
    me = lax.axis_index("narrow")

    @pl.when(me < n - 1)
    def _():
        copies[0].wait_send()

    @pl.when(me > 0)
    def _():
        copies[1].wait_send()


def halo_edges(n, from_before, from_after):
    me = lax.axis_index("narrow")

    @pl.when(me == 0)
    def _():
        from_before[...] = jnp.zeros(from_before.shape, from_before.dtype)

    @pl.when(me == n - 1)
    def _():
        from_after[...] = jnp.zeros(from_after.shape, from_after.dtype)


RING = BLOCKS
CHUNK = 512


def turn(source, columns, target):
    for k in range(source.shape[0] // 128):
        target[:, k * 128 : (k + 1) * 128] = source[k * 128 : (k + 1) * 128, columns].T


def place_of(t):
    g = (t >= FIRST[1]).astype(jnp.int32) + (t >= FIRST[2]).astype(jnp.int32)
    return g, t - jnp.where(g == 0, FIRST[0], jnp.where(g == 1, FIRST[1], FIRST[2]))


def forward_kernel(
    n, w, number, x_ref, reduce_ref, spatial_ref, expand_ref, gain_ref, bias_ref, counts_ref,
    rows_out, one_out, two_out, upper_out, middle_out, lower_out, hidden_out, three_out, inner_out, outer_out,
    reduce_out, spatial_out, expand_out,
    stat_one, stat_two, stat_three, hidden_sum, square_reduce, square_spatial, square_expand,
    ring, rows, weight, wide_weight, reduce, spatial, expand, one, two, upper, middle, lower, hidden, three,
    turned, inner,
    last, first, above, below, halo_sems, ring_sems, weight_sems, wide_sem, out_sems,
    *scratch,
):
    m = [second_counts(counts_ref, g) for g in range(3)]
    sum_one = SumAll(n, w, scratch[:6])
    sum_two = SumAll(n, w, scratch[6:12])
    sum_three = SumAll(n, w, scratch[12:18])
    images = x_ref.shape[1]
    lanes = x_ref.shape[3] // 2
    channels = one.shape[3]
    block = 2 * images
    tail = BLOCKS * block
    starts, _ = halo_rows(images)
    outs = []

    def put(source, target):
        copy = pltpu.make_async_copy(source, target, out_sems.at[len(outs)])
        copy.start()
        outs.append(copy)

    def fetch(t):
        g, j = place_of(t)
        slot = lax.rem(t, RING)
        return pltpu.make_async_copy(x_ref.at[g, :, j], ring.at[slot], ring_sems.at[slot])

    sources = [reduce_ref.at[k : k + CHUNK] for k in range(0, reduce_ref.shape[0], CHUNK)]
    reduce_chunks = len(sources)
    sources += [spatial_ref.at[k : k + CHUNK] for k in range(0, spatial_ref.shape[0], CHUNK)]
    slots = weight.shape[0]

    def weight_copy(k):
        return pltpu.make_async_copy(sources[k], weight.at[k % slots], weight_sems.at[k % slots])

    for t in range(RING):
        fetch(jnp.int32(t)).start()
    for k in range(slots):
        weight_copy(k).start()
    wide_copy = pltpu.make_async_copy(expand_ref, wide_weight, wide_sem)
    greet(n, w)
    rows[tail:, :] = jnp.zeros((rows.shape[0] - tail, rows.shape[1]), BF16)
    three[tail:, :] = jnp.zeros((three.shape[0] - tail, three.shape[1]), BF16)
    for ref in (upper, middle, lower):
        for at in (0, PADDED[1] - 1, PADDED[2] - 1, PADDED_BLOCKS - 1):
            ref[at * block : (at + 1) * block] = jnp.zeros((block, channels), BF16)
    halo_edges(n, above, below)

    def cast_chunk(k, wb_ref, row, square):
        weight_copy(k).wait()
        square = cast_rows(weight.at[k % slots], wb_ref, row, square)
        if k + slots < len(sources):
            weight_copy(k + slots).start()
        return square

    def place(i, _):
        for k in range(2):
            fetch(2 * i + k).wait()
        for k in range(2):
            slot = lax.rem(2 * i + k, RING)
            row = pl.multiple_of((2 * i + k) * block, block)
            for group in range(lanes // 4):
                values = turned_in(lambda j: ring[slot, 8 * j : 8 * j + 8], images // 8, group)
                for c in range(4):
                    at = (4 * group + c) * 128
                    rows[pl.ds(row, block), at : at + 128] = values[c].astype(BF16)

        @pl.when(2 * i + RING < BLOCKS)
        def _():
            for k in range(2):
                fetch(2 * i + k + RING).start()

        return 0

    lax.fori_loop(0, BLOCKS // 2, place, 0)
    wide_copy.start()
    put(rows, rows_out)
    square = jnp.zeros((8, channels), F32)
    for k in range(reduce_chunks):
        square = cast_chunk(k, reduce, k * CHUNK, square)
    square_reduce[...] = jnp.sum(square, axis=0, keepdims=True)
    put(reduce, reduce_out)
    sums = jnp.zeros((1, channels), F32)
    squares = jnp.zeros((1, channels), F32)
    for g in range(3):
        at = slice(FIRST[g] * block, (FIRST[g] + COLUMNS[g]) * block)
        c = dot(rows[at, :], reduce[...]).reshape(COLUMNS[g], 2, images, channels)
        one[FIRST[g] : FIRST[g] + COLUMNS[g]] = c
        sums = sums + two_sums(c[:, 0], c[:, 1], m[g])
        squares = squares + two_sums(c[:, 0] * c[:, 0], c[:, 1] * c[:, 1], m[g])
    met(n, w)
    sum_one.begin(jnp.concatenate([sums, squares], axis=0))
    put(one, one_out)
    square = jnp.zeros((8, channels), F32)
    middle_chunk = (reduce_chunks + len(sources)) // 2
    for k in range(reduce_chunks, middle_chunk):
        square = cast_chunk(k, spatial, (k - reduce_chunks) * CHUNK, square)
    for g in range(3):
        value = one[FIRST[g] : FIRST[g] + COLUMNS[g]]
        value = jnp.stack([value[:, 0], value[:, 1] * m[g]], axis=1)
        hidden[FIRST[g] * block : (FIRST[g] + COLUMNS[g]) * block] = value.reshape(
            COLUMNS[g] * block, channels
        ).astype(BF16)
    hidden[tail:] = jnp.zeros((hidden.shape[0] - tail, channels), BF16)
    sum_one.middle()
    turn(hidden, slice(0, channels), turned.at[:channels])
    lane = lax.broadcasted_iota(jnp.int32, (16, turned.shape[1]), 1)
    place = lax.div(lane, block)
    flag = jnp.where(place < FIRST[1], m[0], jnp.where(place < FIRST[2], m[1], m[2]))
    flag = jnp.where(lax.rem(lane, block) < images, 1.0, flag)
    turned[channels:] = jnp.where(lane < tail, flag, 0.0).astype(BF16)

    def inner_chunk(k):
        at = slice(k * 256, (k + 1) * 256)
        inner[:, at] = dot(turned[...], rows[:, at])

    inner_chunks = rows.shape[1] // 256
    for k in range(middle_chunk, len(sources)):
        square = cast_chunk(k, spatial, (k - reduce_chunks) * CHUNK, square)
    for k in range(inner_chunks // 4):
        inner_chunk(k)
    square_spatial[...] = jnp.sum(square, axis=0, keepdims=True)
    put(spatial, spatial_out)
    stats = sum_one.end()
    stat_one[...] = stats

    a, b, _, _ = forward_scale(stats, norm_params(gain_ref, bias_ref, 0, channels), number)
    copies = []
    for g in range(3):
        v = one[FIRST[g] : FIRST[g] + COLUMNS[g]] * a + b
        value = v * half_of(v)[0]
        slot_one, slot_two = value[:, 0], value[:, 1] * m[g]
        count = padded_rows(COLUMNS[g] * images)
        first[starts[g] : starts[g] + count] = pack_halo(slot_one)
        last[starts[g] : starts[g] + count] = pack_halo(
            jnp.where(m[g] > 0.5, slot_two, slot_one)
        )
        copies.append(halo_copies(n, g, count, starts, last, above, first, below, halo_sems))
        halo_start(n, copies[g])
        both = jnp.stack([slot_one, slot_two], axis=1).reshape(COLUMNS[g] * block, channels)
        middle[PADDED[g] * block : (PADDED[g] + COLUMNS[g]) * block] = both.astype(BF16)

    def taps(ref, g, level):
        at, count = PADDED[g] * block, COLUMNS[g] * block
        shifted = [ref[at + d * block : at + d * block + count, :] for d in (-1, 0, 1)]
        return dot(
            jnp.concatenate(shifted, axis=1),
            spatial[3 * level * channels : 3 * (level + 1) * channels, :],
        )

    def put_groups(source, target):
        for g in range(3):
            count = COLUMNS[g] * block
            put(
                source.at[PADDED[g] * block : PADDED[g] * block + count],
                target.at[FIRST[g] * block : FIRST[g] * block + count],
            )

    for g in range(3):
        two[FIRST[g] : FIRST[g] + COLUMNS[g]] = taps(middle, g, 1).reshape(
            COLUMNS[g], 2, images, channels
        )
    put_groups(middle, middle_out)
    sums = jnp.zeros((1, channels), F32)
    squares = jnp.zeros((1, channels), F32)
    for g in range(3):
        halo_arrived(n, copies[g])
        at, count = PADDED[g] * block, COLUMNS[g] * block
        height = padded_rows(COLUMNS[g] * images)
        up = unpack_halo(above[starts[g] : starts[g] + height], COLUMNS[g], images)
        down = unpack_halo(below[starts[g] : starts[g] + height], COLUMNS[g], images)
        own = middle[at : at + count].astype(F32).reshape(COLUMNS[g], 2, images, channels)
        upper[at : at + count] = (
            jnp.stack([up, own[:, 0]], axis=1).reshape(count, channels).astype(BF16)
        )
        lower[at : at + count] = (
            jnp.stack([jnp.where(m[g] > 0.5, own[:, 1], down), down], axis=1)
            .reshape(count, channels)
            .astype(BF16)
        )
        c = taps(upper, g, 0) + taps(lower, g, 2)
        c = c.reshape(COLUMNS[g], 2, images, channels) + two[FIRST[g] : FIRST[g] + COLUMNS[g]]
        two[FIRST[g] : FIRST[g] + COLUMNS[g]] = c
        sums = sums + two_sums(c[:, 0], c[:, 1], m[g])
        squares = squares + two_sums(c[:, 0] * c[:, 0], c[:, 1] * c[:, 1], m[g])
    sum_two.begin(jnp.concatenate([sums, squares], axis=0))
    put(two, two_out)
    put_groups(upper, upper_out)
    put_groups(lower, lower_out)
    wide_copy.wait()
    half = wide_weight.shape[0] // 2
    square = jnp.zeros((8, wide_weight.shape[1]), F32)
    square = cast_rows(wide_weight.at[:half], expand, 0, square)
    for k in range(inner_chunks // 4, inner_chunks // 2):
        inner_chunk(k)
    sum_two.middle()
    square = cast_rows(wide_weight.at[half:], expand, half, square)
    square_expand[...] = jnp.sum(square, axis=0, keepdims=True)
    put(expand, expand_out)
    for k in range(inner_chunks // 2, inner_chunks):
        inner_chunk(k)
    put(inner, inner_out)
    inner_done = outs[-1]
    for g in range(3):
        halo_sent(n, copies[g])
    stats = sum_two.end()
    stat_two[...] = stats

    a, b, _, _ = forward_scale(stats, norm_params(gain_ref, bias_ref, 1, channels), number)
    sums = jnp.zeros((1, channels), F32)
    for g in range(3):
        v = two[FIRST[g] : FIRST[g] + COLUMNS[g]] * a + b
        value = v * half_of(v)[0]
        both = jnp.stack([value[:, 0], value[:, 1] * m[g]], axis=1)
        sums = sums + jnp.sum(both, axis=(0, 1, 2))[None]
        hidden[FIRST[g] * block : (FIRST[g] + COLUMNS[g]) * block] = both.reshape(
            COLUMNS[g] * block, channels
        ).astype(BF16)
    hidden_sum[...] = sums
    put(hidden.at[:tail], hidden_out.at[:tail])
    sums, squares = [], []
    for part in range(three.shape[1] // 512):
        s = jnp.zeros((1, 512), F32)
        q = jnp.zeros((1, 512), F32)
        columns = slice(part * 512, (part + 1) * 512)
        for g in range(3):
            at = slice(FIRST[g] * block, (FIRST[g] + COLUMNS[g]) * block)
            c = dot(hidden[at, :], expand[:, columns])
            three[at, columns] = c.astype(BF16)
            s = s + jnp.sum(c, axis=0, keepdims=True)
            q = q + jnp.sum(c * c, axis=0, keepdims=True)
        put(three.at[:tail, columns], three_out.at[:, columns])
        sums.append(s)
        squares.append(q)
    sum_three.begin(
        jnp.concatenate(
            [jnp.concatenate(sums, axis=1), jnp.concatenate(squares, axis=1)], axis=0
        )
    )
    turn(hidden, slice(0, channels), turned.at[:channels])
    inner_done.wait()
    outs = [copy for copy in outs if copy is not inner_done]

    def outer_chunk(k):
        at = slice(k * 256, (k + 1) * 256)
        inner[:channels, at] = dot(turned[:channels], three[:, at])

    for k in range(inner_chunks // 4):
        outer_chunk(k)
    sum_three.middle()
    for k in range(inner_chunks // 4, inner_chunks):
        outer_chunk(k)
    put_last = pltpu.make_async_copy(inner.at[:channels], outer_out, out_sems.at[31])
    put_last.start()
    stat_three[...] = sum_three.end()
    for copy in outs:
        copy.wait()
    put_last.wait()


DEPTH = 10
AHEAD = DEPTH - 2


def top_kernel(
    number, inner, conv_ref, rows_ref, up_ref, stats_ref, gain_ref, bias_ref, counts_ref,
    out_ref, grad_ref, total,
    conv_ring, rows_ring, up_ring, out_ring, grad_ring, up_one, up_two, out_one, out_two, order, coefficients, sems,
):
    images = up_ref.shape[1]
    lanes = up_ref.shape[3] // 2
    block = 2 * images

    def rows_of(t):
        return pl.ds(pl.multiple_of(t * block, block), block)

    def copy(which, t):
        slot = lax.rem(t, DEPTH)
        g, j = place_of(t)
        source, target = (
            lambda: (conv_ref.at[rows_of(t)], conv_ring.at[slot]),
            lambda: (rows_ref.at[rows_of(t)], rows_ring.at[slot]),
            lambda: (up_ref.at[g, :, j], up_ring.at[slot]),
            lambda: (out_ring.at[slot], out_ref.at[g, :, j]),
            lambda: (grad_ring.at[slot], grad_ref.at[rows_of(t)]),
        )[which]()
        return pltpu.make_async_copy(source, target, sems.at[which, slot])

    def each(which, t, do):
        @pl.when((t >= 0) & (t < BLOCKS))
        def _():
            do(copy(which, t))

    def start(which, t):
        each(which, t, lambda c: c.start())

    def wait(which, t):
        each(which, t, lambda c: c.wait())

    for t in range(AHEAD + 1):
        start(2, jnp.int32(t))
        if t < AHEAD:
            start(0, jnp.int32(t))
            start(1, jnp.int32(t))
    total[...] = jnp.zeros(total.shape, F32)
    params = norm_params(gain_ref, bias_ref, 2, inner)
    a, b, scale, mean = forward_scale(stats_ref[...], params, number)
    coefficients[0:1] = a
    coefficients[1:2] = b
    order[0] = to_rows(lanes)
    order[1] = from_rows(lanes)
    out_two[...] = jnp.zeros(out_two.shape, F32)

    def enter(t, stage):
        slot = lax.rem(t, DEPTH)
        turn_in(
            order[0], lambda k: up_ring[slot, 8 * k : 8 * k + 8].reshape(16 * lanes, 128), stage
        )

    def leave(t, stage):
        slot = lax.rem(t + DEPTH, DEPTH)

        def store(k, value):
            out_ring[slot, 8 * k : 8 * k + 8] = value.reshape(8, 2 * lanes, 128)

        turn_out(order[1], stage, store)

    def work(t, stage_up, stage_out):
        slot = lax.rem(t, DEPTH)
        m = second_counts(counts_ref, place_of(t)[0])
        for c in range(lanes):
            at = slice(c * 128, (c + 1) * 128)
            raw = conv_ring[slot, :, at].astype(F32)
            v = raw * coefficients[0:1, at] + coefficients[1:2, at]
            v = v + rows_ring[slot, :, at].astype(F32)
            h, squared = half_of(v)
            out = v * h
            slope = h + out * (1.0 - h) * (2.0 * C0 + 6.0 * C1 * squared)
            put_staged(stage_out, c, 0, out[:images])
            put_staged(stage_out, c, 1, out[images:] * m)
            grad = jnp.concatenate(
                [
                    slope[:images] * staged(stage_up, c, 0),
                    slope[images:] * (staged(stage_up, c, 1) * m),
                ],
                axis=0,
            )
            grad_ring[slot, :, at] = grad.astype(BF16)
            total[0, :, at] += jnp.sum((grad * raw).reshape(block // 8, 8, 128), axis=0)
            total[1, :, at] += jnp.sum(grad.reshape(block // 8, 8, 128), axis=0)

    wait(2, jnp.int32(0))
    enter(jnp.int32(0), up_one)

    def pair(i, _):
        t = 2 * i
        for k in (0, 1):
            start(0, t + AHEAD + k)
            start(1, t + AHEAD + k)
            start(2, t + AHEAD + k + 1)
        for k in (0, 1):
            wait(0, t + k)
            wait(1, t + k)
            wait(2, t + k + 1)
            wait(3, t + k - 1 - DEPTH)
            wait(4, t + k - DEPTH)
        enter(t + 1, up_two)
        work(t, up_one, out_one)
        leave(t - 1, out_two)
        enter(t + 2, up_one)
        work(t + 1, up_two, out_two)
        leave(t, out_one)
        for k in (0, 1):
            start(3, t + k - 1)
            start(4, t + k)
        return 0

    lax.fori_loop(0, BLOCKS // 2, pair, 0)
    last = jnp.int32(BLOCKS - 1)
    wait(3, last - DEPTH)
    leave(last, out_two)
    start(3, last)
    for k in range(DEPTH):
        wait(3, last - k)
        wait(4, last - k)
    out_ring[0] = jnp.zeros(out_ring.shape[1:], BF16)
    copies = []
    for g in range(3):
        for j in range(COLUMNS[g], out_ref.shape[2]):
            copies.append(
                pltpu.make_async_copy(
                    out_ring.at[0], out_ref.at[g, :, j], sems.at[5, len(copies)]
                )
            )
            copies[-1].start()
    value = jnp.sum(total[...], axis=1)
    gains = scale * (value[0:1] - mean * value[1:2])
    total[0] = jnp.concatenate([gains, jnp.zeros((7, gains.shape[1]), F32)], axis=0)
    for copy in copies:
        copy.wait()


def unravel(index, sizes):
    digits = []
    for size in reversed(sizes):
        digits.append(index % size if isinstance(index, int) else lax.rem(index, size))
        index = index // size if isinstance(index, int) else lax.div(index, size)
    return digits[::-1]


def mesh_digits(n, w):
    if (n, w) == (4, 8):
        return (
            [("narrow", 2, 2), ("narrow", 1, 2), ("wide", 2, 4), ("wide", 1, 2)],
            [(1, 3, 0, 2), (1, 0, 3, 2)],
        )
    return [("narrow", 1, n), ("wide", 1, w)], [(0, 1), (0, 1)]


def digit_sizes(n, w):
    return [d[2] for d in mesh_digits(n, w)[0]]


def narrow_digits(n, w):
    return [d[2] for d in mesh_digits(n, w)[0] if d[0] == "narrow"]


def wide_digits(n, w):
    return [d[2] for d in mesh_digits(n, w)[0] if d[0] == "wide"]


def weight_parts(w, rows):
    share = rows // w
    if rows >= 4096 and share % 64 == 0:
        return 4
    return 2 if share % 32 == 0 else 1


def block_shapes(n, w, rows, columns):
    parts = weight_parts(w, rows)
    return [(*digit_sizes(n, w), rows // w // parts, columns // n)] * parts


def put_blocks(n, w, refs, value, row, rows, place_n=None, place_w=0, lane=0):
    share = rows // w
    part = share // len(refs)
    at, end = row, row + value.shape[0]
    columns = refs[0].shape[-1]
    while at < end:
        stop = min(end, (at // part + 1) * part)
        wide = at // share
        ref = refs[at // part % len(refs)]
        inside = slice(at % part, at % part + stop - at)
        piece = value[at - row : stop - row]
        wide = unravel(place_w + wide, wide_digits(n, w))
        if place_n is not None:
            lanes = slice(lane, lane + piece.shape[1])
            ref[(*unravel(place_n, narrow_digits(n, w)), *wide, inside, lanes)] = piece.astype(BF16)
        else:
            for k in range(n):
                ref[(*unravel(k, narrow_digits(n, w)), *wide, inside, slice(None))] = piece[
                    :, k * columns : (k + 1) * columns
                ].astype(BF16)
        at = stop


def scatter_scratch(n, w, rows, columns):
    digits, orders = mesh_digits(n, w)
    scratch = []
    for part, shape in enumerate(block_shapes(n, w, rows, columns)):
        left = list(range(len(digits)))
        for d in orders[part % 2]:
            left.remove(d)
            size = digits[d][2]
            scratch.append(VMEM((size - 1, *(digits[k][2] for k in left), *shape[-2:]), BF16))
            scratch.append(pltpu.SemaphoreType.DMA((size - 1,)))
            scratch.append(pltpu.SemaphoreType.DMA((size - 1,)))
    return scratch


class Scatter:
    def __init__(self, n, w, source, scratch, order):
        self.digits = mesh_digits(n, w)[0]
        self.order = order
        self.scratch = scratch
        self.sources = [source] + [scratch[3 * k].at[0] for k in range(len(order))]
        self.copies = []
        self.steps = len(order)

    def own(self, d):
        axis, stride, size = self.digits[d]
        return lax.rem(lax.div(lax.axis_index(axis), stride), size)

    def pick(self, ref, step, value):
        left = [d for d in range(len(self.digits)) if d not in self.order[:step]]
        return ref.at[tuple(value if d == self.order[step] else slice(None) for d in left)]

    def start(self, step):
        d = self.order[step]
        axis, stride, size = self.digits[d]
        landing, send, recv = self.scratch[3 * step : 3 * step + 3]
        mine = self.own(d)
        for k in range(1, size):
            other = lax.rem(mine + k, size)
            copy = pltpu.make_async_remote_copy(
                src_ref=self.pick(self.sources[step], step, other),
                dst_ref=landing.at[k - 1],
                send_sem=send.at[k - 1],
                recv_sem=recv.at[k - 1],
                device_id={axis: lax.axis_index(axis) + (other - mine) * stride},
                device_id_type=MESH,
            )
            copy.start()
            self.copies.append((step, copy))

    def finish(self, step):
        for at, copy in self.copies:
            if at == step:
                copy.wait_recv()
        d = self.order[step]
        size = self.digits[d][2]
        landing = self.scratch[3 * step]
        left = [k for k in range(len(self.digits)) if k not in self.order[: step + 1]]
        sizes = [self.digits[k][2] for k in left]
        mine = self.own(d)
        source = self.pick(self.sources[step], step, mine)

        def total(at):
            value = source[at].astype(F32)
            for k in range(size - 1):
                value = value + landing[(k, *at)].astype(F32)
            return value

        if step == self.steps - 1:
            return total((slice(None), slice(None)))
        count = 1
        for k in sizes:
            count *= k

        together = 4 if count % 4 == 0 else 1

        def add(index, _):
            for k in range(together):
                at = tuple(unravel(index * together + k, sizes))
                landing[(0, *at)] = total(at).astype(BF16)
            return 0

        lax.fori_loop(0, count // together, add, 0)

    def done(self):
        for _, copy in self.copies:
            copy.wait_send()


def share_out(n, slots, value, send, recv):
    me = lax.axis_index("narrow")
    row = 0
    for piece in value:
        slots[me, row : row + piece.shape[0]] = piece.astype(BF16)
        row += piece.shape[0]
    copies = []
    for k in range(1, n):
        copy = pltpu.make_async_remote_copy(
            src_ref=slots.at[me],
            dst_ref=slots.at[me],
            send_sem=send.at[k],
            recv_sem=recv.at[k],
            device_id={"narrow": lax.rem(me + k, n)},
            device_id_type=MESH,
        )
        copy.start()
        copies.append(copy)
    return copies


BETA = 1.0 - STEP ** (-0.8)


class Refs:
    def __init__(self, refs):
        self.refs = list(refs)

    def take(self, count):
        taken, self.refs = self.refs[:count], self.refs[count:]
        return taken

    def one(self):
        return self.take(1)[0]


def backward_kernel(
    n, w, number, shapes, three_ref, grad_ref, hidden_ref, expand_ref, two_ref, spatial_ref,
    upper_ref, middle_ref, lower_ref, one_ref, rows_ref, reduce_ref, inner_ref, outer_ref, sums_ref, hidden_sum, stat_one, stat_two, stat_three,
    gain_ref, bias_ref, counts_ref, reduce_rows_ref, spatial_rows_ref, expand_rows_ref, *refs,
):
    refs = Refs(refs)
    parts = [weight_parts(w, shape[0]) for shape in shapes]
    input_ref, columns_ref = refs.take(2)
    shares = refs.take(3)
    norm_one, norm_two, norm_three = refs.take(3)
    three, wide, hidden, turned, expand, spatial, two, one, u, coefficients = refs.take(10)
    inner_ring, inner_sems = refs.take(2)
    to_before, to_after, from_after, from_before, halo_sems, in_sems = refs.take(6)
    gradients = [refs.take(parts[k]) for k in range(3)]
    orders = mesh_digits(n, w)[1]
    steps = len(orders[0])
    scatters = [
        [
            Scatter(n, w, gradients[k][p], refs.take(3 * steps), orders[p % 2])
            for p in range(parts[k])
        ]
        for k in range(3)
    ]
    share_sems = [refs.take(2) for _ in range(3)]
    sum_three = SumAll(n, w, refs.take(6))
    sum_two = SumAll(n, w, refs.take(6))
    sum_one = SumAll(n, w, refs.take(6))
    column_scratch = refs.take(3)

    images = two.shape[2]
    channels = two.shape[3]
    block = 2 * images
    tail = BLOCKS * block
    deep = three.shape[0]
    m = [second_counts(counts_ref, g) for g in range(3)]
    starts, _ = halo_rows(images)

    ins = {}

    def get(name, source, target):
        ins[name] = pltpu.make_async_copy(source, target, in_sems.at[len(ins)])
        ins[name].start()

    get("hidden", hidden_ref.at[:tail], hidden.at[:tail])
    get("three", three_ref, three.at[:tail])
    get("grad", grad_ref, wide.at[:tail])
    get("expand", expand_ref, expand)
    get("two", two_ref, two)
    get("one", one_ref, one)
    greet(n, w)

    def norm_scale(which, stat, grads):
        params = norm_params(gain_ref, bias_ref, which, channels)
        return backward_scale(stat[...], params, grads, number)

    sent = {}

    def advance(which, step, half=None):
        if step >= steps:
            return
        count = parts[which]
        if half is not None and count == 1:
            if half == 0:
                return
            half = None
        first = 0 if half is None else half * (count // 2)
        last = count if half is None else first + count // 2
        for scatter in scatters[which][first:last]:
            value = scatter.finish(step)
            if step < steps - 1:
                scatter.start(step + 1)
            else:
                sent.setdefault(which, []).append(value)
        if step == steps - 1 and last == count:
            sent[which] = share_out(n, shares[which], sent[which], *share_sems[which])

    def launch(which):
        for scatter in scatters[which]:
            scatter.start(0)

    value = jnp.concatenate(
        [sums_ref[0, 0:1], jnp.sum(sums_ref[1], axis=0, keepdims=True)],
        axis=0,
    )
    halo_edges(n, from_before, from_after)
    wide[tail:, :] = jnp.zeros((deep - tail, wide.shape[1]), BF16)
    hidden[tail:deep] = jnp.zeros((deep - tail, channels), BF16)
    met(n, w)
    sum_three.begin(value)
    ins["hidden"].wait()
    turn(hidden.at[:deep], slice(0, channels), turned.at[0])
    ins["grad"].wait()

    def held(k):
        return (k // 6, slice(None), slice(k % 6 * 256, (k % 6 + 1) * 256))

    inner_chunks = wide.shape[1] // 256

    def raw_chunk(k):
        value = dot(turned[0], wide[:, k * 256 : (k + 1) * 256])
        high = value.astype(BF16)
        spatial[held(k)] = high
        spatial[held(inner_chunks + k)] = (value - high.astype(F32)).astype(BF16)

    def raw_value(k):
        return spatial[held(k)].astype(F32) + spatial[held(inner_chunks + k)].astype(F32)

    def inner_copy(ref, k):
        return pltpu.make_async_copy(
            ref.at[:, k * 256 : (k + 1) * 256],
            inner_ring.at[k % 2, : ref.shape[0]],
            inner_sems.at[k % 2],
        )

    def column(value):
        return jnp.broadcast_to(value, (128, channels)).T[:, 0:1]

    for k in range(2):
        raw_chunk(k)
    sum_three.middle()
    for k in range(2, inner_chunks):
        raw_chunk(k)
    for k in range(2):
        inner_copy(outer_ref, k).start()
    ins["three"].wait()
    ins["expand"].wait()
    grads = sum_three.end()
    norm_three[...] = grads
    a, b, c = norm_scale(2, stat_three, grads)
    coefficients[0:1] = a
    coefficients[1:2] = b
    coefficients[2:3] = c
    def back_three(g):
        rows = slice(FIRST[g] * block, (FIRST[g] + COLUMNS[g]) * block)
        for k in range(inner_chunks):
            at = slice(k * 256, (k + 1) * 256)
            a, b, c = coefficients[0:1, at], coefficients[1:2, at], coefficients[2:3, at]
            up = wide[rows, at].astype(F32) * a
            raw = (three[rows, at].astype(F32) * b + c).reshape(COLUMNS[g], 2, images, 256)
            raw = jnp.stack([raw[:, 0], raw[:, 1] * m[g]], axis=1).reshape(up.shape)
            wide[rows, at] = (up - raw).astype(BF16)

    ins["two"].wait()
    a, b, scale, mean = forward_scale(
        stat_two[...], norm_params(gain_ref, bias_ref, 1, channels), number
    )
    sums = jnp.zeros((1, channels), F32)
    gains = jnp.zeros((1, channels), F32)
    back_three(0)
    for g in range(3):
        if g < 2:
            back_three(g + 1)
        blocks = slice(FIRST[g], FIRST[g] + COLUMNS[g])
        raw = two[blocks]
        v = raw * a + b
        rows = slice(FIRST[g] * block, (FIRST[g] + COLUMNS[g]) * block)
        value = slope_of(v, *half_of(v)) * dot_t(wide[rows, :], expand[...]).reshape(raw.shape)
        value = jnp.stack([value[:, 0], value[:, 1] * m[g]], axis=1)
        u[blocks] = value
        sums = sums + jnp.sum(value, axis=(0, 1, 2))[None]
        gains = gains + jnp.sum(value * ((raw - mean) * scale), axis=(0, 1, 2))[None]
    for k, source in enumerate((upper_ref, middle_ref, lower_ref)):
        get(k, source.at[:tail], wide.at[:tail, k * channels : (k + 1) * channels])
    sum_two.begin(jnp.concatenate([gains, sums], axis=0))
    for at in (0, PADDED[1] - 1, PADDED[2] - 1, PADDED_BLOCKS - 1):
        hidden[at * block : (at + 1) * block] = jnp.zeros((block, channels), BF16)
    per = inner_chunks // n
    sum_column = column(hidden_sum[...])

    def expand_chunk(k):
        at = slice(k * 256, (k + 1) * 256)
        a, b, c = coefficients[0:1, at], coefficients[1:2, at], coefficients[2:3, at]
        inner_copy(outer_ref, k).wait()
        value = raw_value(k) * a - inner_ring[k % 2, :channels] * b - sum_column * c
        put_blocks(
            n, w, gradients[2], value, 0, channels, place_n=k // per, lane=k % per * 256
        )
        if k + 2 < inner_chunks:
            inner_copy(outer_ref, k + 2).start()

    for k in range(inner_chunks // 2):
        expand_chunk(k)
    sum_two.middle()
    for k in range(inner_chunks // 2, inner_chunks):
        expand_chunk(k)
    launch(2)
    for tap in range(9):
        get(
            ("spatial", tap),
            spatial_ref.at[tap * channels : (tap + 1) * channels],
            spatial.at[tap // 3, :, tap % 3 * channels : (tap % 3 + 1) * channels],
        )
    ins[0].wait()
    turn(wide, slice(0, channels), turned.at[0])
    for k in (1, 2):
        ins[k].wait()
        turn(wide, slice(k * channels, (k + 1) * channels), turned.at[k])
    get("rows", rows_ref, wide)
    grads = sum_two.end()
    norm_two[...] = grads
    a, b, c = norm_scale(1, stat_two, grads)
    for g in range(3):
        blocks = slice(FIRST[g], FIRST[g] + COLUMNS[g])
        up = u[blocks] * a
        raw = two[blocks] * b + c
        value = jnp.stack([up[:, 0] - raw[:, 0], up[:, 1] - raw[:, 1] * m[g]], axis=1)
        hidden[PADDED[g] * block : (PADDED[g] + COLUMNS[g]) * block] = value.reshape(
            COLUMNS[g] * block, channels
        ).astype(BF16)
    three[tail:, :] = jnp.zeros((deep - tail, three.shape[1]), BF16)
    for offset in range(3):
        for g in range(3):
            start = (PADDED[g] - (offset - 1)) * block
            three[
                FIRST[g] * block : (FIRST[g] + COLUMNS[g]) * block,
                offset * channels : (offset + 1) * channels,
            ] = hidden[start : start + COLUMNS[g] * block, :]
    advance(2, 0)
    for level in range(3):
        for offset in range(3):
            value = dot(turned[level], three[:, offset * channels : (offset + 1) * channels])
            put_blocks(n, w, gradients[1], value, (3 * level + offset) * channels, shapes[1][0])
        if level > 0:
            advance(2, level)
    launch(1)
    get("again", grad_ref, three.at[:tail])
    for tap in range(9):
        ins["spatial", tap].wait()

    def taps(g, level):
        at, count = PADDED[g] * block, COLUMNS[g] * block
        shifted = [hidden[at - d * block : at - d * block + count, :] for d in (-1, 0, 1)]
        value = dot_t(jnp.concatenate(shifted, axis=1), spatial[level])
        return value.reshape(COLUMNS[g], 2, images, channels)

    copies = []
    for g in range(3):
        flag = m[g] > 0.5
        blocks = slice(FIRST[g], FIRST[g] + COLUMNS[g])
        rows = padded_rows(COLUMNS[g] * images)
        upper = taps(g, 0)
        lower = taps(g, 2)
        to_before[starts[g] : starts[g] + rows] = pack_halo(upper[:, 0])
        to_after[starts[g] : starts[g] + rows] = pack_halo(
            lower[:, 1] + jnp.where(flag, 0.0, lower[:, 0])
        )
        copies.append(
            halo_copies(
                n, g, rows, starts, to_after, from_before, to_before, from_after, halo_sems
            )
        )
        halo_start(n, copies[g])
        u[blocks] = jnp.stack([upper[:, 1], jnp.where(flag, lower[:, 0], 0.0)], axis=1)
    advance(1, 0)
    ins["one"].wait()

    a, b, scale, mean = forward_scale(stat_one[...], norm_params(gain_ref, bias_ref, 0, channels), number)
    sums = jnp.zeros((1, channels), F32)
    gains = jnp.zeros((1, channels), F32)
    for g in range(3):
        flag = m[g] > 0.5
        blocks = slice(FIRST[g], FIRST[g] + COLUMNS[g])
        middle = taps(g, 1)
        rows = padded_rows(COLUMNS[g] * images)
        halo_arrived(n, copies[g])
        before = unpack_halo(from_before[starts[g] : starts[g] + rows], COLUMNS[g], images)
        after = unpack_halo(from_after[starts[g] : starts[g] + rows], COLUMNS[g], images)
        first = u[blocks][:, 0] + middle[:, 0] + before + jnp.where(flag, 0.0, after)
        second = u[blocks][:, 1] + middle[:, 1] + jnp.where(flag, after, 0.0)
        raw = one[blocks]
        v = raw * a + b
        slope = slope_of(v, *half_of(v))
        value = jnp.stack([slope[:, 0] * first, slope[:, 1] * second * m[g]], axis=1)
        u[blocks] = value
        sums = sums + jnp.sum(value, axis=(0, 1, 2))[None]
        gains = gains + jnp.sum(value * ((raw - mean) * scale), axis=(0, 1, 2))[None]
    sum_one.begin(jnp.concatenate([gains, sums], axis=0))
    for k in range(2):
        inner_copy(inner_ref, k).start()
    for g in range(3):
        hidden[FIRST[g] * block : (FIRST[g] + COLUMNS[g]) * block] = (
            u[FIRST[g] : FIRST[g] + COLUMNS[g]].reshape(COLUMNS[g] * block, channels).astype(BF16)
        )
    hidden[tail:deep] = jnp.zeros((deep - tail, channels), BF16)
    turn(hidden.at[:deep], slice(0, channels), turned.at[0])
    ins["rows"].wait()

    for k in range(2):
        raw_chunk(k)
    sum_one.middle()
    for k in range(2, inner_chunks):
        raw_chunk(k)
        if k == 4:
            advance(2, 3)
        if k == 5:
            advance(1, 1, 0)
    for k in range(4):
        at = slice(k * channels, (k + 1) * channels)
        get(("reduce", k), reduce_ref.at[at], wide.at[:channels, at])
    for g in range(3):
        halo_sent(n, copies[g])
    grads = sum_one.end()
    norm_one[...] = grads
    a, b, c = norm_scale(0, stat_one, grads)
    a_column, b_column, c_column = column(a), column(b), column(c)
    advance(1, 1, 1)
    per = 256 // (shapes[0][0] // w)
    for k in range(inner_chunks):
        inner_copy(inner_ref, k).wait()
        value = raw_value(k) * a_column - inner_ring[k % 2, :channels] * b_column
        value = value - inner_ring[k % 2, channels : channels + 1] * c_column
        put_blocks(n, w, gradients[0], value.T, 0, shapes[0][0], place_w=k * per)
        if k + 2 < inner_chunks:
            inner_copy(inner_ref, k + 2).start()
    launch(0)
    advance(1, 2, 0)
    advance(0, 0)
    for g in range(3):
        blocks = slice(FIRST[g], FIRST[g] + COLUMNS[g])
        up = u[blocks] * a
        raw = one[blocks] * b + c
        value = jnp.stack([up[:, 0] - raw[:, 0], up[:, 1] - raw[:, 1] * m[g]], axis=1)
        hidden[FIRST[g] * block : (FIRST[g] + COLUMNS[g]) * block] = value.reshape(
            COLUMNS[g] * block, channels
        ).astype(BF16)
    for k in range(4):
        ins["reduce", k].wait()
    ins["again"].wait()

    def input_step(k, _):
        at = pl.ds(pl.multiple_of(k * 256, 256), 256)
        weight = wide[
            pl.ds(pl.multiple_of(lax.rem(k, 2) * 256, 256), 256),
            pl.ds(pl.multiple_of(lax.div(k, 2) * channels, channels), channels),
        ]
        for g in range(3):
            rows = slice(FIRST[g] * block, (FIRST[g] + COLUMNS[g]) * block)
            value = dot_t(hidden[rows, :], weight) + three[rows, at].astype(F32)
            three[rows, at] = value.astype(BF16)
        return 0

    lax.fori_loop(0, inner_chunks // 2, input_step, 0)
    advance(1, 2, 1)
    advance(0, 1)
    lax.fori_loop(inner_chunks // 2, inner_chunks, input_step, 0)
    get("out", three.at[:tail], input_ref)
    advance(1, 3, 0)
    advance(0, 2)
    columns, totals = [None] * 3, [None] * 3

    def column_sums(which):
        for copy in sent[which]:
            copy.wait_recv()
        old = (reduce_rows_ref, spatial_rows_ref, expand_rows_ref)[which]
        by_column, total = [], None
        for k in range(n):
            value = shares[which][k].astype(F32)
            square = value * value + EPS_ONE
            by_column.append(jnp.sum(square, axis=0, keepdims=True))
            part = jnp.sum(by_column[-1], axis=1, keepdims=True)
            total = part if total is None else total + part
        columns[which] = jnp.concatenate(by_column, axis=1)
        total = BETA * jnp.sum(old[...].reshape(1, -1), axis=1, keepdims=True) + (
            1.0 - BETA
        ) / shapes[which][1] * total
        totals[which] = jnp.broadcast_to(total, (1, 128))

    column_sums(2)
    advance(1, 3, 1)
    advance(0, 3)
    column_sums(1)
    column_sums(0)
    columns_ref[...] = sum_over(
        "wide", w, jnp.concatenate(columns + totals, axis=1), *column_scratch
    )
    for which in range(3):
        for scatter in scatters[which]:
            scatter.done()
        for copy in sent[which]:
            copy.wait_send()
    ins["out"].wait()


def final_kernel(
    w, input_ref, sums_ref, reduce_share, spatial_share, expand_share,
    reduce_ref, spatial_ref, expand_ref, square_reduce, square_spatial, square_expand,
    reduce_rows, spatial_rows, expand_rows, reduce_cols, spatial_cols, expand_cols,
    one_ref, two_ref, three_ref, gain_ref, bias_ref, state_ref,
    out_ref, reduce_grad, spatial_grad, expand_grad, reduce_rows_next, reduce_cols_next, spatial_rows_next,
    spatial_cols_next, expand_rows_next, expand_cols_next, reduce_next, spatial_next, expand_next,
    norm_grads, norm_second, norm_next,
    row_ring, out_ring, zeros, reduce_own, spatial_own, expand_own, sems, ring_sems,
):
    me = lax.axis_index("wide")
    own_copies = []
    for k, (source, own) in enumerate(
        ((reduce_ref, reduce_own), (spatial_ref, spatial_own), (expand_ref, expand_own))
    ):
        size = own.shape[0]
        own_copies.append(
            pltpu.make_async_copy(source.at[pl.ds(me * size, size)], own, sems.at[k])
        )
        own_copies[-1].start()
    images = out_ref.shape[1]
    lanes = out_ref.shape[3] // 2
    block = 2 * images

    def copy(which, t):
        slot = lax.rem(t, DEPTH)
        if which == 0:
            rows = pl.ds(pl.multiple_of(t * block, block), block)
            return pltpu.make_async_copy(input_ref.at[rows], row_ring.at[slot], ring_sems.at[0, slot])
        g, j = place_of(t)
        return pltpu.make_async_copy(out_ring.at[slot], out_ref.at[g, :, j], ring_sems.at[1, slot])

    for t in range(DEPTH):
        copy(0, jnp.int32(t)).start()
    zeros[...] = jnp.zeros(zeros.shape, BF16)
    empty = []
    for g in range(3):
        for j in range(COLUMNS[g], out_ref.shape[2]):
            empty.append(
                pltpu.make_async_copy(zeros, out_ref.at[g, :, j], sems.at[3 + len(empty)])
            )
            empty[-1].start()

    def pair(i, _):
        for k in range(2):
            copy(0, 2 * i + k).wait()

        @pl.when(2 * i >= DEPTH)
        def _():
            for k in range(2):
                copy(1, 2 * i + k - DEPTH).wait()

        for k in range(2):
            slot = lax.rem(2 * i + k, DEPTH)
            for group in range(lanes // 8):
                blocks = [
                    row_ring[slot, :, c * 128 : (c + 1) * 128].astype(F32)
                    for c in range(8 * group, 8 * group + 8)
                ]
                for j in range(images // 8):
                    out_ring[slot, 8 * j : 8 * j + 8, 16 * group : 16 * group + 16] = turned_out(
                        blocks, j
                    ).astype(BF16)
        for k in range(2):
            copy(1, 2 * i + k).start()

        @pl.when(2 * i + DEPTH < BLOCKS)
        def _():
            for k in range(2):
                copy(0, 2 * i + k + DEPTH).start()

        return 0

    lax.fori_loop(0, BLOCKS // 2, pair, 0)
    grads = jnp.concatenate([one_ref[...], two_ref[...], three_ref[...]], axis=1)
    norm_grads[...] = grads
    params = jnp.concatenate([gain_ref[...], bias_ref[...]], axis=0)
    second = BETA * state_ref[...] + (1.0 - BETA) * (grads * grads + EPS_ONE)
    norm_second[...] = second
    rate = 0.5 * jnp.maximum(
        jnp.sqrt(jnp.sum(params * params, axis=1, keepdims=True) / params.shape[1]), 0.001
    )
    norm_next[...] = params - rate * grads * lax.rsqrt(second)
    lane = 0
    weights = (
        (reduce_share, reduce_own, square_reduce, reduce_rows, reduce_cols, reduce_grad,
         reduce_rows_next, reduce_cols_next, reduce_next, reduce_ref),
        (spatial_share, spatial_own, square_spatial, spatial_rows, spatial_cols, spatial_grad,
         spatial_rows_next, spatial_cols_next, spatial_next, spatial_ref),
        (expand_share, expand_own, square_expand, expand_rows, expand_cols, expand_grad,
         expand_rows_next, expand_cols_next, expand_next, expand_ref),
    )
    at = 0
    for share, *_ in weights:
        at += share.shape[0] * share.shape[2]
    for which, (
        share, own, square, old_rows, old_cols, grad, next_rows, next_cols, next_w, full
    ) in enumerate(weights):
        n, height, width = share.shape
        all_rows = full.shape[0]
        rate = 0.5 * jnp.maximum(
            jnp.sqrt(
                jnp.sum(square[...], axis=1, keepdims=True) / (full.shape[0] * full.shape[1])
            ),
            0.001,
        )
        row_mean = sums_ref[0:1, at + 128 * which : at + 128 * which + 1] / all_rows
        total = jnp.zeros((height, 1), F32)
        for k in range(n):
            value = share[k].astype(F32)
            grad[:, k * width : (k + 1) * width] = value
            total = total + jnp.sum(value * value + EPS_ONE, axis=1, keepdims=True)
        old = jnp.broadcast_to(old_rows[...].reshape(1, height), (128, height)).T
        by_row = BETA * old + (1.0 - BETA) / (n * width) * total
        next_rows[...] = by_row.T[0:1].reshape(next_rows.shape)
        by_column = BETA * old_cols[...] + (1.0 - BETA) / all_rows * sums_ref[
            0:1, lane : lane + n * width
        ]
        next_cols[...] = by_column
        lane += n * width
        second = by_row[:, 0:1] * (by_column / row_mean)
        own_copies[which].wait()
        next_w[...] = own[...] - rate * grad[...] * lax.rsqrt(second)
    for t in range(BLOCKS - DEPTH, BLOCKS):
        copy(1, jnp.int32(t)).wait()
    for done in empty:
        done.wait()


def pixels_first(x):
    g, i, s, c, k = x.shape
    x = jnp.transpose(x, (0, 1, 3, 2, 4)).reshape(g, i, c, s, k // 128, 128)
    return jnp.transpose(x, (0, 1, 2, 4, 3, 5)).reshape(g, i, c, s * k // 128, 128)


def slots_first(x, slots):
    g, i, c, r, k = x.shape
    x = x.reshape(g, i, c, r // slots, slots, k)
    x = jnp.transpose(x, (0, 1, 2, 4, 3, 5)).reshape(g, i, c, slots, r // slots * k)
    return jnp.transpose(x, (0, 1, 3, 2, 4))


def call(kernel, outs, ins, scratch, collective_id=None, **more):
    params = dict(vmem_limit_bytes=LIMIT)
    if collective_id is not None:
        params.update(collective_id=collective_id, has_side_effects=True)
    smem = [x.ndim == 1 for x in ins]
    specs = dict(
        in_specs=[pl.BlockSpec(memory_space=pltpu.SMEM if s else VMEM) for s in smem],
        out_specs=tuple(pl.BlockSpec(memory_space=VMEM) for _ in outs),
    )
    specs.update(more)
    return pl.pallas_call(
        kernel,
        out_shape=tuple(jax.ShapeDtypeStruct(shape, dtype) for shape, dtype in outs),
        scratch_shapes=scratch,
        compiler_params=pltpu.CompilerParams(**params),
        **specs,
    )(*ins)


def shards(
    n, w, images, upstream, row_counts, w_reduce, w_spatial, w_expand, norm_gain, norm_bias,
    reduce_rows, reduce_cols, spatial_rows, spatial_cols, expand_rows, expand_cols, norm_state,
):
    groups, count, slots, across, outer = images.shape
    inner = w_reduce.shape[1]
    block = slots * count
    tail = BLOCKS * block
    deep = -(-tail // 256) * 256
    number = float(w * count * sum(c * c for c in COLUMNS))
    counts = row_counts.reshape(groups)
    x = pixels_first(images)
    up = pixels_first(upstream)
    params = (norm_gain.reshape(1, -1), norm_bias.reshape(1, -1))
    whole = (BLOCKS, slots, count, inner)
    narrow_sums = reduce_scratch(n, w, 2, inner)
    outer_sums = reduce_scratch(n, w, 2, outer)
    _, halo = halo_rows(count)
    halo_scratch = [VMEM((halo, inner), BF16)] * 4 + [pltpu.SemaphoreType.DMA((4, 3))]
    stage = VMEM((count // 8, slots * outer // 16, 128), F32)
    order = (slots * outer // 16, slots * outer // 16)

    weights = (w_reduce, w_spatial, w_expand)
    full = pl.BlockSpec(memory_space=VMEM)
    smem = pl.BlockSpec(memory_space=pltpu.SMEM)
    far = pl.BlockSpec(memory_space=pl.ANY)
    dma = pltpu.SemaphoreType.DMA
    padded = ((PADDED_BLOCKS * block, inner), BF16)
    compact = ((deep, inner), BF16)
    inner_images = ((inner + 16, outer), F32)
    forward_arrays = [
        ((deep, outer), BF16), (whole, F32), (whole, F32), compact, compact, compact, compact,
        ((tail, outer), BF16), inner_images, (w_expand.shape, F32), *[(v.shape, BF16) for v in weights],
    ]
    (
        rows, conv_one, conv_two, upper, middle, lower, hidden_two, conv_three, one_images, two_three, *rounded,
        stats_one, stats_two, stats_three, hidden_sum, square_one, square_two, square_three,
    ) = call(
        functools.partial(forward_kernel, n, w, number),
        forward_arrays
        + [((2, v), F32) for v in (inner, inner, outer)]
        + [((1, v), F32) for v in (inner, inner, inner, outer)],
        (x, *weights, *params, counts),
        [
            VMEM((RING, *x.shape[1:2], *x.shape[3:]), BF16),
            VMEM((deep, outer), BF16),
            VMEM((4, CHUNK, inner), F32),
            VMEM(w_expand.shape, F32),
            *[VMEM(v.shape, BF16) for v in weights],
            VMEM(whole, F32),
            VMEM(whole, F32),
            *[VMEM(*padded)] * 3,
            VMEM((deep, inner), BF16),
            VMEM((deep, outer), BF16),
            VMEM((inner + 16, deep), BF16),
            VMEM(*inner_images),
            *halo_scratch,
            dma((RING,)),
            dma((4,)),
            dma,
            dma((32,)),
        ]
        + narrow_sums
        + narrow_sums
        + outer_sums,
        0,
        in_specs=[far] * 4 + [full, full, smem],
        out_specs=(far,) * 13 + (full,) * 7,
    )
    row_ring = VMEM((DEPTH, block, outer), BF16)
    map_ring = VMEM((DEPTH, *x.shape[1:2], *x.shape[3:]), BF16)
    output, grad_summed, sums_three = call(
        functools.partial(top_kernel, number, inner),
        [(x.shape, BF16), ((tail, outer), BF16), ((2, 8, outer), F32)],
        (conv_three, rows, up, stats_three, *params, counts),
        [
            row_ring,
            row_ring,
            map_ring,
            map_ring,
            row_ring,
            *[stage] * 4,
            VMEM((2, *order), BF16),
            VMEM((2, outer), F32),
            dma((6, DEPTH)),
        ],
        in_specs=[far] * 3 + [full] * 3 + [smem],
        out_specs=(far, far, full),
    )
    blocks = [block_shapes(n, w, *weight.shape) for weight in weights]
    rows_old = [reduce_rows, spatial_rows, expand_rows]
    cols_old = [v.reshape(1, -1) for v in (reduce_cols, spatial_cols, expand_cols)]
    lanes = sum(v.shape[1] for v in weights) + 3 * 128
    scatter = []
    for weight in weights:
        scatter += scatter_scratch(n, w, *weight.shape)
    input_grad, sums, *more = call(
        functools.partial(backward_kernel, n, w, number, [v.shape for v in weights]),
        [((tail, outer), BF16), ((1, lanes), F32)]
        + [((n, v.shape[0] // w, v.shape[1] // n), BF16) for v in weights]
        + [((2, v), F32) for v in (inner, inner, outer)],
        (
            conv_three, grad_summed, hidden_two, rounded[2], conv_two, rounded[1],
            upper, middle, lower, conv_one, rows, rounded[0], one_images, two_three, sums_three, hidden_sum,
            stats_one, stats_two, stats_three, *params, counts, *rows_old,
        ),
        [
            VMEM((deep, outer), BF16),
            VMEM((deep, outer), BF16),
            VMEM(*padded),
            VMEM((3, inner, deep), BF16),
            VMEM(w_expand.shape, BF16),
            VMEM((3, inner, 3 * inner), BF16),
            VMEM(whole, F32),
            VMEM(whole, F32),
            VMEM(whole, F32),
            VMEM((4, outer), F32),
            VMEM((2, inner + 16, 256), F32),
            dma((2,)),
            *halo_scratch,
            dma((32,)),
            *[VMEM(shape, BF16) for which in range(3) for shape in blocks[which]],
        ]
        + scatter
        + [dma((n,))] * 6
        + outer_sums
        + narrow_sums
        + narrow_sums
        + [VMEM((w, 1, lanes), F32), dma((w,)), dma((w,))],
        1,
        in_specs=[far] * 14 + [full] * 7 + [smem] + [full] * 3,
        out_specs=(far,) + (full,) * 7,
    )
    shares, (grads_one, grads_two, grads_three) = more[:3], more[3:]
    heights = [v.shape[0] // w for v in weights]
    slabs = [((h, v.shape[1]), F32) for h, v in zip(heights, weights)]
    vectors = []
    for h, v in zip(heights, weights):
        vectors += [((h,), F32), ((1, v.shape[1]), F32)]
    outs = call(
        functools.partial(final_kernel, w),
        [(x.shape, BF16)] + slabs + vectors + slabs + [(norm_state.shape, F32)] * 3,
        (
            input_grad, sums, *shares, *weights, square_one, square_two, square_three,
            *rows_old, *cols_old, grads_one, grads_two, grads_three, *params, norm_state,
        ),
        [
            row_ring,
            map_ring,
            VMEM((*x.shape[1:2], *x.shape[3:]), BF16),
            *[VMEM(shape, dtype) for shape, dtype in slabs],
            dma((16,)),
            dma((2, DEPTH)),
        ],
        in_specs=[far] + [full] * 4 + [far] * 3 + [full] * 15,
        out_specs=(far,) + (full,) * 15,
    )
    input_grad, *outs = outs
    for k in range(3, 9):
        outs[k] = outs[k].reshape(-1)
    return (slots_first(output, slots), slots_first(input_grad, slots), *outs)


def solution(mesh):
    maps = P(None, "wide", "narrow", None, None)
    in_specs = (
        maps, maps, P(None, "wide", "narrow"), P(), P(), P(), P(), P(),
        P("wide"), P(), P("wide"), P(), P("wide"), P(), P(),
    )
    out_specs = (
        maps, maps, P("wide", None), P("wide", None), P("wide", None),
        P("wide"), P(), P("wide"), P(), P("wide"), P(),
        P("wide", None), P("wide", None), P("wide", None), P(), P(), P(),
    )
    return jax.shard_map(
        functools.partial(shards, mesh.shape["narrow"], mesh.shape["wide"]),
        mesh=mesh,
        in_specs=in_specs,
        out_specs=out_specs,
        check_vma=False,
    )
```

```python
import functools

import jax
import jax.numpy as jnp
from jax import lax
from jax.experimental import pallas as pl
from jax.experimental.pallas import tpu as pltpu
from jax.sharding import PartitionSpec as P

MESH = pl.DeviceIdType.MESH
VMEM = pltpu.VMEM
F32 = jnp.float32
BF16 = jnp.bfloat16

STEP = 10
EPS = 1e-05
EPS_ONE = 1e-30
LIMIT = 63 * 1024 * 1024

COLUMNS = (5, 6, 7)
FIRST = (0, 5, 11)
PADDED = (1, 7, 14)
BLOCKS = 18
PADDED_BLOCKS = 22

C0 = 0.7978845608
C1 = C0 * 0.044715


def half_of(v):
    squared = v * v
    return 0.5 + 0.5 * jnp.tanh(v * (C0 + C1 * squared)), squared


def slope_of(v, h, squared):
    return h + v * h * (1.0 - h) * (2.0 * C0 + 6.0 * C1 * squared)


def dot(a, b):
    return jnp.dot(a, b, preferred_element_type=F32)


def dot_t(a, b):
    return lax.dot_general(a, b, (((1,), (1,)), ((), ())), preferred_element_type=F32)


def turned_in(load, count, group):
    pieces = [
        jnp.transpose(load(k)[:, 8 * group : 8 * group + 8].astype(F32), (1, 0, 2))
        for k in range(count)
    ]
    return [
        jnp.concatenate([piece[2 * c + slot] for slot in range(2) for piece in pieces], axis=0)
        for c in range(4)
    ]


def turned_out(blocks, k):
    images = blocks[0].shape[0] // 2
    rows = [
        block[slot * images + 8 * k : slot * images + 8 * k + 8]
        for block in blocks
        for slot in range(2)
    ]
    halves = [jnp.transpose(jnp.stack(rows[at : at + 8]), (1, 0, 2)) for at in (0, 8)]
    return jnp.concatenate(halves, axis=1)


def to_rows(lanes):
    size = 16 * lanes
    to = lax.broadcasted_iota(jnp.int32, (size, size), 0)
    at = lax.broadcasted_iota(jnp.int32, (size, size), 1)
    return (at == lax.rem(to, 8) * (2 * lanes) + to // 8).astype(F32).astype(BF16)


def from_rows(lanes):
    size = 16 * lanes
    to = lax.broadcasted_iota(jnp.int32, (size, size), 1)
    at = lax.broadcasted_iota(jnp.int32, (size, size), 0)
    return (at == lax.rem(to, 8) * (2 * lanes) + to // 8).astype(F32).astype(BF16)


def turn_in(order, load, stage):
    count = stage.shape[0]
    for k in range(0, count, 2):
        if k + 1 < count:
            both = dot(order, jnp.concatenate([load(k), load(k + 1)], axis=1))
            stage[k] = both[:, :128]
            stage[k + 1] = both[:, 128:]
        else:
            stage[k] = dot(order, load(k))


def turn_out(order, stage, store):
    count = stage.shape[0]
    for k in range(0, count, 2):
        if k + 1 < count:
            both = jnp.concatenate([stage[k].astype(BF16), stage[k + 1].astype(BF16)], axis=1)
            both = dot(order, both).astype(BF16)
            store(k, both[:, :128])
            store(k + 1, both[:, 128:])
        else:
            store(k, dot(order, stage[k].astype(BF16)).astype(BF16))


def staged(stage, c, slot):
    row = (2 * c + slot) * 8
    return jnp.concatenate([stage[k, row : row + 8, :] for k in range(stage.shape[0])], axis=0)


def put_staged(stage, c, slot, value):
    row = (2 * c + slot) * 8
    for k in range(stage.shape[0]):
        stage[k, row : row + 8, :] = value[8 * k : 8 * k + 8]


def cast_rows(value_ref, wb_ref, row, square):
    step = 64

    def add(k, square):
        value = value_ref[pl.ds(pl.multiple_of(k * step, step), step), :]
        wb_ref[pl.ds(pl.multiple_of(row + k * step, step), step), :] = value.astype(BF16)
        return square + jnp.sum((value * value).reshape(step // 8, 8, value.shape[1]), axis=0)

    return lax.fori_loop(0, value_ref.shape[0] // step, add, square)


def reduce_scratch(n, w, rows, channels):
    return [
        VMEM((n, rows, channels), F32),
        VMEM((w, rows, channels), F32),
        pltpu.SemaphoreType.DMA((n,)),
        pltpu.SemaphoreType.DMA((n,)),
        pltpu.SemaphoreType.DMA((w,)),
        pltpu.SemaphoreType.DMA((w,)),
    ]


def greet(n, w):
    me_n, me_w = lax.axis_index("narrow"), lax.axis_index("wide")
    barrier = pltpu.get_barrier_semaphore()
    for k in range(1, n):
        pl.semaphore_signal(
            barrier, inc=1, device_id={"narrow": lax.rem(me_n + k, n)}, device_id_type=MESH
        )
    for k in range(1, w):
        pl.semaphore_signal(
            barrier, inc=1, device_id={"wide": lax.rem(me_w + k, w)}, device_id_type=MESH
        )


def met(n, w):
    pl.semaphore_wait(pltpu.get_barrier_semaphore(), n + w - 2)


def sum_over(axis, size, value, slots, send, recv):
    me = lax.axis_index(axis)
    slots[me] = value
    copies = []
    for k in range(1, size):
        copy = pltpu.make_async_remote_copy(
            src_ref=slots.at[me],
            dst_ref=slots.at[me],
            send_sem=send.at[k],
            recv_sem=recv.at[k],
            device_id={axis: lax.rem(me + k, size)},
            device_id_type=MESH,
        )
        copy.start()
        copies.append(copy)
    for copy in copies:
        copy.wait_recv()
    total = slots[0]
    for k in range(1, size):
        total = total + slots[k]
    for copy in copies:
        copy.wait_send()
    return total


class SumAll:
    def __init__(self, n, w, scratch):
        self.axes = (("narrow", n, scratch[0], *scratch[2:4]), ("wide", w, scratch[1], *scratch[4:6]))
        self.copies = [[], []]

    def send(self, which, value):
        axis, size, slots, send, recv = self.axes[which]
        me = lax.axis_index(axis)
        slots[me] = value
        for k in range(1, size):
            copy = pltpu.make_async_remote_copy(
                src_ref=slots.at[me],
                dst_ref=slots.at[me],
                send_sem=send.at[k],
                recv_sem=recv.at[k],
                device_id={axis: lax.rem(me + k, size)},
                device_id_type=MESH,
            )
            copy.start()
            self.copies[which].append(copy)

    def total(self, which):
        _, size, slots, _, _ = self.axes[which]
        for copy in self.copies[which]:
            copy.wait_recv()
        total = slots[0]
        for k in range(1, size):
            total = total + slots[k]
        return total

    def begin(self, value):
        self.send(0, value)

    def middle(self):
        self.send(1, self.total(0))

    def end(self):
        total = self.total(1)
        for copies in self.copies:
            for copy in copies:
                copy.wait_send()
        return total


def forward_scale(stats, params, number):
    mean = stats[0:1] / number
    scale = lax.rsqrt(stats[1:2] / number - mean * mean + EPS)
    a = scale * params[0]
    return a, params[1] - mean * a, scale, mean


def backward_scale(stats, params, grads, number):
    mean = stats[0:1] / number
    scale = lax.rsqrt(stats[1:2] / number - mean * mean + EPS)
    a = scale * params[0]
    gain_grad, bias_grad = grads[0:1], grads[1:2]
    over = a / number
    return a, over * scale * gain_grad, over * (bias_grad - mean * scale * gain_grad)


def norm_params(gain_ref, bias_ref, which, inner):
    lane = (0, inner, 2 * inner, gain_ref.shape[1])
    at = slice(lane[which], lane[which + 1])
    return gain_ref[0:1, at], bias_ref[0:1, at]


def second_counts(counts_ref, g):
    return jnp.where(counts_ref[g] == 2, 1.0, 0.0)


def two_sums(first, second, m):
    return jnp.sum(first, axis=(0, 1))[None] + m * jnp.sum(second, axis=(0, 1))[None]


def padded_rows(count):
    return -(-count // 16) * 16


def halo_rows(images):
    starts, at = [], 0
    for g in range(3):
        starts.append(at)
        at += padded_rows(COLUMNS[g] * images)
    return starts, at


def pack_halo(value):
    count = value.shape[0] * value.shape[1]
    value = value.reshape(count, value.shape[2])
    extra = padded_rows(count) - count
    if extra:
        value = jnp.concatenate([value, jnp.zeros((extra, value.shape[1]), F32)], axis=0)
    return value.astype(BF16)


def unpack_halo(value, columns, images):
    return value.astype(F32)[: columns * images].reshape(columns, images, value.shape[1])


def halo_copies(n, g, count, starts, up_src, up_dst, down_src, down_dst, sems):
    me = lax.axis_index("narrow")
    rows = pl.ds(starts[g], count)
    forward = pltpu.make_async_remote_copy(
        src_ref=up_src.at[rows],
        dst_ref=up_dst.at[rows],
        send_sem=sems.at[0, g],
        recv_sem=sems.at[1, g],
        device_id={"narrow": lax.rem(me + 1, n)},
        device_id_type=MESH,
    )
    backward = pltpu.make_async_remote_copy(
        src_ref=down_src.at[rows],
        dst_ref=down_dst.at[rows],
        send_sem=sems.at[2, g],
        recv_sem=sems.at[3, g],
        device_id={"narrow": lax.rem(me + n - 1, n)},
        device_id_type=MESH,
    )
    return forward, backward


def halo_start(n, copies):
    me = lax.axis_index("narrow")

    @pl.when(me < n - 1)
    def _():
        copies[0].start()

    @pl.when(me > 0)
    def _():
        copies[1].start()


def halo_arrived(n, copies):
    me = lax.axis_index("narrow")

    @pl.when(me > 0)
    def _():
        copies[0].wait_recv()

    @pl.when(me < n - 1)
    def _():
        copies[1].wait_recv()


def halo_sent(n, copies):
    me = lax.axis_index("narrow")

    @pl.when(me < n - 1)
    def _():
        copies[0].wait_send()

    @pl.when(me > 0)
    def _():
        copies[1].wait_send()


def halo_edges(n, from_before, from_after):
    me = lax.axis_index("narrow")

    @pl.when(me == 0)
    def _():
        from_before[...] = jnp.zeros(from_before.shape, from_before.dtype)

    @pl.when(me == n - 1)
    def _():
        from_after[...] = jnp.zeros(from_after.shape, from_after.dtype)


RING = BLOCKS
CHUNK = 512


def turn(source, columns, target):
    for k in range(source.shape[0] // 128):
        target[:, k * 128 : (k + 1) * 128] = source[k * 128 : (k + 1) * 128, columns].T


def place_of(t):
    g = (t >= FIRST[1]).astype(jnp.int32) + (t >= FIRST[2]).astype(jnp.int32)
    return g, t - jnp.where(g == 0, FIRST[0], jnp.where(g == 1, FIRST[1], FIRST[2]))


def forward_kernel(
    n, w, number, x_ref, reduce_ref, spatial_ref, expand_ref, gain_ref, bias_ref, counts_ref,
    rows_out, one_out, two_out, upper_out, middle_out, lower_out, hidden_out, three_out, inner_out, outer_out,
    reduce_out, spatial_out, expand_out,
    stat_one, stat_two, stat_three, hidden_sum, square_reduce, square_spatial, square_expand,
    ring, rows, weight, wide_weight, reduce, spatial, expand, one, two, upper, middle, lower, hidden, three,
    turned, inner,
    last, first, above, below, halo_sems, ring_sems, weight_sems, wide_sem, out_sems,
    *scratch,
):
    m = [second_counts(counts_ref, g) for g in range(3)]
    sum_one = SumAll(n, w, scratch[:6])
    sum_two = SumAll(n, w, scratch[6:12])
    sum_three = SumAll(n, w, scratch[12:18])
    images = x_ref.shape[1]
    lanes = x_ref.shape[3] // 2
    channels = one.shape[3]
    block = 2 * images
    tail = BLOCKS * block
    starts, _ = halo_rows(images)
    outs = []

    def put(source, target):
        copy = pltpu.make_async_copy(source, target, out_sems.at[len(outs)])
        copy.start()
        outs.append(copy)

    def fetch(t):
        g, j = place_of(t)
        slot = lax.rem(t, RING)
        return pltpu.make_async_copy(x_ref.at[g, :, j], ring.at[slot], ring_sems.at[slot])

    sources = [reduce_ref.at[k : k + CHUNK] for k in range(0, reduce_ref.shape[0], CHUNK)]
    reduce_chunks = len(sources)
    sources += [spatial_ref.at[k : k + CHUNK] for k in range(0, spatial_ref.shape[0], CHUNK)]
    slots = weight.shape[0]

    def weight_copy(k):
        return pltpu.make_async_copy(sources[k], weight.at[k % slots], weight_sems.at[k % slots])

    for t in range(RING):
        fetch(jnp.int32(t)).start()
    for k in range(slots):
        weight_copy(k).start()
    wide_copy = pltpu.make_async_copy(expand_ref, wide_weight, wide_sem)
    greet(n, w)
    rows[tail:, :] = jnp.zeros((rows.shape[0] - tail, rows.shape[1]), BF16)
    three[tail:, :] = jnp.zeros((three.shape[0] - tail, three.shape[1]), BF16)
    for ref in (upper, middle, lower):
        for at in (0, PADDED[1] - 1, PADDED[2] - 1, PADDED_BLOCKS - 1):
            ref[at * block : (at + 1) * block] = jnp.zeros((block, channels), BF16)
    halo_edges(n, above, below)

    def cast_chunk(k, wb_ref, row, square):
        weight_copy(k).wait()
        square = cast_rows(weight.at[k % slots], wb_ref, row, square)
        if k + slots < len(sources):
            weight_copy(k + slots).start()
        return square

    def place(i, _):
        for k in range(2):
            fetch(2 * i + k).wait()
        for k in range(2):
            slot = lax.rem(2 * i + k, RING)
            row = pl.multiple_of((2 * i + k) * block, block)
            for group in range(lanes // 4):
                values = turned_in(lambda j: ring[slot, 8 * j : 8 * j + 8], images // 8, group)
                for c in range(4):
                    at = (4 * group + c) * 128
                    rows[pl.ds(row, block), at : at + 128] = values[c].astype(BF16)

        @pl.when(2 * i + RING < BLOCKS)
        def _():
            for k in range(2):
                fetch(2 * i + k + RING).start()

        return 0

    lax.fori_loop(0, BLOCKS // 2, place, 0)
    wide_copy.start()
    put(rows, rows_out)
    square = jnp.zeros((8, channels), F32)
    for k in range(reduce_chunks):
        square = cast_chunk(k, reduce, k * CHUNK, square)
    square_reduce[...] = jnp.sum(square, axis=0, keepdims=True)
    put(reduce, reduce_out)
    sums = jnp.zeros((1, channels), F32)
    squares = jnp.zeros((1, channels), F32)
    for g in range(3):
        at = slice(FIRST[g] * block, (FIRST[g] + COLUMNS[g]) * block)
        c = dot(rows[at, :], reduce[...]).reshape(COLUMNS[g], 2, images, channels)
        one[FIRST[g] : FIRST[g] + COLUMNS[g]] = c
        sums = sums + two_sums(c[:, 0], c[:, 1], m[g])
        squares = squares + two_sums(c[:, 0] * c[:, 0], c[:, 1] * c[:, 1], m[g])
    met(n, w)
    sum_one.begin(jnp.concatenate([sums, squares], axis=0))
    put(one, one_out)
    square = jnp.zeros((8, channels), F32)
    middle_chunk = (reduce_chunks + len(sources)) // 2
    for k in range(reduce_chunks, middle_chunk):
        square = cast_chunk(k, spatial, (k - reduce_chunks) * CHUNK, square)
    for g in range(3):
        value = one[FIRST[g] : FIRST[g] + COLUMNS[g]]
        value = jnp.stack([value[:, 0], value[:, 1] * m[g]], axis=1)
        hidden[FIRST[g] * block : (FIRST[g] + COLUMNS[g]) * block] = value.reshape(
            COLUMNS[g] * block, channels
        ).astype(BF16)
    hidden[tail:] = jnp.zeros((hidden.shape[0] - tail, channels), BF16)
    sum_one.middle()
    turn(hidden, slice(0, channels), turned.at[:channels])
    lane = lax.broadcasted_iota(jnp.int32, (16, turned.shape[1]), 1)
    place = lax.div(lane, block)
    flag = jnp.where(place < FIRST[1], m[0], jnp.where(place < FIRST[2], m[1], m[2]))
    flag = jnp.where(lax.rem(lane, block) < images, 1.0, flag)
    turned[channels:] = jnp.where(lane < tail, flag, 0.0).astype(BF16)

    def inner_chunk(k):
        at = slice(k * 256, (k + 1) * 256)
        inner[:, at] = dot(turned[...], rows[:, at])

    inner_chunks = rows.shape[1] // 256
    for k in range(middle_chunk, len(sources)):
        square = cast_chunk(k, spatial, (k - reduce_chunks) * CHUNK, square)
    for k in range(inner_chunks // 4):
        inner_chunk(k)
    square_spatial[...] = jnp.sum(square, axis=0, keepdims=True)
    put(spatial, spatial_out)
    stats = sum_one.end()
    stat_one[...] = stats

    a, b, _, _ = forward_scale(stats, norm_params(gain_ref, bias_ref, 0, channels), number)
    copies = []
    for g in range(3):
        v = one[FIRST[g] : FIRST[g] + COLUMNS[g]] * a + b
        value = v * half_of(v)[0]
        slot_one, slot_two = value[:, 0], value[:, 1] * m[g]
        count = padded_rows(COLUMNS[g] * images)
        first[starts[g] : starts[g] + count] = pack_halo(slot_one)
        last[starts[g] : starts[g] + count] = pack_halo(
            jnp.where(m[g] > 0.5, slot_two, slot_one)
        )
        copies.append(halo_copies(n, g, count, starts, last, above, first, below, halo_sems))
        halo_start(n, copies[g])
        both = jnp.stack([slot_one, slot_two], axis=1).reshape(COLUMNS[g] * block, channels)
        middle[PADDED[g] * block : (PADDED[g] + COLUMNS[g]) * block] = both.astype(BF16)

    def taps(ref, g, level):
        at, count = PADDED[g] * block, COLUMNS[g] * block
        shifted = [ref[at + d * block : at + d * block + count, :] for d in (-1, 0, 1)]
        return dot(
            jnp.concatenate(shifted, axis=1),
            spatial[3 * level * channels : 3 * (level + 1) * channels, :],
        )

    def put_groups(source, target):
        for g in range(3):
            count = COLUMNS[g] * block
            put(
                source.at[PADDED[g] * block : PADDED[g] * block + count],
                target.at[FIRST[g] * block : FIRST[g] * block + count],
            )

    for g in range(3):
        two[FIRST[g] : FIRST[g] + COLUMNS[g]] = taps(middle, g, 1).reshape(
            COLUMNS[g], 2, images, channels
        )
    put_groups(middle, middle_out)
    sums = jnp.zeros((1, channels), F32)
    squares = jnp.zeros((1, channels), F32)
    for g in range(3):
        halo_arrived(n, copies[g])
        at, count = PADDED[g] * block, COLUMNS[g] * block
        height = padded_rows(COLUMNS[g] * images)
        up = unpack_halo(above[starts[g] : starts[g] + height], COLUMNS[g], images)
        down = unpack_halo(below[starts[g] : starts[g] + height], COLUMNS[g], images)
        own = middle[at : at + count].astype(F32).reshape(COLUMNS[g], 2, images, channels)
        upper[at : at + count] = (
            jnp.stack([up, own[:, 0]], axis=1).reshape(count, channels).astype(BF16)
        )
        lower[at : at + count] = (
            jnp.stack([jnp.where(m[g] > 0.5, own[:, 1], down), down], axis=1)
            .reshape(count, channels)
            .astype(BF16)
        )
        c = taps(upper, g, 0) + taps(lower, g, 2)
        c = c.reshape(COLUMNS[g], 2, images, channels) + two[FIRST[g] : FIRST[g] + COLUMNS[g]]
        two[FIRST[g] : FIRST[g] + COLUMNS[g]] = c
        sums = sums + two_sums(c[:, 0], c[:, 1], m[g])
        squares = squares + two_sums(c[:, 0] * c[:, 0], c[:, 1] * c[:, 1], m[g])
    sum_two.begin(jnp.concatenate([sums, squares], axis=0))
    put(two, two_out)
    put_groups(upper, upper_out)
    put_groups(lower, lower_out)
    wide_copy.wait()
    half = wide_weight.shape[0] // 2
    square = jnp.zeros((8, wide_weight.shape[1]), F32)
    square = cast_rows(wide_weight.at[:half], expand, 0, square)
    for k in range(inner_chunks // 4, inner_chunks // 2):
        inner_chunk(k)
    sum_two.middle()
    square = cast_rows(wide_weight.at[half:], expand, half, square)
    square_expand[...] = jnp.sum(square, axis=0, keepdims=True)
    put(expand, expand_out)
    for k in range(inner_chunks // 2, inner_chunks):
        inner_chunk(k)
    put(inner, inner_out)
    inner_done = outs[-1]
    for g in range(3):
        halo_sent(n, copies[g])
    stats = sum_two.end()
    stat_two[...] = stats

    a, b, _, _ = forward_scale(stats, norm_params(gain_ref, bias_ref, 1, channels), number)
    sums = jnp.zeros((1, channels), F32)
    for g in range(3):
        v = two[FIRST[g] : FIRST[g] + COLUMNS[g]] * a + b
        value = v * half_of(v)[0]
        both = jnp.stack([value[:, 0], value[:, 1] * m[g]], axis=1)
        sums = sums + jnp.sum(both, axis=(0, 1, 2))[None]
        hidden[FIRST[g] * block : (FIRST[g] + COLUMNS[g]) * block] = both.reshape(
            COLUMNS[g] * block, channels
        ).astype(BF16)
    hidden_sum[...] = sums
    put(hidden.at[:tail], hidden_out.at[:tail])
    sums, squares = [], []
    for part in range(three.shape[1] // 512):
        s = jnp.zeros((1, 512), F32)
        q = jnp.zeros((1, 512), F32)
        columns = slice(part * 512, (part + 1) * 512)
        for g in range(3):
            at = slice(FIRST[g] * block, (FIRST[g] + COLUMNS[g]) * block)
            c = dot(hidden[at, :], expand[:, columns])
            three[at, columns] = c.astype(BF16)
            s = s + jnp.sum(c, axis=0, keepdims=True)
            q = q + jnp.sum(c * c, axis=0, keepdims=True)
        put(three.at[:tail, columns], three_out.at[:, columns])
        sums.append(s)
        squares.append(q)
    sum_three.begin(
        jnp.concatenate(
            [jnp.concatenate(sums, axis=1), jnp.concatenate(squares, axis=1)], axis=0
        )
    )
    turn(hidden, slice(0, channels), turned.at[:channels])
    inner_done.wait()
    outs = [copy for copy in outs if copy is not inner_done]

    def outer_chunk(k):
        at = slice(k * 256, (k + 1) * 256)
        inner[:channels, at] = dot(turned[:channels], three[:, at])

    for k in range(inner_chunks // 4):
        outer_chunk(k)
    sum_three.middle()
    for k in range(inner_chunks // 4, inner_chunks):
        outer_chunk(k)
    put_last = pltpu.make_async_copy(inner.at[:channels], outer_out, out_sems.at[31])
    put_last.start()
    stat_three[...] = sum_three.end()
    for copy in outs:
        copy.wait()
    put_last.wait()


DEPTH = 10
AHEAD = DEPTH - 2


def top_kernel(
    number, inner, conv_ref, rows_ref, up_ref, stats_ref, gain_ref, bias_ref, counts_ref,
    out_ref, grad_ref, total,
    conv_ring, rows_ring, up_ring, out_ring, grad_ring, up_one, up_two, out_one, out_two, order, coefficients, sems,
):
    images = up_ref.shape[1]
    lanes = up_ref.shape[3] // 2
    block = 2 * images

    def rows_of(t):
        return pl.ds(pl.multiple_of(t * block, block), block)

    def copy(which, t):
        slot = lax.rem(t, DEPTH)
        g, j = place_of(t)
        source, target = (
            lambda: (conv_ref.at[rows_of(t)], conv_ring.at[slot]),
            lambda: (rows_ref.at[rows_of(t)], rows_ring.at[slot]),
            lambda: (up_ref.at[g, :, j], up_ring.at[slot]),
            lambda: (out_ring.at[slot], out_ref.at[g, :, j]),
            lambda: (grad_ring.at[slot], grad_ref.at[rows_of(t)]),
        )[which]()
        return pltpu.make_async_copy(source, target, sems.at[which, slot])

    def each(which, t, do):
        @pl.when((t >= 0) & (t < BLOCKS))
        def _():
            do(copy(which, t))

    def start(which, t):
        each(which, t, lambda c: c.start())

    def wait(which, t):
        each(which, t, lambda c: c.wait())

    for t in range(AHEAD + 1):
        start(2, jnp.int32(t))
        if t < AHEAD:
            start(0, jnp.int32(t))
            start(1, jnp.int32(t))
    total[...] = jnp.zeros(total.shape, F32)
    params = norm_params(gain_ref, bias_ref, 2, inner)
    a, b, scale, mean = forward_scale(stats_ref[...], params, number)
    coefficients[0:1] = a
    coefficients[1:2] = b
    order[0] = to_rows(lanes)
    order[1] = from_rows(lanes)
    out_two[...] = jnp.zeros(out_two.shape, F32)

    def enter(t, stage):
        slot = lax.rem(t, DEPTH)
        turn_in(
            order[0], lambda k: up_ring[slot, 8 * k : 8 * k + 8].reshape(16 * lanes, 128), stage
        )

    def leave(t, stage):
        slot = lax.rem(t + DEPTH, DEPTH)

        def store(k, value):
            out_ring[slot, 8 * k : 8 * k + 8] = value.reshape(8, 2 * lanes, 128)

        turn_out(order[1], stage, store)

    def work(t, stage_up, stage_out):
        slot = lax.rem(t, DEPTH)
        m = second_counts(counts_ref, place_of(t)[0])
        for c in range(lanes):
            at = slice(c * 128, (c + 1) * 128)
            raw = conv_ring[slot, :, at].astype(F32)
            v = raw * coefficients[0:1, at] + coefficients[1:2, at]
            v = v + rows_ring[slot, :, at].astype(F32)
            h, squared = half_of(v)
            out = v * h
            slope = h + out * (1.0 - h) * (2.0 * C0 + 6.0 * C1 * squared)
            put_staged(stage_out, c, 0, out[:images])
            put_staged(stage_out, c, 1, out[images:] * m)
            grad = jnp.concatenate(
                [
                    slope[:images] * staged(stage_up, c, 0),
                    slope[images:] * (staged(stage_up, c, 1) * m),
                ],
                axis=0,
            )
            grad_ring[slot, :, at] = grad.astype(BF16)
            total[0, :, at] += jnp.sum((grad * raw).reshape(block // 8, 8, 128), axis=0)
            total[1, :, at] += jnp.sum(grad.reshape(block // 8, 8, 128), axis=0)

    wait(2, jnp.int32(0))
    enter(jnp.int32(0), up_one)

    def pair(i, _):
        t = 2 * i
        for k in (0, 1):
            start(0, t + AHEAD + k)
            start(1, t + AHEAD + k)
            start(2, t + AHEAD + k + 1)
        for k in (0, 1):
            wait(0, t + k)
            wait(1, t + k)
            wait(2, t + k + 1)
            wait(3, t + k - 1 - DEPTH)
            wait(4, t + k - DEPTH)
        enter(t + 1, up_two)
        work(t, up_one, out_one)
        leave(t - 1, out_two)
        enter(t + 2, up_one)
        work(t + 1, up_two, out_two)
        leave(t, out_one)
        for k in (0, 1):
            start(3, t + k - 1)
            start(4, t + k)
        return 0

    lax.fori_loop(0, BLOCKS // 2, pair, 0)
    last = jnp.int32(BLOCKS - 1)
    wait(3, last - DEPTH)
    leave(last, out_two)
    start(3, last)
    for k in range(DEPTH):
        wait(3, last - k)
        wait(4, last - k)
    out_ring[0] = jnp.zeros(out_ring.shape[1:], BF16)
    copies = []
    for g in range(3):
        for j in range(COLUMNS[g], out_ref.shape[2]):
            copies.append(
                pltpu.make_async_copy(
                    out_ring.at[0], out_ref.at[g, :, j], sems.at[5, len(copies)]
                )
            )
            copies[-1].start()
    value = jnp.sum(total[...], axis=1)
    gains = scale * (value[0:1] - mean * value[1:2])
    total[0] = jnp.concatenate([gains, jnp.zeros((7, gains.shape[1]), F32)], axis=0)
    for copy in copies:
        copy.wait()


def unravel(index, sizes):
    digits = []
    for size in reversed(sizes):
        digits.append(index % size if isinstance(index, int) else lax.rem(index, size))
        index = index // size if isinstance(index, int) else lax.div(index, size)
    return digits[::-1]


def mesh_digits(n, w):
    if (n, w) == (4, 8):
        return (
            [("narrow", 2, 2), ("narrow", 1, 2), ("wide", 2, 4), ("wide", 1, 2)],
            [(1, 3, 0, 2), (1, 0, 3, 2)],
        )
    return [("narrow", 1, n), ("wide", 1, w)], [(0, 1), (0, 1)]


def digit_sizes(n, w):
    return [d[2] for d in mesh_digits(n, w)[0]]


def narrow_digits(n, w):
    return [d[2] for d in mesh_digits(n, w)[0] if d[0] == "narrow"]


def wide_digits(n, w):
    return [d[2] for d in mesh_digits(n, w)[0] if d[0] == "wide"]


def weight_parts(w, rows):
    share = rows // w
    if rows >= 4096 and share % 64 == 0:
        return 4
    return 2 if share % 32 == 0 else 1


def block_shapes(n, w, rows, columns):
    parts = weight_parts(w, rows)
    return [(*digit_sizes(n, w), rows // w // parts, columns // n)] * parts


def put_blocks(n, w, refs, value, row, rows, place_n=None, place_w=0, lane=0):
    share = rows // w
    part = share // len(refs)
    at, end = row, row + value.shape[0]
    columns = refs[0].shape[-1]
    while at < end:
        stop = min(end, (at // part + 1) * part)
        wide = at // share
        ref = refs[at // part % len(refs)]
        inside = slice(at % part, at % part + stop - at)
        piece = value[at - row : stop - row]
        wide = unravel(place_w + wide, wide_digits(n, w))
        if place_n is not None:
            lanes = slice(lane, lane + piece.shape[1])
            ref[(*unravel(place_n, narrow_digits(n, w)), *wide, inside, lanes)] = piece.astype(BF16)
        else:
            for k in range(n):
                ref[(*unravel(k, narrow_digits(n, w)), *wide, inside, slice(None))] = piece[
                    :, k * columns : (k + 1) * columns
                ].astype(BF16)
        at = stop


def scatter_scratch(n, w, rows, columns):
    digits, orders = mesh_digits(n, w)
    scratch = []
    for part, shape in enumerate(block_shapes(n, w, rows, columns)):
        left = list(range(len(digits)))
        for d in orders[part % 2]:
            left.remove(d)
            size = digits[d][2]
            scratch.append(VMEM((size - 1, *(digits[k][2] for k in left), *shape[-2:]), BF16))
            scratch.append(pltpu.SemaphoreType.DMA((size - 1,)))
            scratch.append(pltpu.SemaphoreType.DMA((size - 1,)))
    return scratch


class Scatter:
    def __init__(self, n, w, source, scratch, order):
        self.digits = mesh_digits(n, w)[0]
        self.order = order
        self.scratch = scratch
        self.sources = [source] + [scratch[3 * k].at[0] for k in range(len(order))]
        self.copies = []
        self.steps = len(order)

    def own(self, d):
        axis, stride, size = self.digits[d]
        return lax.rem(lax.div(lax.axis_index(axis), stride), size)

    def pick(self, ref, step, value):
        left = [d for d in range(len(self.digits)) if d not in self.order[:step]]
        return ref.at[tuple(value if d == self.order[step] else slice(None) for d in left)]

    def start(self, step):
        d = self.order[step]
        axis, stride, size = self.digits[d]
        landing, send, recv = self.scratch[3 * step : 3 * step + 3]
        mine = self.own(d)
        for k in range(1, size):
            other = lax.rem(mine + k, size)
            copy = pltpu.make_async_remote_copy(
                src_ref=self.pick(self.sources[step], step, other),
                dst_ref=landing.at[k - 1],
                send_sem=send.at[k - 1],
                recv_sem=recv.at[k - 1],
                device_id={axis: lax.axis_index(axis) + (other - mine) * stride},
                device_id_type=MESH,
            )
            copy.start()
            self.copies.append((step, copy))

    def finish(self, step):
        for at, copy in self.copies:
            if at == step:
                copy.wait_recv()
        d = self.order[step]
        size = self.digits[d][2]
        landing = self.scratch[3 * step]
        left = [k for k in range(len(self.digits)) if k not in self.order[: step + 1]]
        sizes = [self.digits[k][2] for k in left]
        mine = self.own(d)
        source = self.pick(self.sources[step], step, mine)

        def total(at):
            value = source[at].astype(F32)
            for k in range(size - 1):
                value = value + landing[(k, *at)].astype(F32)
            return value

        if step == self.steps - 1:
            return total((slice(None), slice(None)))
        count = 1
        for k in sizes:
            count *= k

        together = 4 if count % 4 == 0 else 1

        def add(index, _):
            for k in range(together):
                at = tuple(unravel(index * together + k, sizes))
                landing[(0, *at)] = total(at).astype(BF16)
            return 0

        lax.fori_loop(0, count // together, add, 0)

    def done(self):
        for _, copy in self.copies:
            copy.wait_send()


def share_out(n, slots, value, send, recv):
    me = lax.axis_index("narrow")
    row = 0
    for piece in value:
        slots[me, row : row + piece.shape[0]] = piece.astype(BF16)
        row += piece.shape[0]
    copies = []
    for k in range(1, n):
        copy = pltpu.make_async_remote_copy(
            src_ref=slots.at[me],
            dst_ref=slots.at[me],
            send_sem=send.at[k],
            recv_sem=recv.at[k],
            device_id={"narrow": lax.rem(me + k, n)},
            device_id_type=MESH,
        )
        copy.start()
        copies.append(copy)
    return copies


BETA = 1.0 - STEP ** (-0.8)


class Refs:
    def __init__(self, refs):
        self.refs = list(refs)

    def take(self, count):
        taken, self.refs = self.refs[:count], self.refs[count:]
        return taken

    def one(self):
        return self.take(1)[0]


def backward_kernel(
    n, w, number, shapes, three_ref, grad_ref, hidden_ref, expand_ref, two_ref, spatial_ref,
    upper_ref, middle_ref, lower_ref, one_ref, rows_ref, reduce_ref, inner_ref, outer_ref, sums_ref, hidden_sum, stat_one, stat_two, stat_three,
    gain_ref, bias_ref, counts_ref, reduce_rows_ref, spatial_rows_ref, expand_rows_ref, *refs,
):
    refs = Refs(refs)
    parts = [weight_parts(w, shape[0]) for shape in shapes]
    input_ref, columns_ref = refs.take(2)
    shares = refs.take(3)
    norm_one, norm_two, norm_three = refs.take(3)
    three, wide, hidden, turned, expand, spatial, two, one, u, coefficients = refs.take(10)
    inner_ring, inner_sems = refs.take(2)
    to_before, to_after, from_after, from_before, halo_sems, in_sems = refs.take(6)
    gradients = [refs.take(parts[k]) for k in range(3)]
    orders = mesh_digits(n, w)[1]
    steps = len(orders[0])
    scatters = [
        [
            Scatter(n, w, gradients[k][p], refs.take(3 * steps), orders[p % 2])
            for p in range(parts[k])
        ]
        for k in range(3)
    ]
    share_sems = [refs.take(2) for _ in range(3)]
    sum_three = SumAll(n, w, refs.take(6))
    sum_two = SumAll(n, w, refs.take(6))
    sum_one = SumAll(n, w, refs.take(6))
    column_scratch = refs.take(3)

    images = two.shape[2]
    channels = two.shape[3]
    block = 2 * images
    tail = BLOCKS * block
    deep = three.shape[0]
    m = [second_counts(counts_ref, g) for g in range(3)]
    starts, _ = halo_rows(images)

    ins = {}

    def get(name, source, target):
        ins[name] = pltpu.make_async_copy(source, target, in_sems.at[len(ins)])
        ins[name].start()

    get("hidden", hidden_ref.at[:tail], hidden.at[:tail])
    get("grad", grad_ref, wide.at[:tail])
    get("three", three_ref, three.at[:tail])
    get("expand", expand_ref, expand)
    get("two", two_ref, two)
    get("one", one_ref, one)
    greet(n, w)

    def norm_scale(which, stat, grads):
        params = norm_params(gain_ref, bias_ref, which, channels)
        return backward_scale(stat[...], params, grads, number)

    sent = {}

    def advance(which, step, half=None):
        if step >= steps:
            return
        count = parts[which]
        if half is not None and count == 1:
            if half == 0:
                return
            half = None
        first = 0 if half is None else half * (count // 2)
        last = count if half is None else first + count // 2
        for scatter in scatters[which][first:last]:
            value = scatter.finish(step)
            if step < steps - 1:
                scatter.start(step + 1)
            else:
                sent.setdefault(which, []).append(value)
        if step == steps - 1 and last == count:
            sent[which] = share_out(n, shares[which], sent[which], *share_sems[which])

    def launch(which):
        for scatter in scatters[which]:
            scatter.start(0)

    value = jnp.concatenate(
        [sums_ref[0, 0:1], jnp.sum(sums_ref[1], axis=0, keepdims=True)],
        axis=0,
    )
    halo_edges(n, from_before, from_after)
    wide[tail:, :] = jnp.zeros((deep - tail, wide.shape[1]), BF16)
    hidden[tail:deep] = jnp.zeros((deep - tail, channels), BF16)
    met(n, w)
    sum_three.begin(value)
    ins["hidden"].wait()
    turn(hidden.at[:deep], slice(0, channels), turned.at[0])
    ins["grad"].wait()

    def held(k):
        return (k // 6, slice(None), slice(k % 6 * 256, (k % 6 + 1) * 256))

    inner_chunks = wide.shape[1] // 256

    def raw_chunk(k):
        value = dot(turned[0], wide[:, k * 256 : (k + 1) * 256])
        high = value.astype(BF16)
        spatial[held(k)] = high
        spatial[held(inner_chunks + k)] = (value - high.astype(F32)).astype(BF16)

    def raw_value(k):
        return spatial[held(k)].astype(F32) + spatial[held(inner_chunks + k)].astype(F32)

    def inner_copy(ref, k):
        return pltpu.make_async_copy(
            ref.at[:, k * 256 : (k + 1) * 256],
            inner_ring.at[k % 2, : ref.shape[0]],
            inner_sems.at[k % 2],
        )

    def column(value):
        return jnp.broadcast_to(value, (128, channels)).T[:, 0:1]

    for k in range(2):
        raw_chunk(k)
    sum_three.middle()
    for k in range(2, inner_chunks):
        raw_chunk(k)
    for k in range(2):
        inner_copy(outer_ref, k).start()
    ins["three"].wait()
    ins["expand"].wait()
    grads = sum_three.end()
    norm_three[...] = grads
    a, b, c = norm_scale(2, stat_three, grads)
    coefficients[0:1] = a
    coefficients[1:2] = b
    coefficients[2:3] = c
    def back_three(g):
        rows = slice(FIRST[g] * block, (FIRST[g] + COLUMNS[g]) * block)
        for k in range(inner_chunks):
            at = slice(k * 256, (k + 1) * 256)
            a, b, c = coefficients[0:1, at], coefficients[1:2, at], coefficients[2:3, at]
            up = wide[rows, at].astype(F32) * a
            raw = (three[rows, at].astype(F32) * b + c).reshape(COLUMNS[g], 2, images, 256)
            raw = jnp.stack([raw[:, 0], raw[:, 1] * m[g]], axis=1).reshape(up.shape)
            wide[rows, at] = (up - raw).astype(BF16)

    ins["two"].wait()
    a, b, scale, mean = forward_scale(
        stat_two[...], norm_params(gain_ref, bias_ref, 1, channels), number
    )
    sums = jnp.zeros((1, channels), F32)
    gains = jnp.zeros((1, channels), F32)
    back_three(0)
    for g in range(3):
        if g < 2:
            back_three(g + 1)
        blocks = slice(FIRST[g], FIRST[g] + COLUMNS[g])
        raw = two[blocks]
        v = raw * a + b
        rows = slice(FIRST[g] * block, (FIRST[g] + COLUMNS[g]) * block)
        value = slope_of(v, *half_of(v)) * dot_t(wide[rows, :], expand[...]).reshape(raw.shape)
        value = jnp.stack([value[:, 0], value[:, 1] * m[g]], axis=1)
        u[blocks] = value
        sums = sums + jnp.sum(value, axis=(0, 1, 2))[None]
        gains = gains + jnp.sum(value * ((raw - mean) * scale), axis=(0, 1, 2))[None]
    for k, source in enumerate((upper_ref, middle_ref, lower_ref)):
        get(k, source.at[:tail], wide.at[:tail, k * channels : (k + 1) * channels])
    sum_two.begin(jnp.concatenate([gains, sums], axis=0))
    for at in (0, PADDED[1] - 1, PADDED[2] - 1, PADDED_BLOCKS - 1):
        hidden[at * block : (at + 1) * block] = jnp.zeros((block, channels), BF16)
    per = inner_chunks // n
    sum_column = column(hidden_sum[...])

    def expand_chunk(k):
        at = slice(k * 256, (k + 1) * 256)
        a, b, c = coefficients[0:1, at], coefficients[1:2, at], coefficients[2:3, at]
        inner_copy(outer_ref, k).wait()
        value = raw_value(k) * a - inner_ring[k % 2, :channels] * b - sum_column * c
        put_blocks(
            n, w, gradients[2], value, 0, channels, place_n=k // per, lane=k % per * 256
        )
        if k + 2 < inner_chunks:
            inner_copy(outer_ref, k + 2).start()

    for k in range(inner_chunks // 2):
        expand_chunk(k)
    sum_two.middle()
    for k in range(inner_chunks // 2, inner_chunks):
        expand_chunk(k)
    launch(2)
    for tap in range(9):
        get(
            ("spatial", tap),
            spatial_ref.at[tap * channels : (tap + 1) * channels],
            spatial.at[tap // 3, :, tap % 3 * channels : (tap % 3 + 1) * channels],
        )
    ins[0].wait()
    turn(wide, slice(0, channels), turned.at[0])
    for k in (1, 2):
        ins[k].wait()
        turn(wide, slice(k * channels, (k + 1) * channels), turned.at[k])
    get("rows", rows_ref, wide)
    grads = sum_two.end()
    norm_two[...] = grads
    a, b, c = norm_scale(1, stat_two, grads)
    for g in range(3):
        blocks = slice(FIRST[g], FIRST[g] + COLUMNS[g])
        up = u[blocks] * a
        raw = two[blocks] * b + c
        value = jnp.stack([up[:, 0] - raw[:, 0], up[:, 1] - raw[:, 1] * m[g]], axis=1)
        hidden[PADDED[g] * block : (PADDED[g] + COLUMNS[g]) * block] = value.reshape(
            COLUMNS[g] * block, channels
        ).astype(BF16)
    three[tail:, :] = jnp.zeros((deep - tail, three.shape[1]), BF16)
    for offset in range(3):
        for g in range(3):
            start = (PADDED[g] - (offset - 1)) * block
            three[
                FIRST[g] * block : (FIRST[g] + COLUMNS[g]) * block,
                offset * channels : (offset + 1) * channels,
            ] = hidden[start : start + COLUMNS[g] * block, :]
    advance(2, 0)
    for level in range(3):
        for offset in range(3):
            value = dot(turned[level], three[:, offset * channels : (offset + 1) * channels])
            put_blocks(n, w, gradients[1], value, (3 * level + offset) * channels, shapes[1][0])
        if level > 0:
            advance(2, level)
    launch(1)
    get("again", grad_ref, three.at[:tail])
    for tap in range(9):
        ins["spatial", tap].wait()

    def taps(g, level):
        at, count = PADDED[g] * block, COLUMNS[g] * block
        shifted = [hidden[at - d * block : at - d * block + count, :] for d in (-1, 0, 1)]
        value = dot_t(jnp.concatenate(shifted, axis=1), spatial[level])
        return value.reshape(COLUMNS[g], 2, images, channels)

    copies = []
    for g in range(3):
        flag = m[g] > 0.5
        blocks = slice(FIRST[g], FIRST[g] + COLUMNS[g])
        rows = padded_rows(COLUMNS[g] * images)
        upper = taps(g, 0)
        lower = taps(g, 2)
        to_before[starts[g] : starts[g] + rows] = pack_halo(upper[:, 0])
        to_after[starts[g] : starts[g] + rows] = pack_halo(
            lower[:, 1] + jnp.where(flag, 0.0, lower[:, 0])
        )
        copies.append(
            halo_copies(
                n, g, rows, starts, to_after, from_before, to_before, from_after, halo_sems
            )
        )
        halo_start(n, copies[g])
        u[blocks] = jnp.stack([upper[:, 1], jnp.where(flag, lower[:, 0], 0.0)], axis=1)
    advance(1, 0)
    ins["one"].wait()

    a, b, scale, mean = forward_scale(stat_one[...], norm_params(gain_ref, bias_ref, 0, channels), number)
    sums = jnp.zeros((1, channels), F32)
    gains = jnp.zeros((1, channels), F32)
    for g in range(3):
        flag = m[g] > 0.5
        blocks = slice(FIRST[g], FIRST[g] + COLUMNS[g])
        middle = taps(g, 1)
        rows = padded_rows(COLUMNS[g] * images)
        halo_arrived(n, copies[g])
        before = unpack_halo(from_before[starts[g] : starts[g] + rows], COLUMNS[g], images)
        after = unpack_halo(from_after[starts[g] : starts[g] + rows], COLUMNS[g], images)
        first = u[blocks][:, 0] + middle[:, 0] + before + jnp.where(flag, 0.0, after)
        second = u[blocks][:, 1] + middle[:, 1] + jnp.where(flag, after, 0.0)
        raw = one[blocks]
        v = raw * a + b
        slope = slope_of(v, *half_of(v))
        value = jnp.stack([slope[:, 0] * first, slope[:, 1] * second * m[g]], axis=1)
        u[blocks] = value
        sums = sums + jnp.sum(value, axis=(0, 1, 2))[None]
        gains = gains + jnp.sum(value * ((raw - mean) * scale), axis=(0, 1, 2))[None]
    sum_one.begin(jnp.concatenate([gains, sums], axis=0))
    for k in range(2):
        inner_copy(inner_ref, k).start()
    for g in range(3):
        hidden[FIRST[g] * block : (FIRST[g] + COLUMNS[g]) * block] = (
            u[FIRST[g] : FIRST[g] + COLUMNS[g]].reshape(COLUMNS[g] * block, channels).astype(BF16)
        )
    hidden[tail:deep] = jnp.zeros((deep - tail, channels), BF16)
    turn(hidden.at[:deep], slice(0, channels), turned.at[0])
    ins["rows"].wait()

    for k in range(2):
        raw_chunk(k)
    sum_one.middle()
    for k in range(2, inner_chunks):
        raw_chunk(k)
        if k == 4:
            advance(2, 3)
        if k == 5:
            advance(1, 1, 0)
    for k in range(4):
        at = slice(k * channels, (k + 1) * channels)
        get(("reduce", k), reduce_ref.at[at], wide.at[:channels, at])
    for g in range(3):
        halo_sent(n, copies[g])
    grads = sum_one.end()
    norm_one[...] = grads
    a, b, c = norm_scale(0, stat_one, grads)
    a_column, b_column, c_column = column(a), column(b), column(c)
    advance(1, 1, 1)
    per = 256 // (shapes[0][0] // w)
    for k in range(inner_chunks):
        inner_copy(inner_ref, k).wait()
        value = raw_value(k) * a_column - inner_ring[k % 2, :channels] * b_column
        value = value - inner_ring[k % 2, channels : channels + 1] * c_column
        put_blocks(n, w, gradients[0], value.T, 0, shapes[0][0], place_w=k * per)
        if k + 2 < inner_chunks:
            inner_copy(inner_ref, k + 2).start()
    launch(0)
    advance(1, 2, 0)
    advance(0, 0)
    for g in range(3):
        blocks = slice(FIRST[g], FIRST[g] + COLUMNS[g])
        up = u[blocks] * a
        raw = one[blocks] * b + c
        value = jnp.stack([up[:, 0] - raw[:, 0], up[:, 1] - raw[:, 1] * m[g]], axis=1)
        hidden[FIRST[g] * block : (FIRST[g] + COLUMNS[g]) * block] = value.reshape(
            COLUMNS[g] * block, channels
        ).astype(BF16)
    for k in range(4):
        ins["reduce", k].wait()
    ins["again"].wait()

    def input_step(k, _):
        at = pl.ds(pl.multiple_of(k * 256, 256), 256)
        weight = wide[
            pl.ds(pl.multiple_of(lax.rem(k, 2) * 256, 256), 256),
            pl.ds(pl.multiple_of(lax.div(k, 2) * channels, channels), channels),
        ]
        for g in range(3):
            rows = slice(FIRST[g] * block, (FIRST[g] + COLUMNS[g]) * block)
            value = dot_t(hidden[rows, :], weight) + three[rows, at].astype(F32)
            three[rows, at] = value.astype(BF16)
        return 0

    lax.fori_loop(0, inner_chunks // 2, input_step, 0)
    advance(1, 2, 1)
    advance(0, 1)
    lax.fori_loop(inner_chunks // 2, inner_chunks, input_step, 0)
    get("out", three.at[:tail], input_ref)
    advance(1, 3, 0)
    advance(0, 2)
    columns, totals = [None] * 3, [None] * 3

    def column_sums(which):
        for copy in sent[which]:
            copy.wait_recv()
        old = (reduce_rows_ref, spatial_rows_ref, expand_rows_ref)[which]
        by_column, total = [], None
        for k in range(n):
            value = shares[which][k].astype(F32)
            square = value * value + EPS_ONE
            by_column.append(jnp.sum(square, axis=0, keepdims=True))
            part = jnp.sum(by_column[-1], axis=1, keepdims=True)
            total = part if total is None else total + part
        columns[which] = jnp.concatenate(by_column, axis=1)
        total = BETA * jnp.sum(old[...].reshape(1, -1), axis=1, keepdims=True) + (
            1.0 - BETA
        ) / shapes[which][1] * total
        totals[which] = jnp.broadcast_to(total, (1, 128))

    column_sums(2)
    advance(1, 3, 1)
    advance(0, 3)
    column_sums(1)
    column_sums(0)
    columns_ref[...] = sum_over(
        "wide", w, jnp.concatenate(columns + totals, axis=1), *column_scratch
    )
    for which in range(3):
        for scatter in scatters[which]:
            scatter.done()
        for copy in sent[which]:
            copy.wait_send()
    ins["out"].wait()


def final_kernel(
    w, input_ref, sums_ref, reduce_share, spatial_share, expand_share,
    reduce_ref, spatial_ref, expand_ref, square_reduce, square_spatial, square_expand,
    reduce_rows, spatial_rows, expand_rows, reduce_cols, spatial_cols, expand_cols,
    one_ref, two_ref, three_ref, gain_ref, bias_ref, state_ref,
    out_ref, reduce_grad, spatial_grad, expand_grad, reduce_rows_next, reduce_cols_next, spatial_rows_next,
    spatial_cols_next, expand_rows_next, expand_cols_next, reduce_next, spatial_next, expand_next,
    norm_grads, norm_second, norm_next,
    row_ring, out_ring, zeros, reduce_own, spatial_own, expand_own, sems, ring_sems,
):
    me = lax.axis_index("wide")
    own_copies = []
    for k, (source, own) in enumerate(
        ((reduce_ref, reduce_own), (spatial_ref, spatial_own), (expand_ref, expand_own))
    ):
        size = own.shape[0]
        own_copies.append(
            pltpu.make_async_copy(source.at[pl.ds(me * size, size)], own, sems.at[k])
        )
        own_copies[-1].start()
    images = out_ref.shape[1]
    lanes = out_ref.shape[3] // 2
    block = 2 * images

    def copy(which, t):
        slot = lax.rem(t, DEPTH)
        if which == 0:
            rows = pl.ds(pl.multiple_of(t * block, block), block)
            return pltpu.make_async_copy(input_ref.at[rows], row_ring.at[slot], ring_sems.at[0, slot])
        g, j = place_of(t)
        return pltpu.make_async_copy(out_ring.at[slot], out_ref.at[g, :, j], ring_sems.at[1, slot])

    for t in range(DEPTH):
        copy(0, jnp.int32(t)).start()
    zeros[...] = jnp.zeros(zeros.shape, BF16)
    empty = []
    for g in range(3):
        for j in range(COLUMNS[g], out_ref.shape[2]):
            empty.append(
                pltpu.make_async_copy(zeros, out_ref.at[g, :, j], sems.at[3 + len(empty)])
            )
            empty[-1].start()

    def pair(i, _):
        for k in range(2):
            copy(0, 2 * i + k).wait()

        @pl.when(2 * i >= DEPTH)
        def _():
            for k in range(2):
                copy(1, 2 * i + k - DEPTH).wait()

        for k in range(2):
            slot = lax.rem(2 * i + k, DEPTH)
            for group in range(lanes // 8):
                blocks = [
                    row_ring[slot, :, c * 128 : (c + 1) * 128].astype(F32)
                    for c in range(8 * group, 8 * group + 8)
                ]
                for j in range(images // 8):
                    out_ring[slot, 8 * j : 8 * j + 8, 16 * group : 16 * group + 16] = turned_out(
                        blocks, j
                    ).astype(BF16)
        for k in range(2):
            copy(1, 2 * i + k).start()

        @pl.when(2 * i + DEPTH < BLOCKS)
        def _():
            for k in range(2):
                copy(0, 2 * i + k + DEPTH).start()

        return 0

    lax.fori_loop(0, BLOCKS // 2, pair, 0)
    grads = jnp.concatenate([one_ref[...], two_ref[...], three_ref[...]], axis=1)
    norm_grads[...] = grads
    params = jnp.concatenate([gain_ref[...], bias_ref[...]], axis=0)
    second = BETA * state_ref[...] + (1.0 - BETA) * (grads * grads + EPS_ONE)
    norm_second[...] = second
    rate = 0.5 * jnp.maximum(
        jnp.sqrt(jnp.sum(params * params, axis=1, keepdims=True) / params.shape[1]), 0.001
    )
    norm_next[...] = params - rate * grads * lax.rsqrt(second)
    lane = 0
    weights = (
        (reduce_share, reduce_own, square_reduce, reduce_rows, reduce_cols, reduce_grad,
         reduce_rows_next, reduce_cols_next, reduce_next, reduce_ref),
        (spatial_share, spatial_own, square_spatial, spatial_rows, spatial_cols, spatial_grad,
         spatial_rows_next, spatial_cols_next, spatial_next, spatial_ref),
        (expand_share, expand_own, square_expand, expand_rows, expand_cols, expand_grad,
         expand_rows_next, expand_cols_next, expand_next, expand_ref),
    )
    at = 0
    for share, *_ in weights:
        at += share.shape[0] * share.shape[2]
    for which, (
        share, own, square, old_rows, old_cols, grad, next_rows, next_cols, next_w, full
    ) in enumerate(weights):
        n, height, width = share.shape
        all_rows = full.shape[0]
        rate = 0.5 * jnp.maximum(
            jnp.sqrt(
                jnp.sum(square[...], axis=1, keepdims=True) / (full.shape[0] * full.shape[1])
            ),
            0.001,
        )
        row_mean = sums_ref[0:1, at + 128 * which : at + 128 * which + 1] / all_rows
        total = jnp.zeros((height, 1), F32)
        for k in range(n):
            value = share[k].astype(F32)
            grad[:, k * width : (k + 1) * width] = value
            total = total + jnp.sum(value * value + EPS_ONE, axis=1, keepdims=True)
        old = jnp.broadcast_to(old_rows[...].reshape(1, height), (128, height)).T
        by_row = BETA * old + (1.0 - BETA) / (n * width) * total
        next_rows[...] = by_row.T[0:1].reshape(next_rows.shape)
        by_column = BETA * old_cols[...] + (1.0 - BETA) / all_rows * sums_ref[
            0:1, lane : lane + n * width
        ]
        next_cols[...] = by_column
        lane += n * width
        second = by_row[:, 0:1] * (by_column / row_mean)
        own_copies[which].wait()
        next_w[...] = own[...] - rate * grad[...] * lax.rsqrt(second)
    for t in range(BLOCKS - DEPTH, BLOCKS):
        copy(1, jnp.int32(t)).wait()
    for done in empty:
        done.wait()


def pixels_first(x):
    g, i, s, c, k = x.shape
    x = jnp.transpose(x, (0, 1, 3, 2, 4)).reshape(g, i, c, s, k // 128, 128)
    return jnp.transpose(x, (0, 1, 2, 4, 3, 5)).reshape(g, i, c, s * k // 128, 128)


def slots_first(x, slots):
    g, i, c, r, k = x.shape
    x = x.reshape(g, i, c, r // slots, slots, k)
    x = jnp.transpose(x, (0, 1, 2, 4, 3, 5)).reshape(g, i, c, slots, r // slots * k)
    return jnp.transpose(x, (0, 1, 3, 2, 4))


def call(kernel, outs, ins, scratch, collective_id=None, **more):
    params = dict(vmem_limit_bytes=LIMIT)
    if collective_id is not None:
        params.update(collective_id=collective_id, has_side_effects=True)
    smem = [x.ndim == 1 for x in ins]
    specs = dict(
        in_specs=[pl.BlockSpec(memory_space=pltpu.SMEM if s else VMEM) for s in smem],
        out_specs=tuple(pl.BlockSpec(memory_space=VMEM) for _ in outs),
    )
    specs.update(more)
    return pl.pallas_call(
        kernel,
        out_shape=tuple(jax.ShapeDtypeStruct(shape, dtype) for shape, dtype in outs),
        scratch_shapes=scratch,
        compiler_params=pltpu.CompilerParams(**params),
        **specs,
    )(*ins)


def shards(
    n, w, images, upstream, row_counts, w_reduce, w_spatial, w_expand, norm_gain, norm_bias,
    reduce_rows, reduce_cols, spatial_rows, spatial_cols, expand_rows, expand_cols, norm_state,
):
    groups, count, slots, across, outer = images.shape
    inner = w_reduce.shape[1]
    block = slots * count
    tail = BLOCKS * block
    deep = -(-tail // 256) * 256
    number = float(w * count * sum(c * c for c in COLUMNS))
    counts = row_counts.reshape(groups)
    x = pixels_first(images)
    up = pixels_first(upstream)
    params = (norm_gain.reshape(1, -1), norm_bias.reshape(1, -1))
    whole = (BLOCKS, slots, count, inner)
    narrow_sums = reduce_scratch(n, w, 2, inner)
    outer_sums = reduce_scratch(n, w, 2, outer)
    _, halo = halo_rows(count)
    halo_scratch = [VMEM((halo, inner), BF16)] * 4 + [pltpu.SemaphoreType.DMA((4, 3))]
    stage = VMEM((count // 8, slots * outer // 16, 128), F32)
    order = (slots * outer // 16, slots * outer // 16)

    weights = (w_reduce, w_spatial, w_expand)
    full = pl.BlockSpec(memory_space=VMEM)
    smem = pl.BlockSpec(memory_space=pltpu.SMEM)
    far = pl.BlockSpec(memory_space=pl.ANY)
    dma = pltpu.SemaphoreType.DMA
    padded = ((PADDED_BLOCKS * block, inner), BF16)
    compact = ((deep, inner), BF16)
    inner_images = ((inner + 16, outer), F32)
    forward_arrays = [
        ((deep, outer), BF16), (whole, F32), (whole, F32), compact, compact, compact, compact,
        ((tail, outer), BF16), inner_images, (w_expand.shape, F32), *[(v.shape, BF16) for v in weights],
    ]
    (
        rows, conv_one, conv_two, upper, middle, lower, hidden_two, conv_three, one_images, two_three, *rounded,
        stats_one, stats_two, stats_three, hidden_sum, square_one, square_two, square_three,
    ) = call(
        functools.partial(forward_kernel, n, w, number),
        forward_arrays
        + [((2, v), F32) for v in (inner, inner, outer)]
        + [((1, v), F32) for v in (inner, inner, inner, outer)],
        (x, *weights, *params, counts),
        [
            VMEM((RING, *x.shape[1:2], *x.shape[3:]), BF16),
            VMEM((deep, outer), BF16),
            VMEM((4, CHUNK, inner), F32),
            VMEM(w_expand.shape, F32),
            *[VMEM(v.shape, BF16) for v in weights],
            VMEM(whole, F32),
            VMEM(whole, F32),
            *[VMEM(*padded)] * 3,
            VMEM((deep, inner), BF16),
            VMEM((deep, outer), BF16),
            VMEM((inner + 16, deep), BF16),
            VMEM(*inner_images),
            *halo_scratch,
            dma((RING,)),
            dma((4,)),
            dma,
            dma((32,)),
        ]
        + narrow_sums
        + narrow_sums
        + outer_sums,
        0,
        in_specs=[far] * 4 + [full, full, smem],
        out_specs=(far,) * 13 + (full,) * 7,
    )
    row_ring = VMEM((DEPTH, block, outer), BF16)
    map_ring = VMEM((DEPTH, *x.shape[1:2], *x.shape[3:]), BF16)
    output, grad_summed, sums_three = call(
        functools.partial(top_kernel, number, inner),
        [(x.shape, BF16), ((tail, outer), BF16), ((2, 8, outer), F32)],
        (conv_three, rows, up, stats_three, *params, counts),
        [
            row_ring,
            row_ring,
            map_ring,
            map_ring,
            row_ring,
            *[stage] * 4,
            VMEM((2, *order), BF16),
            VMEM((2, outer), F32),
            dma((6, DEPTH)),
        ],
        in_specs=[far] * 3 + [full] * 3 + [smem],
        out_specs=(far, far, full),
    )
    blocks = [block_shapes(n, w, *weight.shape) for weight in weights]
    rows_old = [reduce_rows, spatial_rows, expand_rows]
    cols_old = [v.reshape(1, -1) for v in (reduce_cols, spatial_cols, expand_cols)]
    lanes = sum(v.shape[1] for v in weights) + 3 * 128
    scatter = []
    for weight in weights:
        scatter += scatter_scratch(n, w, *weight.shape)
    input_grad, sums, *more = call(
        functools.partial(backward_kernel, n, w, number, [v.shape for v in weights]),
        [((tail, outer), BF16), ((1, lanes), F32)]
        + [((n, v.shape[0] // w, v.shape[1] // n), BF16) for v in weights]
        + [((2, v), F32) for v in (inner, inner, outer)],
        (
            conv_three, grad_summed, hidden_two, rounded[2], conv_two, rounded[1],
            upper, middle, lower, conv_one, rows, rounded[0], one_images, two_three, sums_three, hidden_sum,
            stats_one, stats_two, stats_three, *params, counts, *rows_old,
        ),
        [
            VMEM((deep, outer), BF16),
            VMEM((deep, outer), BF16),
            VMEM(*padded),
            VMEM((3, inner, deep), BF16),
            VMEM(w_expand.shape, BF16),
            VMEM((3, inner, 3 * inner), BF16),
            VMEM(whole, F32),
            VMEM(whole, F32),
            VMEM(whole, F32),
            VMEM((4, outer), F32),
            VMEM((2, inner + 16, 256), F32),
            dma((2,)),
            *halo_scratch,
            dma((32,)),
            *[VMEM(shape, BF16) for which in range(3) for shape in blocks[which]],
        ]
        + scatter
        + [dma((n,))] * 6
        + outer_sums
        + narrow_sums
        + narrow_sums
        + [VMEM((w, 1, lanes), F32), dma((w,)), dma((w,))],
        1,
        in_specs=[far] * 14 + [full] * 7 + [smem] + [full] * 3,
        out_specs=(far,) + (full,) * 7,
    )
    shares, (grads_one, grads_two, grads_three) = more[:3], more[3:]
    heights = [v.shape[0] // w for v in weights]
    slabs = [((h, v.shape[1]), F32) for h, v in zip(heights, weights)]
    vectors = []
    for h, v in zip(heights, weights):
        vectors += [((h,), F32), ((1, v.shape[1]), F32)]
    outs = call(
        functools.partial(final_kernel, w),
        [(x.shape, BF16)] + slabs + vectors + slabs + [(norm_state.shape, F32)] * 3,
        (
            input_grad, sums, *shares, *weights, square_one, square_two, square_three,
            *rows_old, *cols_old, grads_one, grads_two, grads_three, *params, norm_state,
        ),
        [
            row_ring,
            map_ring,
            VMEM((*x.shape[1:2], *x.shape[3:]), BF16),
            *[VMEM(shape, dtype) for shape, dtype in slabs],
            dma((16,)),
            dma((2, DEPTH)),
        ],
        in_specs=[far] + [full] * 4 + [far] * 3 + [full] * 15,
        out_specs=(far,) + (full,) * 15,
    )
    input_grad, *outs = outs
    for k in range(3, 9):
        outs[k] = outs[k].reshape(-1)
    return (slots_first(output, slots), slots_first(input_grad, slots), *outs)


def solution(mesh):
    maps = P(None, "wide", "narrow", None, None)
    in_specs = (
        maps, maps, P(None, "wide", "narrow"), P(), P(), P(), P(), P(),
        P("wide"), P(), P("wide"), P(), P("wide"), P(), P(),
    )
    out_specs = (
        maps, maps, P("wide", None), P("wide", None), P("wide", None),
        P("wide"), P(), P("wide"), P(), P("wide"), P(),
        P("wide", None), P("wide", None), P("wide", None), P(), P(), P(),
    )
    return jax.shard_map(
        functools.partial(shards, mesh.shape["narrow"], mesh.shape["wide"]),
        mesh=mesh,
        in_specs=in_specs,
        out_specs=out_specs,
        check_vma=False,
    )
```
